32 devices in a mesh: dp: 8 (over y, x, core), mp: 4 (over z).
Axes of the slice: x: 2, y: 2, z: 4, core: 2. Of those that a mesh axis runs over, the one named last changes fastest.
Arguments:
- tokens: bfloat16 [8192, 2304], P(('dp', 'mp')), may hold values from -6 to 6
- attn_gain: float32 [2304], replicated, may hold values from 0.25 to 1.75
- mlp_gain: float32 [2304], replicated, may hold values from 0.25 to 1.75
- w_query: bfloat16 [2304, 2304], P('dp', 'mp'), may hold values from -0.125 to 0.125
- w_key: bfloat16 [2304, 2304], P('dp', 'mp'), may hold values from -0.125 to 0.125
- w_value: bfloat16 [2304, 2304], P('dp', 'mp'), may hold values from -0.125 to 0.125
- w_out: bfloat16 [2304, 2304], P('mp', 'dp'), may hold values from -12 to 12
- w_gate: bfloat16 [2304, 5760], P('dp', 'mp'), may hold values from -0.125 to 0.125
- w_up: bfloat16 [2304, 5760], P('dp', 'mp'), may hold values from -0.125 to 0.125
- w_down: bfloat16 [5760, 2304], P('mp', 'dp'), may hold values from -0.5 to 0.5
- prefix: int32 [8], P('dp'), may hold values from 102 to 512, as said below
- out_grad: bfloat16 [8192, 2304], P(('dp', 'mp')), may hold values from -6 to 6
Outputs:
- block_out: bfloat16 [8192, 2304], P(('dp', 'mp'))
- input_grad: bfloat16 [8192, 2304], P(('dp', 'mp'))
- grad_w_query: float32 [2304, 2304], P('dp', 'mp')
- grad_w_key: float32 [2304, 2304], P('dp', 'mp')
- grad_w_value: float32 [2304, 2304], P('dp', 'mp')
- grad_w_out: float32 [2304, 2304], P('mp', 'dp')
- grad_w_gate: float32 [2304, 5760], P('dp', 'mp')
- grad_w_up: float32 [2304, 5760], P('dp', 'mp')
- grad_w_down: float32 [5760, 2304], P('mp', 'dp')
- grad_attn_gain: float32 [2304], replicated
- grad_mlp_gain: float32 [2304], replicated
The draws below stay inside these ranges and needn't reach their ends.
Inputs may be any that keep to these rules, and one draw needn't show every extreme that they name: prefix[s] is the number of leading tokens of sequence s that all its tokens attend to; later tokens attend causally. Both ends of the range occur in every draw.
All inputs are finite; a program needn't handle non-finite values.
Results may differ from the reference program's by a relative error of at most 0.019.
Values may be sent and summed in bfloat16 or wider, within the bound.
No kernel may reach another device: no remote copies, remote signals or barrier semaphores. Data moves between devices by JAX's collectives and lax.ppermute only.
A program may use at most 256 MiB of HBM per device.

```python
from functools import partial
import jax
import jax.numpy as jnp
from jax import lax

D = 2304
H = 36
HD = 64
FF = 5760
LEN = 1024
SEQS = 8
TOKENS = 8192


def draw_prefix(key, part):
    key = jax.random.fold_in(key, 7)
    key_values, key_top, key_bottom = jax.random.split(key, 3)
    values = jax.random.randint(key_values, (SEQS,), LEN // 10, LEN // 2 + 1)
    top_place = jax.random.randint(key_top, (), 0, SEQS)
    bottom_place = (top_place + 1 + jax.random.randint(key_bottom, (), 0, SEQS - 1)) % SEQS
    places = jnp.arange(SEQS)
    values = jnp.where(places == top_place, LEN // 2, values)
    values = jnp.where(places == bottom_place, LEN // 10, values)
    return values.astype(jnp.int32)


def spiked(values, own_key, source, target, blocks, factor):
    def block_of(dim):
        return (jnp.arange(values.shape[dim]) // (values.shape[dim] // blocks)).reshape((-1,) + (1,) * (values.ndim - 1 - dim))

    near = jax.random.permutation(own_key, blocks)[block_of(target)]
    far = (block_of(target) + blocks // 2) % blocks
    return jnp.where((block_of(source) == near) | (block_of(source) == far), factor * values, values)


def levels(rng, shape, pieces, low, top_value):
    level, own = 1.0, jax.random.fold_in(rng, 6)
    for position, parts in pieces:
        heights = jnp.exp(jax.random.uniform(jax.random.fold_in(own, position), (parts,), jnp.float32, low / len(pieces), top_value / len(pieces)))
        level = level * jnp.repeat(heights, shape[position] // parts).reshape([-1 if axis == position else 1 for axis in range(len(shape))])
    return level


def gaussian(own_key, dims, scale, reach, pieces=(), held_as=jnp.bfloat16):
    values = jax.random.normal(own_key, dims, jnp.float32) * scale
    if len(pieces) > 0:
        values = levels(own_key, dims, pieces, -0.22, 0.18) * values
    return jnp.clip(values, min=-reach, max=reach).astype(held_as)


def gaussian_with(rng, dims, scale, most, shards, heavy, kind=jnp.bfloat16):
    values = scale * jax.random.normal(rng, dims, jnp.float32)
    if shards:
        values = values * levels(rng, dims, shards, -0.22, 0.18)
    return jnp.clip(spiked(values, jax.random.fold_in(rng, 3), *heavy), -most, most).astype(kind)


def setup_inputs(seed: int = 0) -> dict:
    streams_of = jax.random.split(jax.random.key(seed), 13)
    return {
        "tokens": gaussian(streams_of[0], (TOKENS, D), 1.0, 6.0, ((0, 32),)),
        "attn_gain": jnp.clip(1.0 + 0.15 * jax.random.normal(streams_of[1], (D,), jnp.float32), 0.25, 1.75),
        "mlp_gain": jnp.clip(1.0 + 0.15 * jax.random.normal(streams_of[2], (D,), jnp.float32), 0.25, 1.75),
        "w_query": gaussian(streams_of[3], (D, H * HD), D ** -0.5, 0.125, ((0, 8), (1, 4))),
        "w_key": gaussian(streams_of[4], (D, H * HD), D ** -0.5, 0.125, ((0, 8), (1, 4))),
        "w_value": gaussian(streams_of[5], (D, H * HD), D ** -0.5, 0.125, ((0, 8), (1, 4))),
        "w_out": gaussian(streams_of[6], (H * HD, D), (3.0 * LEN ** 0.5 / (H * HD) ** 0.5), 12.0, ((0, 4), (1, 8))),
        "w_gate": gaussian(streams_of[7], (D, FF), D ** -0.5, 0.125, ((0, 8), (1, 4))),
        "w_up": gaussian(streams_of[8], (D, FF), D ** -0.5, 0.125, ((0, 8), (1, 4))),
        "w_down": gaussian(streams_of[9], (FF, D), (6.0 / FF ** 0.5), 0.5, ((0, 4), (1, 8))),
        "prefix": draw_prefix(jax.random.fold_in(streams_of[12], 71), 0),
        "out_grad": gaussian_with(streams_of[11], (TOKENS, D), 1.0, 6.0, ((0, 32),), (0, 1, 32, 2.75)),
    }


@jax.custom_vjp
def low(v):
    return lax.optimization_barrier(v.astype(jnp.bfloat16)).astype(jnp.float32)

@jax.custom_vjp
def low_back(v):
    return v

def low_keep(v):
    return (low(v), None)

def low_pass(kept, grad):
    return (grad,)

def back_keep(v):
    return (v, None)

def back_low(kept, grad):
    return (low(grad),)
low.defvjp(low_keep, low_pass)
low_back.defvjp(back_keep, back_low)
EPSILON = 1e-05
BRANCH = 1.4 / 40 ** 0.5
HIGHEST = lax.Precision.HIGHEST

def normalize(value, gain):
    factor = lax.rsqrt(lax.optimization_barrier(jnp.mean(value * value, axis=-1, keepdims=True)) + EPSILON)
    return value * factor * gain

def turned(value):
    half_width = value.shape[-1] // 2
    return jnp.concatenate([-value[..., half_width:], value[..., :half_width]], axis=-1)

def rotate(value):
    width = value.shape[-1]
    half_width = width // 2
    places = jnp.arange(value.shape[-3], dtype=jnp.float32)
    rates = 10000.0 ** (-jnp.arange(half_width, dtype=jnp.float32) * 2.0 / width)
    angles = places[:, None] * rates[None, :]
    cosine = jnp.concatenate([jnp.cos(angles), jnp.cos(angles)], axis=-1)[:, None, :]
    sine = jnp.concatenate([jnp.sin(angles), jnp.sin(angles)], axis=-1)[:, None, :]
    return value * cosine + turned(value) * sine

def attend_sequence(inputs):
    queries, keys_rot, values_act, limit = inputs
    raw_scores = jnp.einsum('qhd,khd->hqk', queries, keys_rot, precision=HIGHEST) * HD ** (-0.5)
    scores = low_back(raw_scores)
    row_place = jnp.arange(LEN, dtype=jnp.int32)[:, None]
    col_place = jnp.arange(LEN, dtype=jnp.int32)[None, :]
    visible = (col_place < limit) | (col_place <= row_place)
    scores = jnp.where(visible[None], scores, -1e+30)
    maximum = lax.optimization_barrier(jnp.max(scores, axis=-1, keepdims=True))
    weights = jnp.exp(scores - maximum)
    chances = low(weights / lax.optimization_barrier(jnp.sum(weights, axis=-1, keepdims=True)))
    return jnp.einsum('hqk,khd->qhd', chances, values_act, precision=HIGHEST)

def forward(prefix, inputs, attn_gain, mlp_gain, w_query, w_key, w_value, w_out, w_gate, w_up, w_down):
    count = inputs.shape[0]
    shape_four = (SEQS, LEN, H, HD)
    normed_one = low(normalize(inputs, attn_gain))
    query_pre = low_back(jnp.dot(normed_one, w_query, precision=HIGHEST))
    key_pre = low_back(jnp.dot(normed_one, w_key, precision=HIGHEST))
    value_pre = low_back(jnp.dot(normed_one, w_value, precision=HIGHEST))
    queries = low(rotate(query_pre.reshape(shape_four)))
    keys_rot = low(rotate(key_pre.reshape(shape_four)))
    values_act = low(value_pre).reshape(shape_four)
    attended = lax.map(jax.checkpoint(attend_sequence), (queries, keys_rot, values_act, prefix))
    attended = low(low_back(attended.reshape(count, H * HD)))
    attn_sum = low_back(jnp.dot(attended, w_out, precision=HIGHEST))
    middle = inputs + BRANCH * attn_sum
    normed_two = low(normalize(middle, mlp_gain))
    gate_act = low_back(jnp.dot(normed_two, w_gate, precision=HIGHEST))
    up_act = low_back(jnp.dot(normed_two, w_up, precision=HIGHEST))
    hidden = low(jax.nn.silu(gate_act) * up_act)
    mlp_sum = low_back(jnp.dot(hidden, w_down, precision=HIGHEST))
    return middle + BRANCH * mlp_sum

def reference(tokens, attn_gain, mlp_gain, w_query, w_key, w_value, w_out, w_gate, w_up, w_down, prefix, out_grad):
    floats = [array.astype(jnp.float32) for array in (tokens, attn_gain, mlp_gain, w_query, w_key, w_value, w_out, w_gate, w_up, w_down)]
    result, pullback = jax.vjp(partial(forward, prefix), *floats)
    grads = pullback(out_grad.astype(jnp.float32))
    return (result.astype(jnp.bfloat16), grads[0].astype(jnp.bfloat16), grads[3], grads[4], grads[5], grads[6], grads[7], grads[8], grads[9], grads[1], grads[2])
```

```python
import functools

import jax
import jax.numpy as jnp
from jax import lax
from jax.experimental import pallas as pl
from jax.experimental.pallas import tpu as pltpu
from jax.sharding import PartitionSpec as P

HD = 64
LEN = 1024
LANES = 128
EPSILON = 1e-05
BRANCH = 1.4 / 40**0.5
MASKED = -1e30
FF_BLOCK = 256
VMEM_LIMIT = 56 * 1024 * 1024

F32 = jnp.float32
BF16 = jnp.bfloat16


def round_up(value, unit):
    return -(-value // unit) * unit


def matmul(left, right):
    return jnp.dot(left, right, preferred_element_type=F32)


def inner_rows(left, right):
    return lax.dot_general(
        left, right, (((0,), (0,)), ((), ())), preferred_element_type=F32
    )


def outer_cols(left, right):
    return lax.dot_general(
        left, right, (((1,), (1,)), ((), ())), preferred_element_type=F32
    )


def params(limit=VMEM_LIMIT):
    return pltpu.CompilerParams(vmem_limit_bytes=limit)


def ring_up(value):
    n = lax.axis_size("mp")
    return lax.ppermute(value, "mp", [(i, (i + 1) % n) for i in range(n)])


def ring_gather(value):
    pieces = [value]
    for _ in range(lax.axis_size("mp") - 1):
        pieces.append(ring_up(pieces[-1]))
    return pieces


def ring_scatter(part):
    n = lax.axis_size("mp")
    place = lax.axis_index("mp")
    total = part((place + n - 1) % n)
    for step in range(1, n):
        arrived = ring_up(total.astype(BF16))
        total = part((place + 2 * n - 1 - step) % n) + arrived.astype(F32)
    return total


def shift_back(value, count):
    n = lax.axis_size("mp")
    return lax.ppermute(value, "mp", [(i, (i - count) % n) for i in range(n)])


def sum_all(value):
    for axis in ("mp", "dp"):
        n = lax.axis_size(axis)
        bit = 1
        while bit < n:
            value = value + lax.ppermute(value, axis, [(i, i ^ bit) for i in range(n)])
            bit *= 2
    return value


def place_kernel(count, place_ref, *refs):
    pieces, out_ref, sems = refs[:count], refs[count], refs[count + 1]
    rows = pieces[0].shape[0]
    place = place_ref[0]
    copies = []
    for k in range(count):
        start = pl.multiple_of(lax.rem(place + count - k, count) * rows, rows)
        copy = pltpu.make_async_copy(
            pieces[k], out_ref.at[pl.ds(start, rows)], sems.at[k]
        )
        copy.start()
        copies.append(copy)
    for copy in copies:
        copy.wait()


def place_rows(pieces, place):
    count = len(pieces)
    rows, width = pieces[0].shape
    return pl.pallas_call(
        functools.partial(place_kernel, count),
        out_shape=jax.ShapeDtypeStruct((count * rows, width), pieces[0].dtype),
        in_specs=[pl.BlockSpec(memory_space=pltpu.SMEM)]
        + [pl.BlockSpec(memory_space=pl.ANY)] * count,
        out_specs=pl.BlockSpec(memory_space=pl.ANY),
        scratch_shapes=[pltpu.SemaphoreType.DMA((count,))],
        name="place",
    )(place, *pieces)


def angle_tables():
    half = HD // 2
    places = jnp.arange(LEN, dtype=F32)
    rates = 10000.0 ** (-jnp.arange(half, dtype=F32) * 2.0 / HD)
    angles = places[:, None] * rates[None, :]
    cosine, sine = jnp.cos(angles), jnp.sin(angles)
    return (
        jnp.concatenate([cosine] * 4, axis=-1),
        jnp.concatenate([-sine, sine] * 2, axis=-1),
    )


def swap_halves(value):
    lane = lax.broadcasted_iota(jnp.int32, value.shape, 1)
    low = (lane % HD) < HD // 2
    return jnp.where(
        low, pltpu.roll(value, LANES - HD // 2, 1), pltpu.roll(value, HD // 2, 1)
    )


def project_kernel(fresh, where_ref, x_ref, gain_ref, w_ref, cos_ref, sin_ref, *refs):
    qkv_ref, norm_ref, copy_ref, held = refs[-4:]

    @pl.when(pl.program_id(0) == 0)
    def _():
        value = x_ref[...].astype(F32)
        factor = lax.rsqrt(jnp.mean(value * value, axis=-1, keepdims=True) + EPSILON)
        normed = (value * factor * gain_ref[...]).astype(BF16)
        held[...] = normed
        norm_ref[...] = normed
        copy_ref[...] = x_ref[...]

    product = matmul(held[...], w_ref[...])
    cosine, sine = cos_ref[...], sin_ref[...]
    query = product[:, :LANES]
    key = product[:, LANES : 2 * LANES]
    query = (query * cosine + swap_halves(query) * sine).astype(BF16)
    qkv_ref[:, :LANES] = query * HD**-0.5
    qkv_ref[:, LANES : 2 * LANES] = (key * cosine + swap_halves(key) * sine).astype(BF16)
    qkv_ref[:, 2 * LANES :] = product[:, 2 * LANES :].astype(BF16)


def project(where, piece, gain, weights, tables, held):
    rows, width = piece.shape
    columns = weights.shape[1]
    block = 3 * LANES
    fresh = held is None
    outs = (
        jax.ShapeDtypeStruct((LEN, columns), BF16),
        jax.ShapeDtypeStruct((LEN, width), BF16),
        jax.ShapeDtypeStruct((LEN, width), BF16),
    )
    specs = [
        pl.BlockSpec((rows, width), lambda i, w: (0, 0)),
        pl.BlockSpec((1, width), lambda i, w: (0, 0)),
        pl.BlockSpec((width, block), lambda i, w: (0, i)),
        pl.BlockSpec((rows, LANES), lambda i, w: (w[0], 0)),
        pl.BlockSpec((rows, LANES), lambda i, w: (w[0], 0)),
    ]
    args = [piece, gain, weights, *tables]
    aliases = {}
    if not fresh:
        for index, array in enumerate(held):
            aliases[1 + len(args)] = index
            args.append(array)
            specs.append(pl.BlockSpec(memory_space=pl.ANY))
    return pl.pallas_call(
        functools.partial(project_kernel, fresh),
        out_shape=outs,
        grid_spec=pltpu.PrefetchScalarGridSpec(
            num_scalar_prefetch=1,
            grid=(columns // block,),
            in_specs=specs,
            out_specs=(
                pl.BlockSpec((rows, block), lambda i, w: (w[0], i)),
                pl.BlockSpec((rows, width), lambda i, w: (w[0], 0)),
                pl.BlockSpec((rows, width), lambda i, w: (w[0], 0)),
            ),
            scratch_shapes=[pltpu.VMEM((rows, width), BF16)],
        ),
        input_output_aliases=aliases,
        compiler_params=params(),
        cost_estimate=pl.CostEstimate(
            flops=2 * rows * width * columns,
            bytes_accessed=2 * width * columns + 6 * rows * width,
            transcendentals=0,
        ),
        name="project",
    )(where, *args)


PARTS = (
    (0, 512, ((0, 512, True),)),
    (512, 256, ((0, 512, False), (512, 256, True))),
    (768, 256, ((0, 768, False), (768, 256, True))),
)


def visible(shape, first_key, first_query, limit):
    key = first_key + lax.broadcasted_iota(jnp.int32, shape, 0)
    query = first_query + lax.broadcasted_iota(jnp.int32, shape, 1)
    return (key < limit) | (key <= query)


def head_only(value, head):
    lane = lax.broadcasted_iota(jnp.int32, value.shape, 1)
    return jnp.where((lane >= HD) == (head == 1), value, jnp.zeros_like(value))


def attend_kernel(heads, prefix_ref, qkv_ref, out_ref, log_ref, turned):
    limit = prefix_ref[0]
    pair = pl.program_id(0)
    values_across = qkv_ref[:, 2 * LANES :].T
    for head in (0, 1):

        @pl.when(2 * pair + head < heads)
        def _():
            queries = head_only(qkv_ref[:, :LANES], head)
            for first, count, spans in PARTS:
                mine = queries[first : first + count]
                scores = []
                for start, keys, masked in spans:
                    raw = outer_cols(qkv_ref[start : start + keys, LANES : 2 * LANES], mine)
                    if masked:
                        raw = jnp.where(visible(raw.shape, start, first, limit), raw, MASKED)
                    scores.append(raw)
                top = functools.reduce(
                    jnp.maximum, [jnp.max(s, axis=0, keepdims=True) for s in scores]
                )
                total = jnp.zeros_like(top)
                summed = jnp.zeros((HD, count), F32)
                for (start, keys, _), raw in zip(spans, scores):
                    weight = jnp.exp(raw - top)
                    total = total + jnp.sum(weight, axis=0, keepdims=True)
                    summed = summed + matmul(
                        values_across[head * HD : (head + 1) * HD, start : start + keys],
                        weight.astype(BF16),
                    )
                turned[head * HD : (head + 1) * HD, first : first + count] = summed / total
                log_ref[0, head : head + 1, first : first + count] = top + jnp.log(total)

        @pl.when(2 * pair + head >= heads)
        def _():
            turned[head * HD : (head + 1) * HD, :] = jnp.zeros((HD, LEN), F32)
            log_ref[0, head : head + 1, :] = jnp.zeros((1, LEN), F32)

    out_ref[...] = turned[...].T.astype(BF16)


def attend(qkv, prefix, heads):
    pairs = qkv.shape[1] // (3 * LANES)
    return pl.pallas_call(
        functools.partial(attend_kernel, heads),
        out_shape=(
            jax.ShapeDtypeStruct((LEN, pairs * LANES), BF16),
            jax.ShapeDtypeStruct((pairs, 2, LEN), F32),
        ),
        grid_spec=pltpu.PrefetchScalarGridSpec(
            num_scalar_prefetch=1,
            grid=(pairs,),
            in_specs=[pl.BlockSpec((LEN, 3 * LANES), lambda i, s: (0, i))],
            out_specs=(
                pl.BlockSpec((LEN, LANES), lambda i, s: (0, i)),
                pl.BlockSpec((1, 2, LEN), lambda i, s: (i, 0, 0)),
            ),
            scratch_shapes=[pltpu.VMEM((LANES, LEN), F32)],
        ),
        compiler_params=params(),
        cost_estimate=pl.CostEstimate(
            flops=16 * LEN * LEN * LANES * heads,
            bytes_accessed=8 * LEN * LANES * pairs,
            transcendentals=LEN * LEN * heads,
        ),
        name="attend",
    )(prefix, qkv)


def attend_back_kernel(
    heads, prefix_ref, qkv_ref, out_ref, grad_ref, log_ref, cos_ref, sin_ref, back_ref,
    turned, grad_key, grad_value,
):
    limit = prefix_ref[0]
    pair = pl.program_id(0)
    keys_across = qkv_ref[:, LANES : 2 * LANES].T
    inner = (out_ref[...].astype(F32) * grad_ref[...].astype(F32)).T
    grad_key[...] = jnp.zeros_like(grad_key)
    grad_value[...] = jnp.zeros_like(grad_value)
    for head in (0, 1):
        band = slice(head * HD, (head + 1) * HD)

        @pl.when(2 * pair + head < heads)
        def _():
            queries = head_only(qkv_ref[:, :LANES], head)
            grads = head_only(grad_ref[...], head)
            inner_row = jnp.sum(inner[band], axis=0, keepdims=True)
            for first, count, spans in PARTS:
                here = slice(first, first + count)
                mine, grad_mine = queries[here], grads[here]
                log_mine = log_ref[0, head : head + 1, here]
                inner_mine = inner_row[:, here]
                summed = jnp.zeros((HD, count), F32)
                for start, keys, masked in spans:
                    there = slice(start, start + keys)
                    raw = outer_cols(qkv_ref[there, LANES : 2 * LANES], mine)
                    chance = jnp.exp(raw - log_mine)
                    if masked:
                        chance = jnp.where(
                            visible(raw.shape, start, first, limit), chance, 0.0
                        )
                    grad_chance = outer_cols(qkv_ref[there, 2 * LANES :], grad_mine)
                    grad_score = (chance * (grad_chance - inner_mine)).astype(BF16)
                    grad_key[there, :] += matmul(grad_score, mine)
                    grad_value[there, :] += matmul(chance.astype(BF16), grad_mine)
                    summed = summed + matmul(keys_across[band, there], grad_score)
                turned[band, here] = summed

        @pl.when(2 * pair + head >= heads)
        def _():
            turned[band, :] = jnp.zeros((HD, LEN), F32)

    cosine, sine = cos_ref[...], sin_ref[...]
    grad_query = turned[...].T * HD**-0.5
    back_ref[:, :LANES] = (grad_query * cosine - swap_halves(grad_query) * sine).astype(BF16)
    back = grad_key[...]
    back_ref[:, LANES : 2 * LANES] = (back * cosine - swap_halves(back) * sine).astype(BF16)
    back_ref[:, 2 * LANES :] = grad_value[...].astype(BF16)


def attend_back(qkv, attended, grad, log_total, tables, prefix, heads):
    pairs = qkv.shape[1] // (3 * LANES)
    return pl.pallas_call(
        functools.partial(attend_back_kernel, heads),
        out_shape=jax.ShapeDtypeStruct(qkv.shape, BF16),
        grid_spec=pltpu.PrefetchScalarGridSpec(
            num_scalar_prefetch=1,
            grid=(pairs,),
            in_specs=[
                pl.BlockSpec((LEN, 3 * LANES), lambda i, s: (0, i)),
                pl.BlockSpec((LEN, LANES), lambda i, s: (0, i)),
                pl.BlockSpec((LEN, LANES), lambda i, s: (0, i)),
                pl.BlockSpec((1, 2, LEN), lambda i, s: (i, 0, 0)),
                pl.BlockSpec((LEN, LANES), lambda i, s: (0, 0)),
                pl.BlockSpec((LEN, LANES), lambda i, s: (0, 0)),
            ],
            out_specs=pl.BlockSpec((LEN, 3 * LANES), lambda i, s: (0, i)),
            scratch_shapes=[
                pltpu.VMEM((LANES, LEN), F32),
                pltpu.VMEM((LEN, LANES), F32),
                pltpu.VMEM((LEN, LANES), F32),
            ],
        ),
        compiler_params=params(),
        cost_estimate=pl.CostEstimate(
            flops=40 * LEN * LEN * LANES * heads,
            bytes_accessed=16 * LEN * LANES * pairs,
            transcendentals=LEN * LEN * heads,
        ),
        name="attend_back",
    )(prefix, qkv, attended, grad, log_total, *tables)


def mlp_kernel(normed_ref, grad_ref, gate_up_ref, down_ref, both_ref, hidden_ref):
    rows = 256
    for start in range(0, LEN, rows):
        here = slice(start, start + rows)
        product = matmul(normed_ref[here], gate_up_ref[...])
        gate, up = product[:, :FF_BLOCK], product[:, FF_BLOCK:]
        grad = matmul(grad_ref[here], down_ref[...])
        sigmoid = jax.nn.sigmoid(gate)
        silu = gate * sigmoid
        hidden_ref[here, :] = (silu * up).astype(BF16)
        both_ref[here, :FF_BLOCK] = (
            grad * up * (sigmoid + silu * (1.0 - sigmoid))
        ).astype(BF16)
        both_ref[here, FF_BLOCK:] = (grad * silu).astype(BF16)


def mlp(normed, grad, gate_up, down):
    width = normed.shape[1]
    hidden = down.shape[1]
    return pl.pallas_call(
        mlp_kernel,
        out_shape=(
            jax.ShapeDtypeStruct((LEN, 2 * hidden), BF16),
            jax.ShapeDtypeStruct((LEN, hidden), BF16),
        ),
        grid=(hidden // FF_BLOCK,),
        in_specs=[
            pl.BlockSpec((LEN, width), lambda i: (0, 0)),
            pl.BlockSpec((LEN, width), lambda i: (0, 0)),
            pl.BlockSpec((width, 2 * FF_BLOCK), lambda i: (0, i)),
            pl.BlockSpec((width, FF_BLOCK), lambda i: (0, i)),
        ],
        out_specs=(
            pl.BlockSpec((LEN, 2 * FF_BLOCK), lambda i: (0, i)),
            pl.BlockSpec((LEN, FF_BLOCK), lambda i: (0, i)),
        ),
        compiler_params=params(),
        cost_estimate=pl.CostEstimate(
            flops=6 * LEN * width * hidden,
            bytes_accessed=4 * LEN * width + 6 * width * hidden + 6 * LEN * hidden,
            transcendentals=LEN * hidden,
        ),
        name="mlp",
    )(normed, grad, gate_up, down)


def widen(value, width):
    return jnp.pad(value, ((0, 0), (0, width - value.shape[1])))


def interleave(values, width, block):
    rows = values[0].shape[0]
    shaped = [widen(v, width).reshape(rows, width // block, block) for v in values]
    return jnp.stack(shaped, axis=2).reshape(rows, len(values) * width)


def separate(value, count, block, width):
    rows = value.shape[0]
    shaped = value.reshape(rows, -1, count, block)
    return [shaped[:, :, i].reshape(rows, -1)[:, :width] for i in range(count)]


def dp_gather(value):
    return lax.all_gather(value, "dp", axis=0, tiled=True)


def dp_scatter(value):
    return lax.psum_scatter(value, "dp", scatter_dimension=0, tiled=True)


def normalize_back(value, gain, incoming):
    factor = lax.rsqrt(jnp.mean(value * value, axis=-1, keepdims=True) + EPSILON)
    normed = value * factor
    scaled = incoming * gain
    inner = jnp.mean(scaled * normed, axis=-1, keepdims=True)
    return (factor * (scaled - normed * inner), jnp.sum(incoming * normed, axis=0))


def body(
    tokens,
    attn_gain,
    mlp_gain,
    w_query,
    w_key,
    w_value,
    w_out,
    w_gate,
    w_up,
    w_down,
    prefix,
    out_grad,
):
    mp = lax.axis_size("mp")
    place = lax.axis_index("mp")
    rows = tokens.shape[0]
    width_heads = w_query.shape[1]
    heads = width_heads // HD
    padded_heads = round_up(width_heads, LANES)
    width_ff = w_gate.shape[1]
    padded_ff = round_up(width_ff, FF_BLOCK)
    own = place * rows

    def row_block(value, index):
        return lax.dynamic_slice_in_dim(value, index * rows, rows, 0)

    tables = angle_tables()
    attn_weights = dp_gather(interleave([w_query, w_key, w_value], padded_heads, LANES))
    out_weights = dp_gather(
        jnp.concatenate(ring_gather(widen(w_out.T, padded_heads)), axis=1)
    )
    gate_up = dp_gather(interleave([w_gate, w_up], padded_ff, FF_BLOCK))
    down = dp_gather(widen(w_down.T, padded_ff))

    held = None
    token_pieces = ring_gather(tokens)
    for k, piece in enumerate(token_pieces):
        where = jnp.reshape((place + mp - k) % mp, (1,))
        held = project(where, piece, attn_gain[None], attn_weights, tables, held)
    qkv, normed_one, whole_tokens = held

    attended, log_total = attend(qkv, prefix, heads)
    attended_pieces = ring_gather(attended)
    attn_sum = jnp.zeros((LEN, out_weights.shape[0]), F32)
    for k, piece in enumerate(attended_pieces):
        attn_sum = attn_sum + outer_cols(
            piece, out_weights[:, k * padded_heads : (k + 1) * padded_heads]
        )
    middle_all = whole_tokens.astype(F32) + BRANCH * attn_sum
    normed_two = (
        middle_all
        * lax.rsqrt(jnp.mean(middle_all * middle_all, axis=-1, keepdims=True) + EPSILON)
        * mlp_gain
    ).astype(BF16)
    middle = row_block(middle_all, place)

    grad_result = out_grad.astype(F32)
    grad_pieces = ring_gather((BRANCH * grad_result).astype(BF16))
    grad_mlp = place_rows(grad_pieces, jnp.reshape(place, (1,)))

    grad_both, hidden = mlp(normed_two, grad_mlp, gate_up, down)

    grad_two = ring_scatter(lambda c: outer_cols(row_block(grad_both, c), gate_up))
    grad_middle_norm, gain_two = normalize_back(middle, mlp_gain, grad_two)
    grad_middle = grad_result + grad_middle_norm
    grad_attn = (BRANCH * grad_middle).astype(BF16)
    grad_attended = matmul(grad_attn, out_weights).astype(BF16)
    arrived = []
    for k in range(mp):
        mine = grad_attended[:, k * padded_heads : (k + 1) * padded_heads]
        arrived.append(mine if k == 0 else shift_back(mine, k))
    grad_heads = place_rows(
        [arrived[(mp - k) % mp] for k in range(mp)], jnp.reshape(place, (1,))
    )

    mlp_sum = ring_scatter(lambda c: outer_cols(row_block(hidden, c), down))
    block_out = middle + BRANCH * mlp_sum

    ff_share = dp_scatter(inner_rows(normed_two, grad_both).astype(BF16)).astype(F32)
    down_share = dp_scatter(inner_rows(grad_mlp, hidden).astype(BF16)).astype(F32)
    grad_w_gate, grad_w_up = separate(ff_share, 2, FF_BLOCK, width_ff)
    grad_w_down = down_share[:, :width_ff].T

    attended_own = jnp.concatenate(
        [row_block(piece, place) for piece in attended_pieces], axis=1
    )
    out_share = dp_scatter(inner_rows(grad_attn, attended_own).astype(BF16))
    out_total = out_share[:, :padded_heads].astype(F32)
    for k in range(1, mp):
        mine = out_share[:, k * padded_heads : (k + 1) * padded_heads]
        out_total = out_total + shift_back(mine, k).astype(F32)
    grad_w_out = out_total[:, :width_heads].T

    back = attend_back(qkv, attended, grad_heads, log_total, tables, prefix, heads)
    attn_share = dp_scatter(inner_rows(normed_one, back).astype(BF16)).astype(F32)
    grad_w_query, grad_w_key, grad_w_value = separate(attn_share, 3, LANES, width_heads)

    grad_one = ring_scatter(lambda c: outer_cols(row_block(back, c), attn_weights))
    grad_input_norm, gain_one = normalize_back(tokens.astype(F32), attn_gain, grad_one)
    input_grad = grad_middle + grad_input_norm
    gains = sum_all(jnp.stack([gain_one, gain_two]))
    return (
        block_out.astype(BF16),
        input_grad.astype(BF16),
        grad_w_query,
        grad_w_key,
        grad_w_value,
        grad_w_out,
        grad_w_gate,
        grad_w_up,
        grad_w_down,
        gains[0],
        gains[1],
    )


def solution(mesh):
    return jax.shard_map(
        body,
        mesh=mesh,
        in_specs=(
            P(("dp", "mp"), None),
            P(),
            P(),
            P("dp", "mp"),
            P("dp", "mp"),
            P("dp", "mp"),
            P("mp", "dp"),
            P("dp", "mp"),
            P("dp", "mp"),
            P("mp", "dp"),
            P("dp"),
            P(("dp", "mp"), None),
        ),
        out_specs=(
            P(("dp", "mp"), None),
            P(("dp", "mp"), None),
            P("dp", "mp"),
            P("dp", "mp"),
            P("dp", "mp"),
            P("mp", "dp"),
            P("dp", "mp"),
            P("dp", "mp"),
            P("mp", "dp"),
            P(),
            P(),
        ),
        check_vma=False,
    )
```

```python
import functools

import jax
import jax.numpy as jnp
import numpy as np
from jax import lax
from jax.experimental import pallas as pl
from jax.experimental.pallas import tpu as pltpu
from jax.sharding import PartitionSpec as P

HD = 64
LEN = 1024
LANES = 128
EPSILON = 1e-05
BRANCH = 1.4 / 40**0.5
MASKED = -1e30
FF_BLOCK = 512
VMEM_LIMIT = 56 * 1024 * 1024

F32 = jnp.float32
BF16 = jnp.bfloat16


def round_up(value, unit):
    return -(-value // unit) * unit


def matmul(left, right):
    return jnp.dot(left, right, preferred_element_type=F32)


def inner_rows(left, right):
    return lax.dot_general(
        left, right, (((0,), (0,)), ((), ())), preferred_element_type=F32
    )


def outer_cols(left, right):
    return lax.dot_general(
        left, right, (((1,), (1,)), ((), ())), preferred_element_type=F32
    )


def cost(micros):
    return pl.CostEstimate(
        flops=int(micros * 3.0e9), bytes_accessed=0, transcendentals=0
    )


def params(limit=VMEM_LIMIT):
    return pltpu.CompilerParams(vmem_limit_bytes=limit)


def ring_up(value):
    n = lax.axis_size("mp")
    return lax.ppermute(value, "mp", [(i, (i + 1) % n) for i in range(n)])


def ring_gather(value):
    pieces = [value]
    for _ in range(lax.axis_size("mp") - 1):
        pieces.append(ring_up(pieces[-1]))
    return pieces


def ring_scatter(part):
    n = lax.axis_size("mp")
    place = lax.axis_index("mp")
    total = part((place + n - 1) % n)
    for step in range(1, n):
        sent = total.astype(BF16)
        arrived = ring_up(sent)
        term = lax.optimization_barrier(part((place + 2 * n - 1 - step) % n))
        total = term + arrived.astype(F32)
    return total


def shift_back(value, count):
    n = lax.axis_size("mp")
    return lax.ppermute(value, "mp", [(i, (i - count) % n) for i in range(n)])


def sum_all(value):
    for axis in ("mp", "dp"):
        n = lax.axis_size(axis)
        bit = 1
        while bit < n:
            value = value + lax.ppermute(value, axis, [(i, i ^ bit) for i in range(n)])
            bit *= 2
    return value


def after(value, *others):
    return lax.optimization_barrier((value, others))[0]


def swap(value, bit):
    n = lax.axis_size("dp")
    return lax.ppermute(value, "dp", [(i, i ^ bit) for i in range(n)])


def dp_gather(value):
    return lax.all_gather(value, "dp", axis=0, tiled=True)


def paired():
    return lax.axis_size("dp") == 8


def split_columns(value):
    if not paired():
        return value[None]
    core = lax.axis_index("dp") % 2
    rows, width = value.shape
    shaped = value.reshape(rows, 4, 2, width // 8)

    def pick(which):
        return lax.dynamic_index_in_dim(shaped, which, 2, False).reshape(rows, width // 2)

    return jnp.stack([pick(core), pick(1 - core)])


def after_all(waits):
    return [pl.BlockSpec(memory_space=pl.ANY)] * len(waits)


def weight_kernel(joined, left_ref, right_ref, *refs):
    value = inner_rows(left_ref[...], right_ref[...])
    if joined:
        value = value + refs[0][...].astype(F32)
    refs[-1][...] = value.astype(BF16)


def weight_grad(left, right, side, height, width, micros, arrived=None, waits=()):
    depth, columns = left.shape[-2:]
    others = right.shape[1]
    specs = [
        pl.BlockSpec((None, depth, height), lambda i, j: (side, 0, i))
        if left.ndim == 3
        else pl.BlockSpec((depth, height), lambda i, j: (0, i)),
        pl.BlockSpec((depth, width), lambda i, j: (0, j)),
    ]
    args = [left, right]
    if arrived is not None:
        specs.append(pl.BlockSpec((height, width), lambda i, j: (i, j)))
        args.append(arrived)
    return pl.pallas_call(
        functools.partial(weight_kernel, arrived is not None),
        out_shape=jax.ShapeDtypeStruct((columns, others), BF16),
        grid=(columns // height, others // width),
        in_specs=specs + after_all(waits),
        out_specs=pl.BlockSpec((height, width), lambda i, j: (i, j)),
        compiler_params=params(),
        cost_estimate=cost(micros),
        name="weight_grad",
    )(*args, *waits)


def scatter_other(left, right, width, micros, waits=()):
    if not paired():
        return None
    return weight_grad(left, right, 1, left.shape[2], width, micros, waits=waits)


def scatter_mine(left, right, width, micros, arrived, waits=()):
    if not paired():
        return inner_rows(left[0], right).astype(BF16)
    return weight_grad(left, right, 0, left.shape[2], width, micros, arrived, waits)


def pass_kernel(*refs):
    pass


def gate(value, *waits):
    return pl.pallas_call(
        pass_kernel,
        out_shape=jax.ShapeDtypeStruct(value.shape, value.dtype),
        in_specs=after_all((value, *waits)),
        out_specs=pl.BlockSpec(memory_space=pl.ANY),
        input_output_aliases={0: 0},
        cost_estimate=cost(1),
        name="gate",
    )(value, *waits)


def join_kernel(one_ref, two_ref, *refs):
    out_ref, zero_ref = refs[-2:]
    out_ref[...] = (one_ref[...].astype(F32) + two_ref[...].astype(F32)).astype(BF16)
    zero_ref[0] = 0


def join_marked(one, two, waits=()):
    whole = pl.BlockSpec(memory_space=pltpu.VMEM)
    return pl.pallas_call(
        join_kernel,
        out_shape=(
            jax.ShapeDtypeStruct(one.shape, BF16),
            jax.ShapeDtypeStruct((1,), jnp.int32),
        ),
        in_specs=[whole, whole] + after_all(waits),
        out_specs=(whole, pl.BlockSpec(memory_space=pltpu.SMEM)),
        compiler_params=params(),
        cost_estimate=cost(3),
        name="join",
    )(one, two, *waits)


def join(one, two, waits=()):
    return join_marked(one, two, waits)[0]


def scatter_first(chip):
    index = lax.axis_index("dp")
    x, y = index // 2 % 2, index // 4
    rows = chip.shape[0] // 4
    half = rows // 2
    chip = chip.reshape(2, 2, rows, -1)

    def pick(array, axis, which):
        return lax.dynamic_index_in_dim(array, which, axis, False)

    one, two = chip[:, :, :half], chip[:, :, half:]
    kept = pick(one, 0, y), pick(two, 1, x)
    return kept, (swap(pick(one, 0, 1 - y), 4), swap(pick(two, 1, 1 - x), 2))


def scatter_join(kept, moved, waits):
    return join(kept[0], moved[0], waits), join(kept[1], moved[1], waits)


def scatter_second(parts):
    index = lax.axis_index("dp")
    x, y = index // 2 % 2, index // 4
    one, two = parts

    def pick(array, which):
        return lax.dynamic_index_in_dim(array, which, 0, False)

    return [
        (pick(one, x), swap(pick(one, 1 - x), 2)),
        (pick(two, y), swap(pick(two, 1 - y), 4)),
    ]


def scatter_whole(partial):
    share = lax.psum_scatter(partial, "dp", scatter_dimension=0, tiled=True)
    half = share.shape[0] // 2
    return [(share[:half], None), (share[half:], None)]


def angle_tables():
    half = HD // 2
    rates = 10000.0 ** (-np.arange(half) * 2.0 / HD)
    angles = np.arange(LEN)[:, None] * rates[None, :]
    cosine, sine = np.cos(angles), np.sin(angles)
    return (
        jnp.asarray(np.concatenate([cosine] * 4, axis=-1), F32),
        jnp.asarray(np.concatenate([-sine, sine] * 2, axis=-1), F32),
    )


def swap_halves(value):
    lane = lax.broadcasted_iota(jnp.int32, value.shape, 1)
    low = (lane % HD) < HD // 2
    return jnp.where(
        low, pltpu.roll(value, LANES - HD // 2, 1), pltpu.roll(value, HD // 2, 1)
    )


def put_split(ref, value, core):
    if ref.shape[0] == 1:
        ref[0] = value
        return
    block = value.shape[1] // 8
    for which in (0, 1):

        @pl.when(core == which)
        def _():
            for side in (0, 1):
                for chip in range(4):
                    start = (2 * chip + (which ^ side)) * block
                    ref[side, :, chip * block : (chip + 1) * block] = value[
                        :, start : start + block
                    ]


def split_shape(rows, width):
    return (2, rows, width // 2) if paired() else (1, rows, width)


def project_kernel(fresh, where_ref, x_ref, gain_ref, w_ref, cos_ref, sin_ref, *refs):
    qkv_ref, norm_ref, copy_ref, mark_ref, held = refs[-5:]
    mark_ref[...] = jnp.zeros_like(mark_ref)

    @pl.when(pl.program_id(0) == 0)
    def _():
        value = x_ref[...].astype(F32)
        factor = lax.rsqrt(jnp.mean(value * value, axis=-1, keepdims=True) + EPSILON)
        normed = (value * factor * gain_ref[...]).astype(BF16)
        held[...] = normed
        put_split(norm_ref, normed, where_ref[1])
        copy_ref[...] = x_ref[...]

    product = matmul(held[...], w_ref[...])
    cosine, sine = cos_ref[...], sin_ref[...]
    query = product[:, :LANES]
    key = product[:, LANES : 2 * LANES]
    query = (query * cosine + swap_halves(query) * sine).astype(BF16)
    qkv_ref[:, :LANES] = query * HD**-0.5
    qkv_ref[:, LANES : 2 * LANES] = (key * cosine + swap_halves(key) * sine).astype(BF16)
    qkv_ref[:, 2 * LANES :] = product[:, 2 * LANES :].astype(BF16)


def project(where, piece, gain, weights, tables, held):
    rows, width = piece.shape
    columns = weights.shape[1]
    block = 3 * LANES
    fresh = held is None
    outs = (
        jax.ShapeDtypeStruct((LEN, columns), BF16),
        jax.ShapeDtypeStruct(split_shape(LEN, width), BF16),
        jax.ShapeDtypeStruct((LEN, width), BF16),
        jax.ShapeDtypeStruct((8, LANES), F32),
    )
    specs = [
        pl.BlockSpec((rows, width), lambda i, w: (0, 0)),
        pl.BlockSpec((1, width), lambda i, w: (0, 0)),
        pl.BlockSpec((width, block), lambda i, w: (0, i)),
        pl.BlockSpec((rows, LANES), lambda i, w: (w[0], 0)),
        pl.BlockSpec((rows, LANES), lambda i, w: (w[0], 0)),
    ]
    args = [piece, gain, weights, *tables]
    aliases = {}
    if not fresh:
        for index, array in enumerate(held):
            aliases[1 + len(args)] = index
            args.append(array)
            specs.append(pl.BlockSpec(memory_space=pl.ANY))
    return pl.pallas_call(
        functools.partial(project_kernel, fresh),
        out_shape=outs,
        grid_spec=pltpu.PrefetchScalarGridSpec(
            num_scalar_prefetch=1,
            grid=(columns // block,),
            in_specs=specs,
            out_specs=(
                pl.BlockSpec((rows, block), lambda i, w: (w[0], i)),
                pl.BlockSpec(split_shape(rows, width), lambda i, w: (0, w[0], 0)),
                pl.BlockSpec((rows, width), lambda i, w: (w[0], 0)),
                pl.BlockSpec((8, LANES), lambda i, w: (0, 0)),
            ),
            scratch_shapes=[pltpu.VMEM((rows, width), BF16)],
        ),
        input_output_aliases=aliases,
        compiler_params=params(),
        cost_estimate=cost(11),
        name="project",
    )(where, *args)


PARTS = (
    (0, 512, ((0, 512, True),)),
    (512, 256, ((0, 512, False), (512, 256, True))),
    (768, 256, ((0, 768, False), (768, 256, True))),
)


def visible(shape, first_key, first_query, limit):
    key = first_key + lax.broadcasted_iota(jnp.int32, shape, 0)
    query = first_query + lax.broadcasted_iota(jnp.int32, shape, 1)
    return (key < limit) | (key <= query)


def head_only(value, head):
    lane = lax.broadcasted_iota(jnp.int32, value.shape, 1)
    return jnp.where((lane >= HD) == (head == 1), value, jnp.zeros_like(value))


def attend_kernel(heads, prefix_ref, qkv_ref, out_ref, log_ref, turned):
    limit = prefix_ref[0]
    pair = pl.program_id(0)
    values_across = qkv_ref[:, 2 * LANES :].T
    for head in (0, 1):

        @pl.when(2 * pair + head < heads)
        def _():
            queries = head_only(qkv_ref[:, :LANES], head)
            for first, count, spans in PARTS:
                mine = queries[first : first + count]
                scores = []
                for start, keys, masked in spans:
                    raw = outer_cols(qkv_ref[start : start + keys, LANES : 2 * LANES], mine)
                    if masked:
                        raw = jnp.where(visible(raw.shape, start, first, limit), raw, MASKED)
                    scores.append(raw)
                top = functools.reduce(
                    jnp.maximum, [jnp.max(s, axis=0, keepdims=True) for s in scores]
                )
                total = jnp.zeros_like(top)
                summed = jnp.zeros((HD, count), F32)
                for (start, keys, _), raw in zip(spans, scores):
                    weight = jnp.exp(raw - top)
                    total = total + jnp.sum(weight, axis=0, keepdims=True)
                    summed = summed + matmul(
                        values_across[head * HD : (head + 1) * HD, start : start + keys],
                        weight.astype(BF16),
                    )
                turned[head * HD : (head + 1) * HD, first : first + count] = summed / total
                log_ref[0, head : head + 1, first : first + count] = top + jnp.log(total)

        @pl.when(2 * pair + head >= heads)
        def _():
            turned[head * HD : (head + 1) * HD, :] = jnp.zeros((HD, LEN), F32)
            log_ref[0, head : head + 1, :] = jnp.zeros((1, LEN), F32)

    out_ref[...] = turned[...].T.astype(BF16)


def attend(qkv, prefix, heads):
    pairs = qkv.shape[1] // (3 * LANES)
    return pl.pallas_call(
        functools.partial(attend_kernel, heads),
        out_shape=(
            jax.ShapeDtypeStruct((LEN, pairs * LANES), BF16),
            jax.ShapeDtypeStruct((pairs, 2, LEN), F32),
        ),
        grid_spec=pltpu.PrefetchScalarGridSpec(
            num_scalar_prefetch=1,
            grid=(pairs,),
            in_specs=[pl.BlockSpec((LEN, 3 * LANES), lambda i, s: (0, i))],
            out_specs=(
                pl.BlockSpec((LEN, LANES), lambda i, s: (0, i)),
                pl.BlockSpec((1, 2, LEN), lambda i, s: (i, 0, 0)),
            ),
            scratch_shapes=[pltpu.VMEM((LANES, LEN), F32)],
        ),
        compiler_params=params(),
        cost_estimate=cost(18),
        name="attend",
    )(prefix, qkv)


def attend_back_kernel(
    heads, count, prefix_ref, qkv_ref, out_ref, *refs
):
    arrived = refs[:count]
    log_ref, cos_ref, sin_ref = refs[count : count + 3]
    back_ref, turned, grad_key, grad_value, grad_ref = refs[-5:]
    limit = prefix_ref[0]
    rows = arrived[0].shape[0]
    for k in range(count):
        start = pl.multiple_of(lax.rem(prefix_ref[1] + k, count) * rows, rows)
        grad_ref[pl.ds(start, rows), :] = arrived[k][...]
    pair = pl.program_id(0)
    keys_across = qkv_ref[:, LANES : 2 * LANES].T
    inner = (out_ref[...].astype(F32) * grad_ref[...].astype(F32)).T
    grad_key[...] = jnp.zeros_like(grad_key)
    grad_value[...] = jnp.zeros_like(grad_value)
    for head in (0, 1):
        band = slice(head * HD, (head + 1) * HD)

        @pl.when(2 * pair + head < heads)
        def _():
            queries = head_only(qkv_ref[:, :LANES], head)
            grads = head_only(grad_ref[...], head)
            inner_row = jnp.sum(inner[band], axis=0, keepdims=True)
            for first, count, spans in PARTS:
                here = slice(first, first + count)
                mine, grad_mine = queries[here], grads[here]
                log_mine = log_ref[0, head : head + 1, here]
                inner_mine = inner_row[:, here]
                summed = jnp.zeros((HD, count), F32)
                for start, keys, masked in spans:
                    there = slice(start, start + keys)
                    raw = outer_cols(qkv_ref[there, LANES : 2 * LANES], mine)
                    chance = jnp.exp(raw - log_mine)
                    if masked:
                        chance = jnp.where(
                            visible(raw.shape, start, first, limit), chance, 0.0
                        )
                    grad_chance = outer_cols(qkv_ref[there, 2 * LANES :], grad_mine)
                    grad_score = (chance * (grad_chance - inner_mine)).astype(BF16)
                    grad_key[there, :] += matmul(grad_score, mine)
                    grad_value[there, :] += matmul(chance.astype(BF16), grad_mine)
                    summed = summed + matmul(keys_across[band, there], grad_score)
                turned[band, here] = summed

        @pl.when(2 * pair + head >= heads)
        def _():
            turned[band, :] = jnp.zeros((HD, LEN), F32)

    cosine, sine = cos_ref[...], sin_ref[...]
    grad_query = turned[...].T * HD**-0.5
    back_ref[:, :LANES] = (grad_query * cosine - swap_halves(grad_query) * sine).astype(BF16)
    back = grad_key[...]
    back_ref[:, LANES : 2 * LANES] = (back * cosine - swap_halves(back) * sine).astype(BF16)
    back_ref[:, 2 * LANES :] = grad_value[...].astype(BF16)


def attend_back(qkv, attended, arrived, log_total, tables, prefix, heads, waits=()):
    pairs = qkv.shape[1] // (3 * LANES)
    count, rows = len(arrived), arrived[0].shape[0]
    return pl.pallas_call(
        functools.partial(attend_back_kernel, heads, count),
        out_shape=jax.ShapeDtypeStruct(qkv.shape, BF16),
        grid_spec=pltpu.PrefetchScalarGridSpec(
            num_scalar_prefetch=1,
            grid=(pairs,),
            in_specs=[
                pl.BlockSpec((LEN, 3 * LANES), lambda i, s: (0, i)),
                pl.BlockSpec((LEN, LANES), lambda i, s: (0, i)),
            ]
            + [pl.BlockSpec((rows, LANES), lambda i, s: (0, i))] * count
            + [
                pl.BlockSpec((1, 2, LEN), lambda i, s: (i, 0, 0)),
                pl.BlockSpec((LEN, LANES), lambda i, s: (0, 0)),
                pl.BlockSpec((LEN, LANES), lambda i, s: (0, 0)),
            ]
            + after_all(waits),
            out_specs=pl.BlockSpec((LEN, 3 * LANES), lambda i, s: (0, i)),
            scratch_shapes=[
                pltpu.VMEM((LANES, LEN), F32),
                pltpu.VMEM((LEN, LANES), F32),
                pltpu.VMEM((LEN, LANES), F32),
                pltpu.VMEM((LEN, LANES), BF16),
            ],
        ),
        compiler_params=params(),
        cost_estimate=cost(28),
        name="attend_back",
    )(prefix, qkv, attended, *arrived, log_total, *tables, *waits)


def middle_kernel(count, place_ref, *refs):
    pieces = refs[:count]
    w_ref, x_ref, gain_ref, normed_ref, own_ref = refs[count:]
    depth = pieces[0].shape[1]
    total = None
    for k in range(count):
        term = outer_cols(pieces[k][...], w_ref[:, k * depth : (k + 1) * depth])
        total = term if total is None else total + term
    middle = x_ref[...].astype(F32) + BRANCH * total
    factor = lax.rsqrt(jnp.mean(middle * middle, axis=-1, keepdims=True) + EPSILON)
    normed_ref[...] = (middle * factor * gain_ref[...]).astype(BF16)
    rows, own = x_ref.shape[0], own_ref.shape[0]
    for part in range(rows // own):

        @pl.when(pl.program_id(0) * (rows // own) + part == place_ref[0])
        def _():
            own_ref[...] = middle[part * own : (part + 1) * own]


def finish_middle(place, pieces, weights, tokens, gain, own):
    width = tokens.shape[1]
    depth = pieces[0].shape[1]
    count = len(pieces)
    rows = 2 * own
    return pl.pallas_call(
        functools.partial(middle_kernel, count),
        out_shape=(
            jax.ShapeDtypeStruct((LEN, width), BF16),
            jax.ShapeDtypeStruct((own, width), F32),
        ),
        grid_spec=pltpu.PrefetchScalarGridSpec(
            num_scalar_prefetch=1,
            grid=(LEN // rows,),
            in_specs=[pl.BlockSpec((rows, depth), lambda i, s: (i, 0))] * count
            + [
                pl.BlockSpec((width, count * depth), lambda i, s: (0, 0)),
                pl.BlockSpec((rows, width), lambda i, s: (i, 0)),
                pl.BlockSpec((1, width), lambda i, s: (0, 0)),
            ],
            out_specs=(
                pl.BlockSpec((rows, width), lambda i, s: (i, 0)),
                pl.BlockSpec((own, width), lambda i, s: (0, 0)),
            ),
        ),
        compiler_params=params(),
        cost_estimate=cost(22),
        name="finish_middle",
    )(place, *pieces, weights, tokens, gain)


def gate_kernel(normed_ref, weight_ref, hidden_ref, slope_ref):
    rows = 256
    for start in range(0, LEN, rows):
        here = slice(start, start + rows)
        product = matmul(normed_ref[here], weight_ref[...])
        gate, up = product[:, :FF_BLOCK], product[:, FF_BLOCK:]
        sigmoid = jax.nn.sigmoid(gate)
        silu = gate * sigmoid
        hidden_ref[here, :] = (silu * up).astype(BF16)
        slope_ref[here, :FF_BLOCK] = (up * (sigmoid + silu * (1.0 - sigmoid))).astype(BF16)
        slope_ref[here, FF_BLOCK:] = silu.astype(BF16)


def feed(normed, gate_up):
    width = normed.shape[1]
    hidden = gate_up.shape[1] // 2
    return pl.pallas_call(
        gate_kernel,
        out_shape=(
            jax.ShapeDtypeStruct((LEN, hidden), BF16),
            jax.ShapeDtypeStruct((LEN, 2 * hidden), BF16),
        ),
        grid=(hidden // FF_BLOCK,),
        in_specs=[
            pl.BlockSpec((LEN, width), lambda i: (0, 0)),
            pl.BlockSpec((width, 2 * FF_BLOCK), lambda i: (0, i)),
        ],
        out_specs=(
            pl.BlockSpec((LEN, FF_BLOCK), lambda i: (0, i)),
            pl.BlockSpec((LEN, 2 * FF_BLOCK), lambda i: (0, i)),
        ),
        compiler_params=params(),
        cost_estimate=cost(21),
        name="feed",
    )(normed, gate_up)


def feed_back_kernel(where_ref, grad_ref, slope_ref, down_ref, weight_ref, *refs):
    both_ref, copy_ref, sum_ref, total = refs[-4:]
    step = pl.program_id(0)

    @pl.when(step == 0)
    def _():
        copy_ref[...] = grad_ref[...]
        total[...] = jnp.zeros_like(total)

    grad = matmul(grad_ref[...], down_ref[...])
    grads = jnp.concatenate([grad, grad], axis=1)
    both = (grads * slope_ref[...].astype(F32)).astype(BF16)
    both_ref[...] = both
    total[...] += outer_cols(both, weight_ref[...])

    @pl.when(step == pl.num_programs(0) - 1)
    def _():
        sum_ref[...] = total[...].astype(sum_ref.dtype)


def feed_back(where, piece, slopes, down, gate_up, held, kind, waits=()):
    rows, width = piece.shape
    hidden = down.shape[1]
    specs = [
        pl.BlockSpec((rows, width), lambda i, w: (0, 0)),
        pl.BlockSpec((rows, 2 * FF_BLOCK), lambda i, w: (w[0], i)),
        pl.BlockSpec((width, FF_BLOCK), lambda i, w: (0, i)),
        pl.BlockSpec((width, 2 * FF_BLOCK), lambda i, w: (0, i)),
    ]
    args = [piece, slopes, down, gate_up]
    aliases = {}
    if held is not None:
        for index, array in enumerate(held):
            aliases[1 + len(args)] = index
            args.append(array)
            specs.append(pl.BlockSpec(memory_space=pl.ANY))
    args += waits
    specs += after_all(waits)
    return pl.pallas_call(
        feed_back_kernel,
        out_shape=(
            jax.ShapeDtypeStruct((LEN, 2 * hidden), BF16),
            jax.ShapeDtypeStruct((LEN, width), BF16),
            jax.ShapeDtypeStruct((rows, width), kind),
        ),
        grid_spec=pltpu.PrefetchScalarGridSpec(
            num_scalar_prefetch=1,
            grid=(hidden // FF_BLOCK,),
            in_specs=specs,
            out_specs=(
                pl.BlockSpec((rows, 2 * FF_BLOCK), lambda i, w: (w[0], i)),
                pl.BlockSpec((rows, width), lambda i, w: (w[0], 0)),
                pl.BlockSpec((rows, width), lambda i, w: (0, 0)),
            ),
            scratch_shapes=[pltpu.VMEM((rows, width), F32)],
        ),
        input_output_aliases=aliases,
        compiler_params=params(),
        cost_estimate=cost(15),
        name="feed_back",
    )(where, *args)


def out_sum_kernel(parts, count, width, *refs):
    terms, outs = grouped(parts, refs)
    half = outs[0].shape[0] // 2
    for index, pair in enumerate(terms):
        value = added(pair)
        here = slice(index * half, (index + 1) * half)
        for k in range(count):
            outs[k][here, :] = value[:, k * width : (k + 1) * width].astype(outs[k].dtype)


def out_sum(parts, count, width):
    rows = 2 * parts[0][0].shape[0]
    arrays = [a for pair in parts for a in pair if a is not None]
    return pl.pallas_call(
        functools.partial(out_sum_kernel, parts_mask(parts), count, width),
        out_shape=tuple(
            jax.ShapeDtypeStruct((rows, width), BF16 if k else F32) for k in range(count)
        ),
        compiler_params=params(),
        cost_estimate=cost(3),
        name="out_sum",
    )(*arrays)


def out_final_kernel(*refs):
    total = refs[0][...]
    for ref in refs[1:-1]:
        total = total + ref[...].astype(F32)
    refs[-1][...] = total.T[: refs[-1].shape[0]]


def out_final(own, moved, width):
    return pl.pallas_call(
        out_final_kernel,
        out_shape=jax.ShapeDtypeStruct((width, own.shape[0]), F32),
        compiler_params=params(),
        cost_estimate=cost(3),
        name="out_final",
    )(own, *moved)


def norm_back(value, gain, incoming):
    factor = lax.rsqrt(jnp.mean(value * value, axis=-1, keepdims=True) + EPSILON)
    normed = value * factor
    scaled_in = incoming * gain
    inner = jnp.mean(scaled_in * normed, axis=-1, keepdims=True)
    return (
        factor * (scaled_in - normed * inner),
        jnp.sum(incoming * normed, axis=0, keepdims=True),
    )


def own_back_kernel(
    core_ref, term_ref, arrived_ref, middle_ref, grad_ref, gain_ref, *refs
):
    sum_ref, send_ref, split_ref, gain_sum_ref, zero_ref = refs[-5:]
    incoming = term_ref[...].astype(F32) + arrived_ref[...].astype(F32)
    back, gain_sum = norm_back(middle_ref[...], gain_ref[...], incoming)
    total = grad_ref[...].astype(F32) + back
    sum_ref[...] = total
    sent = (BRANCH * total).astype(BF16)
    send_ref[...] = sent
    put_split(split_ref, sent, core_ref[0])
    zero_ref[0] = 0

    @pl.when(pl.program_id(0) == 0)
    def _():
        gain_sum_ref[...] = jnp.zeros_like(gain_sum_ref)

    gain_sum_ref[...] += gain_sum


def own_back(core, term, arrived, middle, grad, gain, waits=()):
    rows, width = middle.shape
    step = rows // 2
    block = pl.BlockSpec((step, width), lambda i, s: (i, 0))
    line = pl.BlockSpec((1, width), lambda i, s: (0, 0))
    return pl.pallas_call(
        own_back_kernel,
        out_shape=(
            jax.ShapeDtypeStruct((rows, width), F32),
            jax.ShapeDtypeStruct((rows, width), BF16),
            jax.ShapeDtypeStruct(split_shape(rows, width), BF16),
            jax.ShapeDtypeStruct((1, width), F32),
            jax.ShapeDtypeStruct((1,), jnp.int32),
        ),
        grid_spec=pltpu.PrefetchScalarGridSpec(
            num_scalar_prefetch=1,
            grid=(2,),
            in_specs=[block, block, block, block, line] + after_all(waits),
            out_specs=(
                block,
                block,
                pl.BlockSpec(split_shape(step, width), lambda i, s: (0, i, 0)),
                line,
                pl.BlockSpec(memory_space=pltpu.SMEM),
            ),
        ),
        compiler_params=params(),
        cost_estimate=cost(5),
        name="own_back",
    )(core, term, arrived, middle, grad, gain, *waits)


def finish_input_kernel(term_ref, arrived_ref, x_ref, sum_ref, gain_ref, *refs):
    out_ref, gain_sum_ref, zero_ref = refs[-3:]
    incoming = term_ref[...] + arrived_ref[...].astype(F32)
    back, gain_sum = norm_back(x_ref[...].astype(F32), gain_ref[...], incoming)
    out_ref[...] = (sum_ref[...] + back).astype(BF16)
    zero_ref[0] = 0

    @pl.when(pl.program_id(0) == 0)
    def _():
        gain_sum_ref[...] = jnp.zeros_like(gain_sum_ref)

    gain_sum_ref[...] += gain_sum


def finish_input(term, arrived, x, total, gain, waits=()):
    rows, width = x.shape
    block = pl.BlockSpec((rows // 2, width), lambda i: (i, 0))
    line = pl.BlockSpec((1, width), lambda i: (0, 0))
    return pl.pallas_call(
        finish_input_kernel,
        out_shape=(
            jax.ShapeDtypeStruct((rows, width), BF16),
            jax.ShapeDtypeStruct((1, width), F32),
            jax.ShapeDtypeStruct((1,), jnp.int32),
        ),
        grid=(2,),
        in_specs=[block, block, block, block, line] + after_all(waits),
        out_specs=(block, line, pl.BlockSpec(memory_space=pltpu.SMEM)),
        compiler_params=params(),
        cost_estimate=cost(5),
        name="finish_input",
    )(term, arrived, x, total, gain, *waits)


def finish_block_kernel(middle_ref, term_ref, arrived_ref, *refs):
    total = term_ref[...] + arrived_ref[...].astype(F32)
    refs[-1][...] = (middle_ref[...] + BRANCH * total).astype(BF16)


def finish_block(middle, term, arrived, waits=()):
    rows, width = middle.shape
    block = pl.BlockSpec((rows // 2, width), lambda i: (i, 0))
    return pl.pallas_call(
        finish_block_kernel,
        out_shape=jax.ShapeDtypeStruct((rows, width), BF16),
        grid=(2,),
        in_specs=[block, block, block] + after_all(waits),
        out_specs=block,
        compiler_params=params(),
        cost_estimate=cost(3),
        name="finish_block",
    )(middle, term, arrived, *waits)


def mix(out_ref, refs, block):
    width = refs[0].shape[1]
    count = len(refs)
    for first in range(0, width, block):
        size = min(block, width - first)
        base = first * count
        for index, ref in enumerate(refs):
            spot = base + index * block
            out_ref[:, spot : spot + size] = ref[:, first : first + size]
            if size < block:
                out_ref[:, spot + size : spot + block] = jnp.zeros(
                    (ref.shape[0], block - size), out_ref.dtype
                )


def put_across(out_ref, value):
    rows = value.shape[0]
    out_ref[:, :rows] = value.T
    if rows < out_ref.shape[1]:
        out_ref[:, rows:] = jnp.zeros((out_ref.shape[0], out_ref.shape[1] - rows), BF16)


def pack_kernel(count, block, *refs):
    if count == 1:
        put_across(refs[-1], refs[0][...])
    else:
        mix(refs[-1], refs[:count], block)


def pack(values, block, width, *waits):
    count = len(values)
    rows = values[0].shape[0] if count > 1 else values[0].shape[1]
    whole = pl.BlockSpec(memory_space=pltpu.VMEM)
    return pl.pallas_call(
        functools.partial(pack_kernel, count, block),
        out_shape=jax.ShapeDtypeStruct((rows, count * width), BF16),
        in_specs=[whole] * count + [pl.BlockSpec(memory_space=pl.ANY)] * len(waits),
        out_specs=whole,
        compiler_params=params(),
        cost_estimate=cost(3),
        name="pack",
    )(*values, *waits)


def chain_kernel(count, *refs):
    out_ref = refs[-1]
    width = refs[0].shape[1]
    for k in range(count):
        out_ref[:, k * width : (k + 1) * width] = refs[k][...]


def chain(values, *waits):
    rows, width = values[0].shape
    whole = pl.BlockSpec(memory_space=pltpu.VMEM)
    return pl.pallas_call(
        functools.partial(chain_kernel, len(values)),
        out_shape=jax.ShapeDtypeStruct((rows, len(values) * width), values[0].dtype),
        in_specs=[whole] * len(values) + after_all(waits),
        out_specs=whole,
        compiler_params=params(),
        cost_estimate=cost(2),
        name="chain",
    )(*values, *waits)


def scale_kernel(value_ref, *refs):
    refs[-1][...] = (BRANCH * value_ref[...].astype(F32)).astype(BF16)


def scaled(value, *waits):
    whole = pl.BlockSpec(memory_space=pltpu.VMEM)
    return pl.pallas_call(
        scale_kernel,
        out_shape=jax.ShapeDtypeStruct(value.shape, BF16),
        in_specs=[whole] + [pl.BlockSpec(memory_space=pl.ANY)] * len(waits),
        out_specs=whole,
        compiler_params=params(),
        cost_estimate=cost(3),
        name="scaled",
    )(value, *waits)


def added(terms):
    one, two = terms
    value = one[...].astype(F32)
    return value if two is None else value + two[...].astype(F32)


def grouped(parts, refs):
    refs = list(refs)
    out = [tuple(None if a is None else refs.pop(0) for a in pair) for pair in parts]
    return out, refs


def unmix_kernel(parts, block, *refs):
    terms, outs = grouped(parts, refs)
    width = outs[0].shape[1]
    half = outs[0].shape[0] // 2
    for index, pair in enumerate(terms):
        value = added(pair)
        for first in range(0, width, block):
            size = min(block, width - first)
            for turn, out_ref in enumerate(outs):
                spot = first * len(outs) + turn * block
                out_ref[index * half : (index + 1) * half, first : first + size] = value[
                    :, spot : spot + size
                ]


def unmix(parts, count, block, width):
    rows = 2 * parts[0][0].shape[0]
    arrays = [a for pair in parts for a in pair if a is not None]
    return pl.pallas_call(
        functools.partial(unmix_kernel, parts_mask(parts), block),
        out_shape=tuple(jax.ShapeDtypeStruct((rows, width), F32) for _ in range(count)),
        compiler_params=params(),
        name="unmix",
    )(*arrays)


def parts_mask(parts):
    return [tuple(None if a is None else True for a in pair) for pair in parts]


def turn_kernel(parts, *refs):
    terms, (out_ref,) = grouped(parts, refs)
    value = jnp.concatenate([added(pair) for pair in terms], axis=0)
    out_ref[...] = value.T[: out_ref.shape[0]]


def turn(parts, width):
    rows = 2 * parts[0][0].shape[0]
    arrays = [a for pair in parts for a in pair if a is not None]
    return pl.pallas_call(
        functools.partial(turn_kernel, parts_mask(parts)),
        out_shape=jax.ShapeDtypeStruct((width, rows), F32),
        compiler_params=params(),
        name="turn",
    )(*arrays)


def body(
    tokens,
    attn_gain,
    mlp_gain,
    w_query,
    w_key,
    w_value,
    w_out,
    w_gate,
    w_up,
    w_down,
    prefix,
    out_grad,
):
    mp = lax.axis_size("mp")
    place = lax.axis_index("mp")
    rows = tokens.shape[0]
    width_heads = w_query.shape[1]
    heads = width_heads // HD
    padded_heads = round_up(width_heads, LANES)
    width_ff = w_gate.shape[1]
    padded_ff = round_up(width_ff, FF_BLOCK)
    own = place * rows

    def row_block(value, index):
        return lax.dynamic_slice_in_dim(value, index * rows, rows, 0)

    tables = angle_tables()
    core = lax.axis_index("dp") % 2
    at = [jnp.stack([(place + mp - k) % mp, core]) for k in range(mp)]

    attn_weights = dp_gather(pack([w_query, w_key, w_value], LANES, padded_heads))
    token_pieces = [tokens, ring_up(tokens)]
    ff_pack = pack([w_gate, w_up], FF_BLOCK, padded_ff, token_pieces[1])
    gate_up = dp_gather(ff_pack)
    token_pieces.append(ring_up(token_pieces[1]))
    token_pieces.append(ring_up(token_pieces[2]))
    held = None
    for k in range(mp - 1):
        *held, mark = project(
            at[k], token_pieces[k], attn_gain[None], attn_weights, tables, held
        )
    out_own = pack([w_out], LANES, padded_heads, token_pieces[-1], mark, ff_pack)
    out_pieces = [out_own] + [shift_back(out_own, mp - j) for j in range(1, mp)]
    *held, _ = project(
        at[mp - 1], token_pieces[-1], attn_gain[None], attn_weights, tables, held
    )
    qkv, normed_one, whole_tokens = held
    attended, log_total = attend(qkv, prefix, heads)
    out_pack = chain(out_pieces, attended)
    attended_pieces = [attended, ring_up(attended)]
    out_weights = dp_gather(gate(out_pack, attended_pieces[1], gate_up))
    down_pack = pack([w_down], LANES, padded_ff, attended_pieces[1])
    down = dp_gather(down_pack)
    while len(attended_pieces) < mp:
        attended_pieces.append(ring_up(attended_pieces[-1]))

    grad_own = scaled(out_grad, attended_pieces[-1], down_pack)
    grad_pieces = [grad_own] + [shift_back(grad_own, mp - k) for k in range(1, mp)]
    normed_two, middle = finish_middle(
        at[0], attended_pieces, out_weights, whole_tokens, mlp_gain[None], rows
    )
    hidden, slopes = feed(normed_two, gate_up)

    def back_of(k, held, kind=BF16, waits=()):
        *held, term = feed_back(
            at[k % mp], grad_pieces[k % mp], slopes, down, gate_up, held, kind, waits
        )
        return held, term

    width = normed_two.shape[1]
    grad_pieces.append(ring_up(grad_pieces[-1]))
    held, total = back_of(1, None)
    held, term = back_of(2, held)
    arrived = ring_up(total)
    held, term_three = back_of(3, held)
    (grad_both, grad_mlp), term_own = back_of(4, held, F32)
    total = join(term, arrived, (term_own,))
    arrived = ring_up(total)
    ff_weight = weight_grad(normed_two, grad_both, 0, width // 2, padded_ff, 21)
    total = join(term_three, arrived, (ff_weight,))
    arrived = ring_up(total)
    down_weight = weight_grad(grad_mlp, hidden, 0, width // 2, padded_ff // 2, 12)
    grad_middle, grad_attn, split_attn, gain_two, zero = own_back(
        core[None], term_own, arrived, middle, out_grad, mlp_gain[None], (down_weight,)
    )
    ff_share = scatter_whole(gate(ff_weight, total))
    down_share = scatter_whole(gate(down_weight, zero))

    grad_attended = matmul(grad_attn, out_weights).astype(BF16)
    mine = [
        grad_attended[:, k * padded_heads : (k + 1) * padded_heads] for k in range(mp)
    ]
    attended_own = jnp.concatenate(
        [row_block(piece, place) for piece in attended_pieces], axis=1
    )

    def mlp_chunk(k, zero):
        return lax.optimization_barrier(
            outer_cols(row_block(hidden, at[k % mp][0] + zero[0]), down)
        )

    by_chip = paired()
    arrived = [mine[0]] + [shift_back(mine[k], k) for k in range(1, mp)]
    out_other = scatter_other(split_attn, attended_own, 1280, 5, (grad_attended,))
    chunk_one = mlp_chunk(1, zero).astype(BF16)
    chunk_two = mlp_chunk(2, zero)
    mlp_arrived = ring_up(gate(chunk_one, *arrived[1:]))
    out_arrived = swap(out_other, 1) if by_chip else None
    spots = jnp.stack([prefix[0], place])
    back = attend_back(
        qkv, attended, arrived, log_total, tables, spots, heads,
        (chunk_two, out_other) if by_chip else (chunk_two,),
    )

    def grad_one_term(k, zero=0):
        return lax.optimization_barrier(
            outer_cols(row_block(back, at[k % mp][0] + zero), attn_weights)
        )

    total = grad_one_term(1).astype(BF16)
    arrived = ring_up(total)
    attn_other = scatter_other(normed_one, back, 640, 8, (total,))
    attn_arrived = swap(attn_other, 1) if by_chip else None
    out_chip = scatter_mine(split_attn, attended_own, 1280, 5, out_arrived, (total,))
    term = grad_one_term(2)
    total, zero = join_marked(term, arrived, (out_chip, attn_other) if by_chip else ())
    arrived = ring_up(total)
    mlp_total = join(chunk_two, mlp_arrived, (total,))
    mlp_arrived = ring_up(mlp_total)
    attn_chip = scatter_mine(normed_one, back, 640, 8, attn_arrived, (total,))
    if by_chip:
        out_kept, out_moved = scatter_first(out_chip)
        attn_kept, attn_moved = scatter_first(attn_chip)
    term = grad_one_term(3, zero[0])
    chunk = mlp_chunk(3, zero)
    total, zero = join_marked(term, arrived, (attn_chip,))
    arrived = ring_up(total)
    if by_chip:
        out_half = scatter_join(out_kept, out_moved, (total,))
        out_share = scatter_second(out_half)
        attn_half = scatter_join(attn_kept, attn_moved, (total, *out_half))
        attn_share = scatter_second(attn_half)
        mlp_total = join(chunk, mlp_arrived, (total, *out_half))
    else:
        out_share = scatter_whole(out_chip)
        attn_share = scatter_whole(attn_chip)
        mlp_total = join(chunk, mlp_arrived, (total,))
    term = grad_one_term(4, zero[0])
    mlp_arrived = ring_up(mlp_total)
    input_grad, gain_one, zero = finish_input(
        term, arrived, tokens, grad_middle, attn_gain[None], (mlp_total,)
    )
    out_total, *out_mine = out_sum(out_share, mp, padded_heads)
    out_moved = [shift_back(out_mine[k - 1], k) for k in range(1, mp)]
    gains = sum_all(jnp.concatenate([gain_one, gain_two]))
    chunk = mlp_chunk(4, zero)
    grad_w_query, grad_w_key, grad_w_value = unmix(attn_share, 3, LANES, width_heads)
    grad_w_gate, grad_w_up = unmix(ff_share, 2, FF_BLOCK, width_ff)
    grad_w_down = turn(down_share, width_ff)
    grad_w_out = out_final(out_total, out_moved, width_heads)
    block_out = finish_block(
        middle, chunk, mlp_arrived, (grad_w_gate, grad_w_down, grad_w_query, grad_w_out)
    )
    return (
        block_out,
        input_grad,
        grad_w_query,
        grad_w_key,
        grad_w_value,
        grad_w_out,
        grad_w_gate,
        grad_w_up,
        grad_w_down,
        gains[0],
        gains[1],
    )


def solution(mesh):
    return jax.shard_map(
        body,
        mesh=mesh,
        in_specs=(
            P(("dp", "mp"), None),
            P(),
            P(),
            P("dp", "mp"),
            P("dp", "mp"),
            P("dp", "mp"),
            P("mp", "dp"),
            P("dp", "mp"),
            P("dp", "mp"),
            P("mp", "dp"),
            P("dp"),
            P(("dp", "mp"), None),
        ),
        out_specs=(
            P(("dp", "mp"), None),
            P(("dp", "mp"), None),
            P("dp", "mp"),
            P("dp", "mp"),
            P("dp", "mp"),
            P("mp", "dp"),
            P("dp", "mp"),
            P("dp", "mp"),
            P("mp", "dp"),
            P(),
            P(),
        ),
        check_vma=False,
    )
```

```python
import functools

import jax
import jax.numpy as jnp
import numpy as np
from jax import lax
from jax.experimental import pallas as pl
from jax.experimental.pallas import tpu as pltpu
from jax.sharding import PartitionSpec as P

HD = 64
LEN = 1024
LANES = 128
EPSILON = 1e-05
BRANCH = 1.4 / 40**0.5
MASKED = -1e30
FF_BLOCK = 512
VMEM_LIMIT = 56 * 1024 * 1024

F32 = jnp.float32
BF16 = jnp.bfloat16


def round_up(value, unit):
    return -(-value // unit) * unit


def matmul(left, right):
    return jnp.dot(left, right, preferred_element_type=F32)


def inner_rows(left, right):
    return lax.dot_general(
        left, right, (((0,), (0,)), ((), ())), preferred_element_type=F32
    )


def outer_cols(left, right):
    return lax.dot_general(
        left, right, (((1,), (1,)), ((), ())), preferred_element_type=F32
    )


def cost(micros):
    return pl.CostEstimate(
        flops=int(micros * 3.0e9), bytes_accessed=0, transcendentals=0
    )


def params(limit=VMEM_LIMIT):
    return pltpu.CompilerParams(vmem_limit_bytes=limit)


def ring_up(value):
    n = lax.axis_size("mp")
    return lax.ppermute(value, "mp", [(i, (i + 1) % n) for i in range(n)])


def ring_gather(value):
    pieces = [value]
    for _ in range(lax.axis_size("mp") - 1):
        pieces.append(ring_up(pieces[-1]))
    return pieces


def ring_scatter(part):
    n = lax.axis_size("mp")
    place = lax.axis_index("mp")
    total = part((place + n - 1) % n)
    for step in range(1, n):
        sent = total.astype(BF16)
        arrived = ring_up(sent)
        term = lax.optimization_barrier(part((place + 2 * n - 1 - step) % n))
        total = term + arrived.astype(F32)
    return total


def shift_back(value, count):
    n = lax.axis_size("mp")
    return lax.ppermute(value, "mp", [(i, (i - count) % n) for i in range(n)])


def sum_all(value):
    for axis in ("dp", "mp"):
        n = lax.axis_size(axis)
        bit = 1
        while bit < n:
            value = value + lax.ppermute(value, axis, [(i, i ^ bit) for i in range(n)])
            bit *= 2
    return value


def after(value, *others):
    return lax.optimization_barrier((value, others))[0]


def swap(value, bit):
    n = lax.axis_size("dp")
    return lax.ppermute(value, "dp", [(i, i ^ bit) for i in range(n)])


def dp_gather(value):
    return lax.all_gather(value, "dp", axis=0, tiled=True)


def paired():
    return lax.axis_size("dp") == 8


def split_columns(value):
    if not paired():
        return value[None]
    core = lax.axis_index("dp") % 2
    rows, width = value.shape
    shaped = value.reshape(rows, 4, 2, width // 8)

    def pick(which):
        return lax.dynamic_index_in_dim(shaped, which, 2, False).reshape(rows, width // 2)

    return jnp.stack([pick(core), pick(1 - core)])


def after_all(waits):
    return [pl.BlockSpec(memory_space=pl.ANY)] * len(waits)


def weight_kernel(joined, left_ref, right_ref, *refs):
    value = inner_rows(left_ref[...], right_ref[...])
    if joined:
        value = value + refs[0][...].astype(F32)
    refs[-1][...] = value.astype(BF16)


def weight_grad(left, right, side, height, width, micros, arrived=None, waits=()):
    depth, columns = left.shape[-2:]
    others = right.shape[1]
    specs = [
        pl.BlockSpec((None, depth, height), lambda i, j: (side, 0, i))
        if left.ndim == 3
        else pl.BlockSpec((depth, height), lambda i, j: (0, i)),
        pl.BlockSpec((depth, width), lambda i, j: (0, j)),
    ]
    args = [left, right]
    if arrived is not None:
        specs.append(pl.BlockSpec((height, width), lambda i, j: (i, j)))
        args.append(arrived)
    return pl.pallas_call(
        functools.partial(weight_kernel, arrived is not None),
        out_shape=jax.ShapeDtypeStruct((columns, others), BF16),
        grid=(columns // height, others // width),
        in_specs=specs + after_all(waits),
        out_specs=pl.BlockSpec((height, width), lambda i, j: (i, j)),
        compiler_params=params(),
        cost_estimate=cost(micros),
        name="weight_grad",
    )(*args, *waits)


def scatter_other(left, right, width, micros, waits=()):
    if not paired():
        return None
    return weight_grad(left, right, 1, left.shape[2], width, micros, waits=waits)


def chip_kernel(where_ref, left_ref, right_ref, arrived_ref, *refs):
    one_kept, one_sent, two_kept, two_sent, zero_ref, total = refs[-6:]
    zero_ref[0] = 0
    value = inner_rows(left_ref[...], right_ref[...]) + arrived_ref[...].astype(F32)
    total[...] = value.astype(BF16)
    x, y = where_ref[0], where_ref[1]
    rows = total.shape[0] // 4
    half = rows // 2
    for k in (0, 1):
        for one_ref, two_ref, near_x, near_y in (
            (one_kept, two_kept, x, y),
            (one_sent, two_sent, 1 - x, 1 - y),
        ):
            start = pl.multiple_of((2 * near_y + k) * rows, 16)
            one_ref[k] = total[pl.ds(start, half), :]
            start = pl.multiple_of((2 * k + near_x) * rows + half, 16)
            two_ref[k] = total[pl.ds(start, half), :]


def scatter_chip(where, left, right, width, micros, arrived, waits=()):
    depth, columns = left.shape[1:]
    others = right.shape[1]
    half = columns // 8
    out = jax.ShapeDtypeStruct((2, half, others), BF16)
    block = pl.BlockSpec((2, half, width), lambda j, w: (0, 0, j))
    *parts, zero = pl.pallas_call(
        chip_kernel,
        out_shape=(out, out, out, out, jax.ShapeDtypeStruct((1,), jnp.int32)),
        grid_spec=pltpu.PrefetchScalarGridSpec(
            num_scalar_prefetch=1,
            grid=(others // width,),
            in_specs=[
                pl.BlockSpec((None, depth, columns), lambda j, w: (0, 0, 0)),
                pl.BlockSpec((depth, width), lambda j, w: (0, j)),
                pl.BlockSpec((columns, width), lambda j, w: (0, j)),
            ]
            + after_all(waits),
            out_specs=(block, block, block, block, pl.BlockSpec(memory_space=pltpu.SMEM)),
            scratch_shapes=[pltpu.VMEM((columns, width), BF16)],
        ),
        compiler_params=params(),
        cost_estimate=cost(micros),
        name="scatter_chip",
    )(where, left, right, arrived, *waits)
    return parts, zero


def scatter_first(parts):
    return swap(parts[1], 4), swap(parts[3], 2)


def halves_kernel(where_ref, kept_ref, moved_ref, *refs):
    keep_ref, send_ref, total = refs[-3:]
    total[...] = (kept_ref[...].astype(F32) + moved_ref[...].astype(F32)).astype(BF16)
    keep_ref[...] = total[where_ref[0]]
    send_ref[...] = total[1 - where_ref[0]]


def halves(where, kept, moved, waits):
    whole = pl.BlockSpec(memory_space=pltpu.VMEM)
    out = jax.ShapeDtypeStruct(kept.shape[1:], BF16)
    return pl.pallas_call(
        halves_kernel,
        out_shape=(out, out),
        in_specs=[pl.BlockSpec(memory_space=pltpu.SMEM), whole, whole] + after_all(waits),
        out_specs=(whole, whole),
        scratch_shapes=[pltpu.VMEM(kept.shape, BF16)],
        compiler_params=params(),
        cost_estimate=cost(3),
        name="halves",
    )(where, kept, moved, *waits)


def scatter_halves(where, parts, moved, waits=()):
    return (
        halves(where[0:1], parts[0], moved[0], waits),
        halves(where[1:2], parts[2], moved[1], waits),
    )


def scatter_second(both):
    (one, one_sent), (two, two_sent) = both
    return [(one, swap(one_sent, 2)), (two, swap(two_sent, 4))]


def scatter_plain(left, right):
    return scatter_whole(inner_rows(left[0], right).astype(BF16))


def pass_kernel(*refs):
    pass


def gate(value, *waits):
    return pl.pallas_call(
        pass_kernel,
        out_shape=jax.ShapeDtypeStruct(value.shape, value.dtype),
        in_specs=after_all((value, *waits)),
        out_specs=pl.BlockSpec(memory_space=pl.ANY),
        input_output_aliases={0: 0},
        cost_estimate=cost(1),
        name="gate",
    )(value, *waits)


def join_kernel(one_ref, two_ref, *refs):
    out_ref, zero_ref = refs[-2:]
    out_ref[...] = (one_ref[...].astype(F32) + two_ref[...].astype(F32)).astype(BF16)
    zero_ref[0] = 0


def join_marked(one, two, waits=()):
    whole = pl.BlockSpec(memory_space=pltpu.VMEM)
    return pl.pallas_call(
        join_kernel,
        out_shape=(
            jax.ShapeDtypeStruct(one.shape, BF16),
            jax.ShapeDtypeStruct((1,), jnp.int32),
        ),
        in_specs=[whole, whole] + after_all(waits),
        out_specs=(whole, pl.BlockSpec(memory_space=pltpu.SMEM)),
        compiler_params=params(),
        cost_estimate=cost(3),
        name="join",
    )(one, two, *waits)


def join(one, two, waits=()):
    return join_marked(one, two, waits)[0]


def scatter_mine(left, right, width, micros, arrived, waits=()):
    return weight_grad(left, right, 0, left.shape[2], width, micros, arrived, waits)


def scatter_around(chip):
    share = lax.psum_scatter(
        chip,
        "dp",
        scatter_dimension=0,
        tiled=True,
        axis_index_groups=[[2 * k + core for k in AROUND] for core in (0, 1)],
    )
    return [(share, None)]


def scatter_whole(partial):
    share = lax.psum_scatter(partial, "dp", scatter_dimension=0, tiled=True)
    return [(share, None)]


def angle_tables():
    half = HD // 2
    rates = 10000.0 ** (-np.arange(half) * 2.0 / HD)
    angles = np.arange(LEN)[:, None] * rates[None, :]
    cosine, sine = np.cos(angles), np.sin(angles)
    return (
        jnp.asarray(np.concatenate([cosine] * 4, axis=-1), F32),
        jnp.asarray(np.concatenate([-sine, sine] * 2, axis=-1), F32),
    )


def swap_halves(value):
    lane = lax.broadcasted_iota(jnp.int32, value.shape, 1)
    low = (lane % HD) < HD // 2
    return jnp.where(
        low, pltpu.roll(value, LANES - HD // 2, 1), pltpu.roll(value, HD // 2, 1)
    )


AROUND = (0, 1, 3, 2)


def put_split(ref, value, core, chips=(0, 1, 2, 3)):
    if ref.shape[0] == 1:
        ref[0] = value
        return
    block = value.shape[1] // 8
    for which in (0, 1):

        @pl.when(core == which)
        def _():
            for side in (0, 1):
                for spot, chip in enumerate(chips):
                    start = (2 * chip + (which ^ side)) * block
                    ref[side, :, spot * block : (spot + 1) * block] = value[
                        :, start : start + block
                    ]


def split_shape(rows, width):
    return (2, rows, width // 2) if paired() else (1, rows, width)


def project_kernel(fresh, where_ref, x_ref, gain_ref, w_ref, cos_ref, sin_ref, *refs):
    qkv_ref, norm_ref, copy_ref, mark_ref, held = refs[-5:]
    mark_ref[...] = jnp.zeros_like(mark_ref)

    @pl.when(pl.program_id(0) == 0)
    def _():
        value = x_ref[...].astype(F32)
        factor = lax.rsqrt(jnp.mean(value * value, axis=-1, keepdims=True) + EPSILON)
        normed = (value * factor * gain_ref[...]).astype(BF16)
        held[...] = normed
        put_split(norm_ref, normed, where_ref[1])
        copy_ref[...] = x_ref[...]

    product = matmul(held[...], w_ref[...])
    cosine, sine = cos_ref[...], sin_ref[...]
    query = product[:, :LANES]
    key = product[:, LANES : 2 * LANES]
    query = (query * cosine + swap_halves(query) * sine).astype(BF16)
    qkv_ref[:, :LANES] = query * HD**-0.5
    qkv_ref[:, LANES : 2 * LANES] = (key * cosine + swap_halves(key) * sine).astype(BF16)
    qkv_ref[:, 2 * LANES :] = product[:, 2 * LANES :].astype(BF16)


def project(where, piece, gain, weights, tables, held):
    rows, width = piece.shape
    columns = weights.shape[1]
    block = 3 * LANES
    fresh = held is None
    outs = (
        jax.ShapeDtypeStruct((LEN, columns), BF16),
        jax.ShapeDtypeStruct(split_shape(LEN, width), BF16),
        jax.ShapeDtypeStruct((LEN, width), BF16),
        jax.ShapeDtypeStruct((8, LANES), F32),
    )
    specs = [
        pl.BlockSpec((rows, width), lambda i, w: (0, 0)),
        pl.BlockSpec((1, width), lambda i, w: (0, 0)),
        pl.BlockSpec((width, block), lambda i, w: (0, i)),
        pl.BlockSpec((rows, LANES), lambda i, w: (w[0], 0)),
        pl.BlockSpec((rows, LANES), lambda i, w: (w[0], 0)),
    ]
    args = [piece, gain, weights, *tables]
    aliases = {}
    if not fresh:
        for index, array in enumerate(held):
            aliases[1 + len(args)] = index
            args.append(array)
            specs.append(pl.BlockSpec(memory_space=pl.ANY))
    return pl.pallas_call(
        functools.partial(project_kernel, fresh),
        out_shape=outs,
        grid_spec=pltpu.PrefetchScalarGridSpec(
            num_scalar_prefetch=1,
            grid=(columns // block,),
            in_specs=specs,
            out_specs=(
                pl.BlockSpec((rows, block), lambda i, w: (w[0], i)),
                pl.BlockSpec(split_shape(rows, width), lambda i, w: (0, w[0], 0)),
                pl.BlockSpec((rows, width), lambda i, w: (w[0], 0)),
                pl.BlockSpec((8, LANES), lambda i, w: (0, 0)),
            ),
            scratch_shapes=[pltpu.VMEM((rows, width), BF16)],
        ),
        input_output_aliases=aliases,
        compiler_params=params(),
        cost_estimate=cost(11),
        name="project",
    )(where, *args)


PARTS = (
    (0, 512, ((0, 512, True),)),
    (512, 256, ((0, 512, False), (512, 256, True))),
    (768, 256, ((0, 768, False), (768, 256, True))),
)


def visible(shape, first_key, first_query, limit):
    key = first_key + lax.broadcasted_iota(jnp.int32, shape, 0)
    query = first_query + lax.broadcasted_iota(jnp.int32, shape, 1)
    return (key < limit) | (key <= query)


def head_only(value, head):
    lane = lax.broadcasted_iota(jnp.int32, value.shape, 1)
    return jnp.where((lane >= HD) == (head == 1), value, jnp.zeros_like(value))


def attend_kernel(heads, prefix_ref, qkv_ref, out_ref, send_ref, log_ref, turned):
    limit = prefix_ref[0]
    pair = pl.program_id(0)
    values_across = qkv_ref[:, 2 * LANES :].T
    for head in (0, 1):

        @pl.when(2 * pair + head < heads)
        def _():
            queries = head_only(qkv_ref[:, :LANES], head)
            for first, count, spans in PARTS:
                mine = queries[first : first + count]
                scores = []
                for start, keys, masked in spans:
                    raw = outer_cols(qkv_ref[start : start + keys, LANES : 2 * LANES], mine)
                    if masked:
                        raw = jnp.where(visible(raw.shape, start, first, limit), raw, MASKED)
                    scores.append(raw)
                top = functools.reduce(
                    jnp.maximum, [jnp.max(s, axis=0, keepdims=True) for s in scores]
                )
                total = jnp.zeros_like(top)
                summed = jnp.zeros((HD, count), F32)
                for (start, keys, _), raw in zip(spans, scores):
                    weight = jnp.exp(raw - top)
                    total = total + jnp.sum(weight, axis=0, keepdims=True)
                    summed = summed + matmul(
                        values_across[head * HD : (head + 1) * HD, start : start + keys],
                        weight.astype(BF16),
                    )
                turned[head * HD : (head + 1) * HD, first : first + count] = summed / total
                log_ref[0, head : head + 1, first : first + count] = top + jnp.log(total)

        @pl.when(2 * pair + head >= heads)
        def _():
            turned[head * HD : (head + 1) * HD, :] = jnp.zeros((HD, LEN), F32)
            log_ref[0, head : head + 1, :] = jnp.zeros((1, LEN), F32)

    value = turned[...].T.astype(BF16)
    out_ref[...] = value
    send_ref[...] = value


def attend(qkv, prefix, heads):
    pairs = qkv.shape[1] // (3 * LANES)
    return pl.pallas_call(
        functools.partial(attend_kernel, heads),
        out_shape=(
            jax.ShapeDtypeStruct((LEN, pairs * LANES), BF16),
            jax.ShapeDtypeStruct((LEN, pairs * LANES), BF16),
            jax.ShapeDtypeStruct((pairs, 2, LEN), F32),
        ),
        grid_spec=pltpu.PrefetchScalarGridSpec(
            num_scalar_prefetch=1,
            grid=(pairs,),
            in_specs=[pl.BlockSpec((LEN, 3 * LANES), lambda i, s: (0, i))],
            out_specs=(
                pl.BlockSpec((LEN, LANES), lambda i, s: (0, i)),
                pl.BlockSpec((LEN, LANES), lambda i, s: (0, i)),
                pl.BlockSpec((1, 2, LEN), lambda i, s: (i, 0, 0)),
            ),
            scratch_shapes=[pltpu.VMEM((LANES, LEN), F32)],
        ),
        compiler_params=params(),
        cost_estimate=cost(18),
        name="attend",
    )(prefix, qkv)


def attend_back_kernel(
    heads, count, prefix_ref, qkv_ref, out_ref, *refs
):
    arrived = refs[:count]
    log_ref, cos_ref, sin_ref = refs[count : count + 3]
    back_ref, turned, grad_key, grad_value, grad_ref = refs[-5:]
    limit = prefix_ref[0]
    rows = arrived[0].shape[0]
    for k in range(count):
        start = pl.multiple_of(lax.rem(prefix_ref[1] + k, count) * rows, rows)
        grad_ref[pl.ds(start, rows), :] = arrived[k][...]
    pair = pl.program_id(0)
    keys_across = qkv_ref[:, LANES : 2 * LANES].T
    inner = (out_ref[...].astype(F32) * grad_ref[...].astype(F32)).T
    grad_key[...] = jnp.zeros_like(grad_key)
    grad_value[...] = jnp.zeros_like(grad_value)
    for head in (0, 1):
        band = slice(head * HD, (head + 1) * HD)

        @pl.when(2 * pair + head < heads)
        def _():
            queries = head_only(qkv_ref[:, :LANES], head)
            grads = head_only(grad_ref[...], head)
            inner_row = jnp.sum(inner[band], axis=0, keepdims=True)
            for first, count, spans in PARTS:
                here = slice(first, first + count)
                mine, grad_mine = queries[here], grads[here]
                log_mine = log_ref[0, head : head + 1, here]
                inner_mine = inner_row[:, here]
                summed = jnp.zeros((HD, count), F32)
                for start, keys, masked in spans:
                    there = slice(start, start + keys)
                    raw = outer_cols(qkv_ref[there, LANES : 2 * LANES], mine)
                    chance = jnp.exp(raw - log_mine)
                    if masked:
                        chance = jnp.where(
                            visible(raw.shape, start, first, limit), chance, 0.0
                        )
                    grad_chance = outer_cols(qkv_ref[there, 2 * LANES :], grad_mine)
                    grad_score = (chance * (grad_chance - inner_mine)).astype(BF16)
                    grad_key[there, :] += matmul(grad_score, mine)
                    grad_value[there, :] += matmul(chance.astype(BF16), grad_mine)
                    summed = summed + matmul(keys_across[band, there], grad_score)
                turned[band, here] = summed

        @pl.when(2 * pair + head >= heads)
        def _():
            turned[band, :] = jnp.zeros((HD, LEN), F32)

    cosine, sine = cos_ref[...], sin_ref[...]
    grad_query = turned[...].T * HD**-0.5
    back_ref[:, :LANES] = (grad_query * cosine - swap_halves(grad_query) * sine).astype(BF16)
    back = grad_key[...]
    back_ref[:, LANES : 2 * LANES] = (back * cosine - swap_halves(back) * sine).astype(BF16)
    back_ref[:, 2 * LANES :] = grad_value[...].astype(BF16)


def attend_back(qkv, attended, arrived, log_total, tables, prefix, heads, waits=()):
    pairs = qkv.shape[1] // (3 * LANES)
    count, rows = len(arrived), arrived[0].shape[0]
    return pl.pallas_call(
        functools.partial(attend_back_kernel, heads, count),
        out_shape=jax.ShapeDtypeStruct(qkv.shape, BF16),
        grid_spec=pltpu.PrefetchScalarGridSpec(
            num_scalar_prefetch=1,
            grid=(pairs,),
            in_specs=[
                pl.BlockSpec((LEN, 3 * LANES), lambda i, s: (0, i)),
                pl.BlockSpec((LEN, LANES), lambda i, s: (0, i)),
            ]
            + [pl.BlockSpec((rows, LANES), lambda i, s: (0, i))] * count
            + [
                pl.BlockSpec((1, 2, LEN), lambda i, s: (i, 0, 0)),
                pl.BlockSpec((LEN, LANES), lambda i, s: (0, 0)),
                pl.BlockSpec((LEN, LANES), lambda i, s: (0, 0)),
            ]
            + after_all(waits),
            out_specs=pl.BlockSpec((LEN, 3 * LANES), lambda i, s: (0, i)),
            scratch_shapes=[
                pltpu.VMEM((LANES, LEN), F32),
                pltpu.VMEM((LEN, LANES), F32),
                pltpu.VMEM((LEN, LANES), F32),
                pltpu.VMEM((LEN, LANES), BF16),
            ],
        ),
        compiler_params=params(),
        cost_estimate=cost(28),
        name="attend_back",
    )(prefix, qkv, attended, *arrived, log_total, *tables, *waits)


def middle_kernel(count, place_ref, *refs):
    pieces = refs[:count]
    w_ref, x_ref, gain_ref, normed_ref, split_ref, own_ref = refs[count:]
    depth = pieces[0].shape[1]
    total = None
    for k in range(count):
        term = outer_cols(pieces[k][...], w_ref[:, k * depth : (k + 1) * depth])
        total = term if total is None else total + term
    middle = x_ref[...].astype(F32) + BRANCH * total
    factor = lax.rsqrt(jnp.mean(middle * middle, axis=-1, keepdims=True) + EPSILON)
    normed = (middle * factor * gain_ref[...]).astype(BF16)
    normed_ref[...] = normed
    put_split(split_ref, normed, place_ref[1], AROUND)
    rows, own = x_ref.shape[0], own_ref.shape[0]
    for part in range(rows // own):

        @pl.when(pl.program_id(0) * (rows // own) + part == place_ref[0])
        def _():
            own_ref[...] = middle[part * own : (part + 1) * own]


def finish_middle(place, pieces, weights, tokens, gain, own):
    width = tokens.shape[1]
    depth = pieces[0].shape[1]
    count = len(pieces)
    rows = 2 * own
    return pl.pallas_call(
        functools.partial(middle_kernel, count),
        out_shape=(
            jax.ShapeDtypeStruct((LEN, width), BF16),
            jax.ShapeDtypeStruct(split_shape(LEN, width), BF16),
            jax.ShapeDtypeStruct((own, width), F32),
        ),
        grid_spec=pltpu.PrefetchScalarGridSpec(
            num_scalar_prefetch=1,
            grid=(LEN // rows,),
            in_specs=[pl.BlockSpec((rows, depth), lambda i, s: (i, 0))] * count
            + [
                pl.BlockSpec((width, count * depth), lambda i, s: (0, 0)),
                pl.BlockSpec((rows, width), lambda i, s: (i, 0)),
                pl.BlockSpec((1, width), lambda i, s: (0, 0)),
            ],
            out_specs=(
                pl.BlockSpec((rows, width), lambda i, s: (i, 0)),
                pl.BlockSpec(split_shape(rows, width), lambda i, s: (0, i, 0)),
                pl.BlockSpec((own, width), lambda i, s: (0, 0)),
            ),
        ),
        compiler_params=params(),
        cost_estimate=cost(22),
        name="finish_middle",
    )(place, *pieces, weights, tokens, gain)


def gate_kernel(normed_ref, weight_ref, hidden_ref, slope_ref):
    rows = 256
    for start in range(0, LEN, rows):
        here = slice(start, start + rows)
        product = matmul(normed_ref[here], weight_ref[...])
        gate, up = product[:, :FF_BLOCK], product[:, FF_BLOCK:]
        sigmoid = jax.nn.sigmoid(gate)
        silu = gate * sigmoid
        hidden_ref[here, :] = (silu * up).astype(BF16)
        slope_ref[here, :FF_BLOCK] = (up * (sigmoid + silu * (1.0 - sigmoid))).astype(BF16)
        slope_ref[here, FF_BLOCK:] = silu.astype(BF16)


def feed(normed, gate_up):
    width = normed.shape[1]
    hidden = gate_up.shape[1] // 2
    return pl.pallas_call(
        gate_kernel,
        out_shape=(
            jax.ShapeDtypeStruct((LEN, hidden), BF16),
            jax.ShapeDtypeStruct((LEN, 2 * hidden), BF16),
        ),
        grid=(hidden // FF_BLOCK,),
        in_specs=[
            pl.BlockSpec((LEN, width), lambda i: (0, 0)),
            pl.BlockSpec((width, 2 * FF_BLOCK), lambda i: (0, i)),
        ],
        out_specs=(
            pl.BlockSpec((LEN, FF_BLOCK), lambda i: (0, i)),
            pl.BlockSpec((LEN, 2 * FF_BLOCK), lambda i: (0, i)),
        ),
        compiler_params=params(),
        cost_estimate=cost(21),
        name="feed",
    )(normed, gate_up)


def feed_back_kernel(where_ref, grad_ref, slope_ref, down_ref, weight_ref, *refs):
    both_ref, copy_ref, sum_ref, total = refs[-4:]
    step = pl.program_id(0)

    @pl.when(step == 0)
    def _():
        put_split(copy_ref, grad_ref[...], where_ref[1], AROUND)
        total[...] = jnp.zeros_like(total)

    grad = matmul(grad_ref[...], down_ref[...])
    grads = jnp.concatenate([grad, grad], axis=1)
    both = (grads * slope_ref[...].astype(F32)).astype(BF16)
    both_ref[...] = both
    total[...] += outer_cols(both, weight_ref[...])

    @pl.when(step == pl.num_programs(0) - 1)
    def _():
        sum_ref[...] = total[...].astype(sum_ref.dtype)


def feed_back(where, piece, slopes, down, gate_up, held, kind, waits=()):
    rows, width = piece.shape
    hidden = down.shape[1]
    specs = [
        pl.BlockSpec((rows, width), lambda i, w: (0, 0)),
        pl.BlockSpec((rows, 2 * FF_BLOCK), lambda i, w: (w[0], i)),
        pl.BlockSpec((width, FF_BLOCK), lambda i, w: (0, i)),
        pl.BlockSpec((width, 2 * FF_BLOCK), lambda i, w: (0, i)),
    ]
    args = [piece, slopes, down, gate_up]
    aliases = {}
    if held is not None:
        for index, array in enumerate(held):
            aliases[1 + len(args)] = index
            args.append(array)
            specs.append(pl.BlockSpec(memory_space=pl.ANY))
    args += waits
    specs += after_all(waits)
    return pl.pallas_call(
        feed_back_kernel,
        out_shape=(
            jax.ShapeDtypeStruct((LEN, 2 * hidden), BF16),
            jax.ShapeDtypeStruct(split_shape(LEN, width), BF16),
            jax.ShapeDtypeStruct((rows, width), kind),
        ),
        grid_spec=pltpu.PrefetchScalarGridSpec(
            num_scalar_prefetch=1,
            grid=(hidden // FF_BLOCK,),
            in_specs=specs,
            out_specs=(
                pl.BlockSpec((rows, 2 * FF_BLOCK), lambda i, w: (w[0], i)),
                pl.BlockSpec(split_shape(rows, width), lambda i, w: (0, w[0], 0)),
                pl.BlockSpec((rows, width), lambda i, w: (0, 0)),
            ),
            scratch_shapes=[pltpu.VMEM((rows, width), F32)],
        ),
        input_output_aliases=aliases,
        compiler_params=params(),
        cost_estimate=cost(15),
        name="feed_back",
    )(where, *args)


def out_sum_kernel(parts, count, width, *refs):
    terms, outs = grouped(parts, refs)
    outs = outs[-count:]
    half = outs[0].shape[0] // len(parts)
    for index, pair in enumerate(terms):
        value = added(pair)
        here = slice(index * half, (index + 1) * half)
        for k in range(count):
            outs[k][here, :] = value[:, k * width : (k + 1) * width].astype(outs[k].dtype)


def out_sum(parts, count, width, waits=()):
    rows = len(parts) * parts[0][0].shape[0]
    arrays = [a for pair in parts for a in pair if a is not None]
    return pl.pallas_call(
        functools.partial(out_sum_kernel, parts_mask(parts), count, width),
        out_shape=tuple(
            jax.ShapeDtypeStruct((rows, width), BF16 if k else F32) for k in range(count)
        ),
        in_specs=[pl.BlockSpec(memory_space=pltpu.VMEM)] * len(arrays) + after_all(waits),
        compiler_params=params(),
        cost_estimate=cost(3),
        name="out_sum",
    )(*arrays, *waits)


def out_final_kernel(count, *refs):
    total = refs[0][...]
    for ref in refs[1:count]:
        total = total + ref[...].astype(F32)
    refs[-1][...] = total[:, : refs[-1].shape[1]]


def out_final(own, moved, width, waits):
    whole = pl.BlockSpec(memory_space=pltpu.VMEM)
    count = 1 + len(moved)
    return pl.pallas_call(
        functools.partial(out_final_kernel, count),
        out_shape=jax.ShapeDtypeStruct((own.shape[0], width), F32),
        in_specs=[whole] * count + after_all(waits),
        out_specs=whole,
        compiler_params=params(),
        cost_estimate=cost(3),
        name="out_final",
    )(own, *moved, *waits)


def spread_kernel(count, value_ref, weight_ref, *refs):
    product = matmul(value_ref[...], weight_ref[...]).astype(BF16)
    refs[-1][0] = 0
    for k in range(count):

        @pl.when(pl.program_id(0) == k)
        def _():
            refs[k][...] = product


def spread(value, weights, count):
    rows, depth = value.shape
    width = weights.shape[1] // count
    return pl.pallas_call(
        functools.partial(spread_kernel, count),
        out_shape=tuple(jax.ShapeDtypeStruct((rows, width), BF16) for _ in range(count))
        + (jax.ShapeDtypeStruct((1,), jnp.int32),),
        grid=(count,),
        in_specs=[
            pl.BlockSpec((rows, depth), lambda i: (0, 0)),
            pl.BlockSpec((depth, width), lambda i: (0, i)),
        ],
        out_specs=tuple(pl.BlockSpec((rows, width), lambda i: (0, 0)) for _ in range(count))
        + (pl.BlockSpec(memory_space=pltpu.SMEM),),
        compiler_params=params(),
        cost_estimate=cost(8),
        name="spread",
    )(value, weights)


def norm_back(value, gain, incoming):
    factor = lax.rsqrt(jnp.mean(value * value, axis=-1, keepdims=True) + EPSILON)
    normed = value * factor
    scaled_in = incoming * gain
    inner = jnp.mean(scaled_in * normed, axis=-1, keepdims=True)
    return (
        factor * (scaled_in - normed * inner),
        jnp.sum(incoming * normed, axis=0, keepdims=True),
    )


def own_back_kernel(
    core_ref, term_ref, arrived_ref, middle_ref, grad_ref, gain_ref, *refs
):
    sum_ref, send_ref, split_ref, gain_sum_ref, zero_ref = refs[-5:]
    incoming = term_ref[...].astype(F32) + arrived_ref[...].astype(F32)
    back, gain_sum = norm_back(middle_ref[...], gain_ref[...], incoming)
    total = grad_ref[...].astype(F32) + back
    sum_ref[...] = total
    sent = (BRANCH * total).astype(BF16)
    send_ref[...] = sent
    put_split(split_ref, sent, core_ref[0])
    zero_ref[0] = 0

    @pl.when(pl.program_id(0) == 0)
    def _():
        gain_sum_ref[...] = jnp.zeros_like(gain_sum_ref)

    gain_sum_ref[...] += gain_sum


def own_back(core, term, arrived, middle, grad, gain, waits=()):
    rows, width = middle.shape
    step = rows // 2
    block = pl.BlockSpec((step, width), lambda i, s: (i, 0))
    line = pl.BlockSpec((1, width), lambda i, s: (0, 0))
    return pl.pallas_call(
        own_back_kernel,
        out_shape=(
            jax.ShapeDtypeStruct((rows, width), F32),
            jax.ShapeDtypeStruct((rows, width), BF16),
            jax.ShapeDtypeStruct(split_shape(rows, width), BF16),
            jax.ShapeDtypeStruct((1, width), F32),
            jax.ShapeDtypeStruct((1,), jnp.int32),
        ),
        grid_spec=pltpu.PrefetchScalarGridSpec(
            num_scalar_prefetch=1,
            grid=(2,),
            in_specs=[block, block, block, block, line] + after_all(waits),
            out_specs=(
                block,
                block,
                pl.BlockSpec(split_shape(step, width), lambda i, s: (0, i, 0)),
                line,
                pl.BlockSpec(memory_space=pltpu.SMEM),
            ),
        ),
        compiler_params=params(),
        cost_estimate=cost(5),
        name="own_back",
    )(core, term, arrived, middle, grad, gain, *waits)


def finish_input_kernel(term_ref, arrived_ref, x_ref, sum_ref, gain_ref, *refs):
    out_ref, gain_sum_ref, zero_ref = refs[-3:]
    incoming = term_ref[...] + arrived_ref[...].astype(F32)
    back, gain_sum = norm_back(x_ref[...].astype(F32), gain_ref[...], incoming)
    out_ref[...] = (sum_ref[...] + back).astype(BF16)
    zero_ref[0] = 0

    @pl.when(pl.program_id(0) == 0)
    def _():
        gain_sum_ref[...] = jnp.zeros_like(gain_sum_ref)

    gain_sum_ref[...] += gain_sum


def finish_input(term, arrived, x, total, gain, waits=()):
    rows, width = x.shape
    block = pl.BlockSpec((rows // 2, width), lambda i: (i, 0))
    line = pl.BlockSpec((1, width), lambda i: (0, 0))
    return pl.pallas_call(
        finish_input_kernel,
        out_shape=(
            jax.ShapeDtypeStruct((rows, width), BF16),
            jax.ShapeDtypeStruct((1, width), F32),
            jax.ShapeDtypeStruct((1,), jnp.int32),
        ),
        grid=(2,),
        in_specs=[block, block, block, block, line] + after_all(waits),
        out_specs=(block, line, pl.BlockSpec(memory_space=pltpu.SMEM)),
        compiler_params=params(),
        cost_estimate=cost(5),
        name="finish_input",
    )(term, arrived, x, total, gain, *waits)


def finish_block_kernel(middle_ref, term_ref, arrived_ref, *refs):
    total = term_ref[...] + arrived_ref[...].astype(F32)
    refs[-1][...] = (middle_ref[...] + BRANCH * total).astype(BF16)


def finish_block(middle, term, arrived, waits=()):
    rows, width = middle.shape
    block = pl.BlockSpec((rows // 2, width), lambda i: (i, 0))
    return pl.pallas_call(
        finish_block_kernel,
        out_shape=jax.ShapeDtypeStruct((rows, width), BF16),
        grid=(2,),
        in_specs=[block, block, block] + after_all(waits),
        out_specs=block,
        compiler_params=params(),
        cost_estimate=cost(3),
        name="finish_block",
    )(middle, term, arrived, *waits)


def mix(out_ref, refs, block):
    width = refs[0].shape[1]
    count = len(refs)
    for first in range(0, width, block):
        size = min(block, width - first)
        base = first * count
        for index, ref in enumerate(refs):
            spot = base + index * block
            out_ref[:, spot : spot + size] = ref[:, first : first + size]
            if size < block:
                out_ref[:, spot + size : spot + block] = jnp.zeros(
                    (ref.shape[0], block - size), out_ref.dtype
                )


def pack_kernel(count, block, *refs):
    mix(refs[-1], refs[:count], block)


def pack(values, block, width, *waits):
    count = len(values)
    rows = values[0].shape[0]
    whole = pl.BlockSpec(memory_space=pltpu.VMEM)
    return pl.pallas_call(
        functools.partial(pack_kernel, count, block),
        out_shape=jax.ShapeDtypeStruct((rows, count * width), BF16),
        in_specs=[whole] * count + after_all(waits),
        out_specs=whole,
        compiler_params=params(),
        cost_estimate=cost(3),
        name="pack",
    )(*values, *waits)


def chain_kernel(count, *refs):
    out_ref = refs[-1]
    width = refs[0].shape[1]
    for k in range(count):
        out_ref[:, k * width : (k + 1) * width] = refs[k][...]


def chain(values, *waits):
    rows, width = values[0].shape
    whole = pl.BlockSpec(memory_space=pltpu.VMEM)
    return pl.pallas_call(
        functools.partial(chain_kernel, len(values)),
        out_shape=jax.ShapeDtypeStruct((rows, len(values) * width), values[0].dtype),
        in_specs=[whole] * len(values) + after_all(waits),
        out_specs=whole,
        compiler_params=params(),
        cost_estimate=cost(2),
        name="chain",
    )(*values, *waits)


def own_rows_kernel(count, place_ref, *refs):
    width = refs[0].shape[1]
    for k in range(count):
        refs[-1][:, k * width : (k + 1) * width] = refs[k][...]


def own_rows(place, pieces, rows):
    width = pieces[0].shape[1]
    count = len(pieces)
    return pl.pallas_call(
        functools.partial(own_rows_kernel, count),
        out_shape=jax.ShapeDtypeStruct((rows, count * width), pieces[0].dtype),
        grid_spec=pltpu.PrefetchScalarGridSpec(
            num_scalar_prefetch=1,
            grid=(1,),
            in_specs=[pl.BlockSpec((rows, width), lambda i, s: (s[0], 0))] * count,
            out_specs=pl.BlockSpec((rows, count * width), lambda i, s: (0, 0)),
        ),
        compiler_params=params(),
        cost_estimate=cost(2),
        name="own_rows",
    )(place, *pieces)


def scale_kernel(value_ref, *refs):
    refs[-1][...] = (BRANCH * value_ref[...].astype(F32)).astype(BF16)


def scaled(value, *waits):
    whole = pl.BlockSpec(memory_space=pltpu.VMEM)
    return pl.pallas_call(
        scale_kernel,
        out_shape=jax.ShapeDtypeStruct(value.shape, BF16),
        in_specs=[whole] + [pl.BlockSpec(memory_space=pl.ANY)] * len(waits),
        out_specs=whole,
        compiler_params=params(),
        cost_estimate=cost(3),
        name="scaled",
    )(value, *waits)


def added(terms):
    one, two = terms
    value = one[...].astype(F32)
    return value if two is None else value + two[...].astype(F32)


def grouped(parts, refs):
    refs = list(refs)
    out = [tuple(None if a is None else refs.pop(0) for a in pair) for pair in parts]
    return out, refs


def unmix_kernel(parts, block, count, *refs):
    terms, outs = grouped(parts, refs)
    outs = outs[-count:]
    width = outs[0].shape[1]
    half = outs[0].shape[0] // len(parts)
    for index, pair in enumerate(terms):
        value = added(pair)
        for first in range(0, width, block):
            size = min(block, width - first)
            for turn, out_ref in enumerate(outs):
                spot = first * len(outs) + turn * block
                out_ref[index * half : (index + 1) * half, first : first + size] = value[
                    :, spot : spot + size
                ]


def unmix(parts, count, block, width, waits=()):
    rows = len(parts) * parts[0][0].shape[0]
    arrays = [a for pair in parts for a in pair if a is not None]
    return pl.pallas_call(
        functools.partial(unmix_kernel, parts_mask(parts), block, count),
        out_shape=tuple(jax.ShapeDtypeStruct((rows, width), F32) for _ in range(count)),
        in_specs=[pl.BlockSpec(memory_space=pltpu.VMEM)] * len(arrays) + after_all(waits),
        compiler_params=params(),
        cost_estimate=cost(3),
        name="unmix",
    )(*arrays, *waits)


def parts_mask(parts):
    return [tuple(None if a is None else True for a in pair) for pair in parts]


def body(
    tokens,
    attn_gain,
    mlp_gain,
    w_query,
    w_key,
    w_value,
    w_out,
    w_gate,
    w_up,
    w_down,
    prefix,
    out_grad,
):
    mp = lax.axis_size("mp")
    place = lax.axis_index("mp")
    rows = tokens.shape[0]
    width_heads = w_query.shape[1]
    heads = width_heads // HD
    padded_heads = round_up(width_heads, LANES)
    width_ff = w_gate.shape[1]
    padded_ff = round_up(width_ff, FF_BLOCK)
    own = place * rows

    def row_block(value, index):
        return lax.dynamic_slice_in_dim(value, index * rows, rows, 0)

    tables = angle_tables()
    core = lax.axis_index("dp") % 2
    at = [jnp.stack([(place + mp - k) % mp, core]) for k in range(mp)]

    attn_pack = pack([w_query, w_key, w_value], LANES, padded_heads)
    attn_weights = dp_gather(attn_pack)
    ff_pack = pack([w_gate, w_up], FF_BLOCK, padded_ff, attn_pack)
    gate_up = dp_gather(ff_pack)
    token_pieces = ring_gather(tokens)
    held = None
    for k in range(mp - 1):
        *held, mark = project(
            at[k], token_pieces[k], attn_gain[None], attn_weights, tables, held
        )
    out_own = pack([w_out.T], LANES, padded_heads, token_pieces[-1], mark, ff_pack)
    out_pieces = [out_own] + [shift_back(out_own, mp - j) for j in range(1, mp)]
    *held, _ = project(
        at[mp - 1], token_pieces[-1], attn_gain[None], attn_weights, tables, held
    )
    qkv, normed_one, whole_tokens = held
    attended, attended_send, log_total = attend(qkv, prefix, heads)
    out_pack = chain(out_pieces, attended)
    attended_pieces = [attended, ring_up(gate(attended_send, out_pack))]
    out_weights = dp_gather(gate(out_pack, attended_pieces[1], gate_up))
    down_pack = pack([w_down.T], LANES, padded_ff, attended_pieces[1])
    down = dp_gather(down_pack)
    while len(attended_pieces) < mp:
        attended_pieces.append(ring_up(attended_pieces[-1]))

    grad_pieces = [scaled(out_grad, attended_pieces[-1], down_pack, out_weights)]
    grad_pieces.append(ring_up(grad_pieces[0]))
    normed_two, split_two, middle = finish_middle(
        at[0], attended_pieces, out_weights, whole_tokens, mlp_gain[None], rows
    )
    grad_pieces.append(ring_up(gate(grad_pieces[1], normed_two)))
    hidden, slopes = feed(normed_two, gate_up)
    while len(grad_pieces) < mp:
        grad_pieces.append(ring_up(grad_pieces[-1]))
    by_chip = paired()

    def back_of(k, held, kind=BF16, waits=()):
        *held, term = feed_back(
            at[k % mp], grad_pieces[k % mp], slopes, down, gate_up, held, kind, waits
        )
        return held, term

    width = normed_two.shape[1]
    grad_pieces.append(ring_up(grad_pieces[-1]))
    held, total = back_of(1, None, waits=(grad_pieces[2],))
    arrived = ring_up(total)
    held, term = back_of(2, held, waits=(grad_pieces[3],))
    held, term_three = back_of(3, held)
    total = join(term, arrived, (term_three,))
    arrived = ring_up(total)
    (grad_both, grad_mlp), term_own = back_of(mp, held, F32, (total,))
    attended_own = own_rows(at[0], attended_pieces, rows)
    if by_chip:
        down_other = scatter_other(grad_mlp, hidden, 768, 6)
        total = join(term_three, arrived, (down_other,))
        arrived = ring_up(total)
        ff_other = scatter_other(split_two, grad_both, 1024, 11, (total,))
        down_chip = scatter_mine(
            grad_mlp, hidden, 768, 6, swap(gate(down_other, total), 1), (ff_other,)
        )
        waits = (down_chip, ff_other, attended_own)
    else:
        total = join(term_three, arrived)
        arrived = ring_up(total)
        waits = (attended_own,)
    grad_middle, grad_attn, split_attn, gain_two, zero = own_back(
        core[None], term_own, arrived, middle, out_grad, mlp_gain[None], waits
    )
    *mine, zero = spread(grad_attn, out_weights, mp)
    def mlp_chunk(k, zero):
        return lax.optimization_barrier(
            outer_cols(row_block(hidden, at[k % mp][0] + zero[0]), down)
        )

    arrived = [mine[0]] + [shift_back(mine[k], k) for k in range(1, mp)]
    chunk_one = mlp_chunk(1, zero).astype(BF16)
    if by_chip:
        ff_chip = scatter_mine(
            split_two, grad_both, 1024, 11, swap(gate(ff_other, split_attn), 1), (chunk_one,)
        )
        ff_share = scatter_around(ff_chip)
        down_share = scatter_around(gate(down_chip, zero))
        waits = (ff_chip,)
    else:
        ff_share = scatter_plain(split_two, grad_both)
        down_share = scatter_plain(grad_mlp, hidden)
        waits = ()
    out_other = scatter_other(split_attn, attended_own, 1280, 5, (chunk_one,))
    mlp_arrived = ring_up(gate(chunk_one, *arrived[1:]))
    out_arrived = swap(out_other, 1) if by_chip else None
    spots = jnp.stack([prefix[0], place])
    back = attend_back(
        qkv, attended, arrived, log_total, tables, spots, heads,
        (*waits, out_other) if by_chip else (),
    )

    def grad_one_term(k, zero=0):
        return lax.optimization_barrier(
            outer_cols(row_block(back, at[k % mp][0] + zero), attn_weights)
        )

    total = grad_one_term(1).astype(BF16)
    arrived = ring_up(total)
    index = lax.axis_index("dp")
    chip = jnp.stack([index // 2 % 2, index // 4])
    if by_chip:
        attn_other = scatter_other(normed_one, back, 640, 8, (total, mlp_arrived))
        attn_arrived = swap(attn_other, 1)
        out_parts, zero = scatter_chip(
            chip, split_attn, attended_own, 1280, 8, out_arrived, (total, attn_other)
        )
        out_moved = scatter_first(out_parts)
        chunk = mlp_chunk(2, zero)
        total, zero = join_marked(
            grad_one_term(2, zero[0]), arrived,
            (attn_other, out_parts[1], out_parts[3], chunk),
        )
        arrived = ring_up(total)
        mlp_total = join(chunk, mlp_arrived, (total,))
        mlp_arrived = ring_up(mlp_total)
        attn_parts, zero = scatter_chip(
            chip, normed_one, back, 640, 10, attn_arrived, (total, mlp_total)
        )
        attn_moved = scatter_first(attn_parts)
        term = grad_one_term(3, zero[0])
        chunk = mlp_chunk(3, zero)
        total, zero = join_marked(term, arrived, (attn_parts[1], attn_parts[3], chunk))
        arrived = ring_up(total)
        term = grad_one_term(4, zero[0])
        out_half = scatter_halves(chip, out_parts, out_moved, (total,))
        out_share = scatter_second(out_half)
        mlp_total = join(chunk, mlp_arrived, (total, out_half[0][1], out_half[1][1]))
        mlp_arrived = ring_up(mlp_total)
        attn_half = scatter_halves(chip, attn_parts, attn_moved, (mlp_total,))
        attn_share = scatter_second(attn_half)
        waits = (mlp_total, attn_half[0][1], attn_half[1][1])
    else:
        out_share = scatter_plain(split_attn, attended_own)
        attn_share = scatter_plain(normed_one, back)
        total = join(grad_one_term(2), arrived)
        arrived = ring_up(total)
        mlp_arrived = ring_up(join(mlp_chunk(2, zero), mlp_arrived))
        total = join(grad_one_term(3), arrived)
        arrived = ring_up(total)
        mlp_arrived = ring_up(join(mlp_chunk(3, zero), mlp_arrived))
        term = grad_one_term(4)
        waits = ()
    input_grad, gain_one, zero = finish_input(
        term, arrived, tokens, grad_middle, attn_gain[None], waits
    )
    out_total, *out_mine = out_sum(out_share, mp, padded_heads, (mlp_arrived,))
    out_moved = [shift_back(out_mine[k - 1], k) for k in range(1, mp)]
    gains = sum_all(jnp.concatenate([gain_one, gain_two]))
    chunk = mlp_chunk(4, zero)
    grad_w_query, grad_w_key, grad_w_value = unmix(attn_share, 3, LANES, width_heads)
    grad_w_gate, grad_w_up = unmix(ff_share, 2, FF_BLOCK, width_ff)
    (grad_w_down,) = unmix(down_share, 1, LANES, width_ff)
    grad_w_out = out_final(
        out_total, out_moved, width_heads, (grad_w_gate, grad_w_down, grad_w_query)
    )
    block_out = finish_block(middle, chunk, mlp_arrived, (grad_w_out,))
    return (
        block_out,
        input_grad,
        grad_w_query,
        grad_w_key,
        grad_w_value,
        grad_w_out.T,
        grad_w_gate,
        grad_w_up,
        grad_w_down.T,
        gains[0],
        gains[1],
    )


def solution(mesh):
    return jax.shard_map(
        body,
        mesh=mesh,
        in_specs=(
            P(("dp", "mp"), None),
            P(),
            P(),
            P("dp", "mp"),
            P("dp", "mp"),
            P("dp", "mp"),
            P("mp", "dp"),
            P("dp", "mp"),
            P("dp", "mp"),
            P("mp", "dp"),
            P("dp"),
            P(("dp", "mp"), None),
        ),
        out_specs=(
            P(("dp", "mp"), None),
            P(("dp", "mp"), None),
            P("dp", "mp"),
            P("dp", "mp"),
            P("dp", "mp"),
            P("mp", "dp"),
            P("dp", "mp"),
            P("dp", "mp"),
            P("mp", "dp"),
            P(),
            P(),
        ),
        check_vma=False,
    )
```

```python
import functools

import jax
import jax.numpy as jnp
import numpy as np
from jax import lax
from jax.experimental import pallas as pl
from jax.experimental.pallas import tpu as pltpu
from jax.sharding import PartitionSpec as P

HD = 64
LEN = 1024
LANES = 128
EPSILON = 1e-05
BRANCH = 1.4 / 40**0.5
MASKED = -1e30
FF_BLOCK = 512
VMEM_LIMIT = 56 * 1024 * 1024

F32 = jnp.float32
BF16 = jnp.bfloat16


def round_up(value, unit):
    return -(-value // unit) * unit


def matmul(left, right):
    return jnp.dot(left, right, preferred_element_type=F32)


def inner_rows(left, right):
    return lax.dot_general(
        left, right, (((0,), (0,)), ((), ())), preferred_element_type=F32
    )


def outer_cols(left, right):
    return lax.dot_general(
        left, right, (((1,), (1,)), ((), ())), preferred_element_type=F32
    )


def cost(micros):
    return pl.CostEstimate(
        flops=int(micros * 3.0e9), bytes_accessed=0, transcendentals=0
    )


def params(limit=VMEM_LIMIT):
    return pltpu.CompilerParams(vmem_limit_bytes=limit)


def ring_up(value):
    n = lax.axis_size("mp")
    return lax.ppermute(value, "mp", [(i, (i + 1) % n) for i in range(n)])


def ring_gather(value):
    pieces = [value]
    for _ in range(lax.axis_size("mp") - 1):
        pieces.append(ring_up(pieces[-1]))
    return pieces


def ring_scatter(part):
    n = lax.axis_size("mp")
    place = lax.axis_index("mp")
    total = part((place + n - 1) % n)
    for step in range(1, n):
        sent = total.astype(BF16)
        arrived = ring_up(sent)
        term = lax.optimization_barrier(part((place + 2 * n - 1 - step) % n))
        total = term + arrived.astype(F32)
    return total


def shift_back(value, count):
    n = lax.axis_size("mp")
    return lax.ppermute(value, "mp", [(i, (i - count) % n) for i in range(n)])


def sum_over(value, axis):
    n = lax.axis_size(axis)
    bit = 1
    while bit < n:
        value = value + lax.ppermute(value, axis, [(i, i ^ bit) for i in range(n)])
        bit *= 2
    return value


def swap(value, bit):
    n = lax.axis_size("dp")
    return lax.ppermute(value, "dp", [(i, i ^ bit) for i in range(n)])


def dp_gather(value):
    return lax.all_gather(value, "dp", axis=0, tiled=True)


def paired():
    return lax.axis_size("dp") == 8


def split_columns(value):
    if not paired():
        return value[None]
    core = lax.axis_index("dp") % 2
    rows, width = value.shape
    shaped = value.reshape(rows, 4, 2, width // 8)

    def pick(which):
        return lax.dynamic_index_in_dim(shaped, which, 2, False).reshape(rows, width // 2)

    return jnp.stack([pick(core), pick(1 - core)])


def after_all(waits):
    return [pl.BlockSpec(memory_space=pl.ANY)] * len(waits)


def weight_kernel(joined, left_ref, right_ref, *refs):
    value = inner_rows(left_ref[...], right_ref[...])
    if joined:
        value = value + refs[0][...].astype(F32)
    refs[-1][...] = value.astype(BF16)


def weight_grad(left, right, side, height, width, micros, arrived=None, waits=()):
    depth, columns = left.shape[-2:]
    others = right.shape[1]
    specs = [
        pl.BlockSpec((None, depth, height), lambda i, j: (side, 0, i))
        if left.ndim == 3
        else pl.BlockSpec((depth, height), lambda i, j: (0, i)),
        pl.BlockSpec((depth, width), lambda i, j: (0, j)),
    ]
    args = [left, right]
    if arrived is not None:
        specs.append(pl.BlockSpec((height, width), lambda i, j: (i, j)))
        args.append(arrived)
    return pl.pallas_call(
        functools.partial(weight_kernel, arrived is not None),
        out_shape=jax.ShapeDtypeStruct((columns, others), BF16),
        grid=(columns // height, others // width),
        in_specs=specs + after_all(waits),
        out_specs=pl.BlockSpec((height, width), lambda i, j: (i, j)),
        compiler_params=params(),
        cost_estimate=cost(micros),
        name="weight_grad",
    )(*args, *waits)


def scatter_other(left, right, width, micros, waits=()):
    if not paired():
        return None
    return weight_grad(left, right, 1, left.shape[2], width, micros, waits=waits)


def chip_kernel(where_ref, left_ref, right_ref, arrived_ref, *refs):
    one_kept, one_sent, two_kept, two_sent, zero_ref, total = refs[-6:]
    zero_ref[0] = 0
    value = inner_rows(left_ref[...], right_ref[...]) + arrived_ref[...].astype(F32)
    total[...] = value.astype(BF16)
    x, y = where_ref[0], where_ref[1]
    rows = total.shape[0] // 4
    half = rows // 2
    for k in (0, 1):
        for one_ref, two_ref, near_x, near_y in (
            (one_kept, two_kept, x, y),
            (one_sent, two_sent, 1 - x, 1 - y),
        ):
            start = pl.multiple_of((2 * near_y + k) * rows, 16)
            one_ref[k] = total[pl.ds(start, half), :]
            start = pl.multiple_of((2 * k + near_x) * rows + half, 16)
            two_ref[k] = total[pl.ds(start, half), :]


def scatter_chip(where, left, right, width, micros, arrived, waits=()):
    depth, columns = left.shape[1:]
    others = right.shape[1]
    half = columns // 8
    out = jax.ShapeDtypeStruct((2, half, others), BF16)
    block = pl.BlockSpec((2, half, width), lambda j, w: (0, 0, j))
    *parts, zero = pl.pallas_call(
        chip_kernel,
        out_shape=(out, out, out, out, jax.ShapeDtypeStruct((1,), jnp.int32)),
        grid_spec=pltpu.PrefetchScalarGridSpec(
            num_scalar_prefetch=1,
            grid=(others // width,),
            in_specs=[
                pl.BlockSpec((None, depth, columns), lambda j, w: (0, 0, 0)),
                pl.BlockSpec((depth, width), lambda j, w: (0, j)),
                pl.BlockSpec((columns, width), lambda j, w: (0, j)),
            ]
            + after_all(waits),
            out_specs=(block, block, block, block, pl.BlockSpec(memory_space=pltpu.SMEM)),
            scratch_shapes=[pltpu.VMEM((columns, width), BF16)],
        ),
        compiler_params=params(),
        cost_estimate=cost(micros),
        name="scatter_chip",
    )(where, left, right, arrived, *waits)
    return parts, zero


def scatter_first(parts):
    return swap(parts[1], 4), swap(parts[3], 2)


def halves_kernel(where_ref, kept_ref, moved_ref, *refs):
    keep_ref, send_ref, total = refs[-3:]
    total[...] = (kept_ref[...].astype(F32) + moved_ref[...].astype(F32)).astype(BF16)
    keep_ref[...] = total[where_ref[0]]
    send_ref[...] = total[1 - where_ref[0]]


def halves(where, kept, moved, waits):
    whole = pl.BlockSpec(memory_space=pltpu.VMEM)
    out = jax.ShapeDtypeStruct(kept.shape[1:], BF16)
    return pl.pallas_call(
        halves_kernel,
        out_shape=(out, out),
        in_specs=[pl.BlockSpec(memory_space=pltpu.SMEM), whole, whole] + after_all(waits),
        out_specs=(whole, whole),
        scratch_shapes=[pltpu.VMEM(kept.shape, BF16)],
        compiler_params=params(),
        cost_estimate=cost(3),
        name="halves",
    )(where, kept, moved, *waits)


def scatter_halves(where, parts, moved, waits=()):
    return (
        halves(where[0:1], parts[0], moved[0], waits),
        halves(where[1:2], parts[2], moved[1], waits),
    )


def scatter_second(both):
    (one, one_sent), (two, two_sent) = both
    return [(one, swap(one_sent, 2)), (two, swap(two_sent, 4))]


def scatter_plain(left, right):
    return scatter_whole(inner_rows(left[0], right).astype(BF16))


def pass_kernel(*refs):
    pass


def gate(value, *waits):
    return pl.pallas_call(
        pass_kernel,
        out_shape=jax.ShapeDtypeStruct(value.shape, value.dtype),
        in_specs=after_all((value, *waits)),
        out_specs=pl.BlockSpec(memory_space=pl.ANY),
        input_output_aliases={0: 0},
        cost_estimate=cost(1),
        name="gate",
    )(value, *waits)


def join_kernel(one_ref, two_ref, *refs):
    out_ref, zero_ref = refs[-2:]
    out_ref[...] = (one_ref[...].astype(F32) + two_ref[...].astype(F32)).astype(BF16)
    zero_ref[0] = 0


def join_marked(one, two, waits=()):
    whole = pl.BlockSpec(memory_space=pltpu.VMEM)
    return pl.pallas_call(
        join_kernel,
        out_shape=(
            jax.ShapeDtypeStruct(one.shape, BF16),
            jax.ShapeDtypeStruct((1,), jnp.int32),
        ),
        in_specs=[whole, whole] + after_all(waits),
        out_specs=(whole, pl.BlockSpec(memory_space=pltpu.SMEM)),
        compiler_params=params(),
        cost_estimate=cost(3),
        name="join",
    )(one, two, *waits)


def join(one, two, waits=()):
    return join_marked(one, two, waits)[0]


def scatter_mine(left, right, width, micros, arrived, waits=()):
    return weight_grad(left, right, 0, left.shape[2], width, micros, arrived, waits)


def scatter_around(chip):
    share = lax.psum_scatter(
        chip,
        "dp",
        scatter_dimension=0,
        tiled=True,
        axis_index_groups=[[2 * k + core for k in AROUND] for core in (0, 1)],
    )
    return [(share, None)]


def scatter_whole(partial):
    share = lax.psum_scatter(partial, "dp", scatter_dimension=0, tiled=True)
    return [(share, None)]


def angle_tables():
    half = HD // 2
    rates = 10000.0 ** (-np.arange(half) * 2.0 / HD)
    angles = np.arange(LEN)[:, None] * rates[None, :]
    cosine, sine = np.cos(angles), np.sin(angles)
    return (
        jnp.asarray(np.concatenate([cosine] * 4, axis=-1), F32),
        jnp.asarray(np.concatenate([-sine, sine] * 2, axis=-1), F32),
    )


def swap_halves(value):
    lane = lax.broadcasted_iota(jnp.int32, value.shape, 1)
    low = (lane % HD) < HD // 2
    return jnp.where(
        low, pltpu.roll(value, LANES - HD // 2, 1), pltpu.roll(value, HD // 2, 1)
    )


AROUND = (0, 1, 3, 2)


def put_split(ref, value, core, chips=(0, 1, 2, 3), rows=slice(None)):
    if ref.shape[0] == 1:
        ref[0, rows, :] = value
        return
    block = value.shape[1] // 8
    for which in (0, 1):

        @pl.when(core == which)
        def _():
            for side in (0, 1):
                for spot, chip in enumerate(chips):
                    start = (2 * chip + (which ^ side)) * block
                    ref[side, rows, spot * block : (spot + 1) * block] = value[
                        :, start : start + block
                    ]


def split_shape(rows, width):
    return (2, rows, width // 2) if paired() else (1, rows, width)


def normed_of(value, gain):
    value = value.astype(F32)
    factor = lax.rsqrt(jnp.mean(value * value, axis=-1, keepdims=True) + EPSILON)
    return (value * factor * gain).astype(BF16)


def project_kernel(where_ref, x_ref, gain_ref, w_ref, cos_ref, sin_ref, *refs):
    qkv_ref, mark_ref, held = refs[-3:]

    @pl.when(pl.program_id(0) == 0)
    def _():
        mark_ref[...] = jnp.zeros_like(mark_ref)
        held[...] = normed_of(x_ref[...], gain_ref[...])

    product = matmul(held[...], w_ref[...])
    cosine, sine = cos_ref[...], sin_ref[...]
    query = product[:, :LANES]
    key = product[:, LANES : 2 * LANES]
    query = (query * cosine + swap_halves(query) * sine).astype(BF16)
    qkv_ref[:, :LANES] = query * HD**-0.5
    qkv_ref[:, LANES : 2 * LANES] = (key * cosine + swap_halves(key) * sine).astype(BF16)
    qkv_ref[:, 2 * LANES :] = product[:, 2 * LANES :].astype(BF16)


def project(where, piece, gain, weights, tables, held):
    rows, width = piece.shape
    columns = weights.shape[1]
    block = 3 * LANES
    specs = [
        pl.BlockSpec((rows, width), lambda i, w: (0, 0)),
        pl.BlockSpec((1, width), lambda i, w: (0, 0)),
        pl.BlockSpec((width, block), lambda i, w: (0, i)),
        pl.BlockSpec((rows, LANES), lambda i, w: (w[0], 0)),
        pl.BlockSpec((rows, LANES), lambda i, w: (w[0], 0)),
    ]
    args = [piece, gain, weights, *tables]
    aliases = {}
    if held is not None:
        aliases[1 + len(args)] = 0
        args.append(held)
        specs.append(pl.BlockSpec(memory_space=pl.ANY))
    return pl.pallas_call(
        project_kernel,
        out_shape=(
            jax.ShapeDtypeStruct((LEN, columns), BF16),
            jax.ShapeDtypeStruct((8, LANES), F32),
        ),
        grid_spec=pltpu.PrefetchScalarGridSpec(
            num_scalar_prefetch=1,
            grid=(columns // block,),
            in_specs=specs,
            out_specs=(
                pl.BlockSpec((rows, block), lambda i, w: (w[0], i)),
                pl.BlockSpec((8, LANES), lambda i, w: (0, 0)),
            ),
            scratch_shapes=[pltpu.VMEM((rows, width), BF16)],
        ),
        input_output_aliases=aliases,
        compiler_params=params(),
        cost_estimate=cost(9),
        name="project",
    )(where, *args)


def lay_tokens_kernel(count, place_ref, gain_ref, *refs):
    norm_ref, copy_ref = refs[-2:]
    rows = refs[0].shape[0]
    for k in range(count):
        start = pl.multiple_of(lax.rem(place_ref[0] + count - k, count) * rows, rows)
        here = pl.ds(start, rows)
        copy_ref[here, :] = refs[k][...]
        put_split(norm_ref, normed_of(refs[k][...], gain_ref[...]), place_ref[1], rows=here)


def lay_tokens(place, pieces, gain, waits):
    rows, width = pieces[0].shape
    count = len(pieces)
    whole = pl.BlockSpec(memory_space=pltpu.VMEM)
    return pl.pallas_call(
        functools.partial(lay_tokens_kernel, count),
        out_shape=(
            jax.ShapeDtypeStruct(split_shape(count * rows, width), BF16),
            jax.ShapeDtypeStruct((count * rows, width), BF16),
        ),
        in_specs=[pl.BlockSpec(memory_space=pltpu.SMEM)] + [whole] * (1 + count)
        + after_all(waits),
        out_specs=(whole, whole),
        compiler_params=params(),
        cost_estimate=cost(10),
        name="lay_tokens",
    )(place, gain, *pieces, *waits)


PARTS = (
    (0, 512, ((0, 512, True),)),
    (512, 256, ((0, 512, False), (512, 256, True))),
    (768, 256, ((0, 768, False), (768, 256, True))),
)


def visible(shape, first_key, first_query, limit):
    key = first_key + lax.broadcasted_iota(jnp.int32, shape, 0)
    query = first_query + lax.broadcasted_iota(jnp.int32, shape, 1)
    return (key < limit) | (key <= query)


def head_only(value, head):
    lane = lax.broadcasted_iota(jnp.int32, value.shape, 1)
    return jnp.where((lane >= HD) == (head == 1), value, jnp.zeros_like(value))


def attend_kernel(heads, prefix_ref, qkv_ref, out_ref, send_ref, log_ref, turned):
    limit = prefix_ref[0]
    pair = pl.program_id(0)
    values_across = qkv_ref[:, 2 * LANES :].T
    for head in (0, 1):

        @pl.when(2 * pair + head < heads)
        def _():
            queries = head_only(qkv_ref[:, :LANES], head)
            for first, count, spans in PARTS:
                mine = queries[first : first + count]
                scores = []
                for start, keys, masked in spans:
                    raw = outer_cols(qkv_ref[start : start + keys, LANES : 2 * LANES], mine)
                    if masked:
                        raw = jnp.where(visible(raw.shape, start, first, limit), raw, MASKED)
                    scores.append(raw)
                top = functools.reduce(
                    jnp.maximum, [jnp.max(s, axis=0, keepdims=True) for s in scores]
                )
                total = jnp.zeros_like(top)
                summed = jnp.zeros((HD, count), F32)
                for (start, keys, _), raw in zip(spans, scores):
                    weight = jnp.exp(raw - top)
                    total = total + jnp.sum(weight, axis=0, keepdims=True)
                    summed = summed + matmul(
                        values_across[head * HD : (head + 1) * HD, start : start + keys],
                        weight.astype(BF16),
                    )
                turned[head * HD : (head + 1) * HD, first : first + count] = summed / total
                log_ref[0, head : head + 1, first : first + count] = top + jnp.log(total)

        @pl.when(2 * pair + head >= heads)
        def _():
            turned[head * HD : (head + 1) * HD, :] = jnp.zeros((HD, LEN), F32)
            log_ref[0, head : head + 1, :] = jnp.zeros((1, LEN), F32)

    value = turned[...].T.astype(BF16)
    out_ref[...] = value
    send_ref[...] = value


def attend(qkv, prefix, heads):
    pairs = qkv.shape[1] // (3 * LANES)
    return pl.pallas_call(
        functools.partial(attend_kernel, heads),
        out_shape=(
            jax.ShapeDtypeStruct((LEN, pairs * LANES), BF16),
            jax.ShapeDtypeStruct((LEN, pairs * LANES), BF16),
            jax.ShapeDtypeStruct((pairs, 2, LEN), F32),
        ),
        grid_spec=pltpu.PrefetchScalarGridSpec(
            num_scalar_prefetch=1,
            grid=(pairs,),
            in_specs=[pl.BlockSpec((LEN, 3 * LANES), lambda i, s: (0, i))],
            out_specs=(
                pl.BlockSpec((LEN, LANES), lambda i, s: (0, i)),
                pl.BlockSpec((LEN, LANES), lambda i, s: (0, i)),
                pl.BlockSpec((1, 2, LEN), lambda i, s: (i, 0, 0)),
            ),
            scratch_shapes=[pltpu.VMEM((LANES, LEN), F32)],
        ),
        compiler_params=params(),
        cost_estimate=cost(18),
        name="attend",
    )(prefix, qkv)


def attend_back_kernel(
    heads, count, prefix_ref, qkv_ref, out_ref, *refs
):
    arrived = refs[:count]
    log_ref, cos_ref, sin_ref = refs[count : count + 3]
    back_ref, turned, grad_key, grad_value, grad_ref = refs[-5:]
    limit = prefix_ref[0]
    rows = arrived[0].shape[0]
    for k in range(count):
        start = pl.multiple_of(lax.rem(prefix_ref[1] + k, count) * rows, rows)
        grad_ref[pl.ds(start, rows), :] = arrived[k][...]
    pair = pl.program_id(0)
    keys_across = qkv_ref[:, LANES : 2 * LANES].T
    inner = (out_ref[...].astype(F32) * grad_ref[...].astype(F32)).T
    grad_key[...] = jnp.zeros_like(grad_key)
    grad_value[...] = jnp.zeros_like(grad_value)
    for head in (0, 1):
        band = slice(head * HD, (head + 1) * HD)

        @pl.when(2 * pair + head < heads)
        def _():
            queries = head_only(qkv_ref[:, :LANES], head)
            grads = head_only(grad_ref[...], head)
            inner_row = jnp.sum(inner[band], axis=0, keepdims=True)
            for first, count, spans in PARTS:
                here = slice(first, first + count)
                mine, grad_mine = queries[here], grads[here]
                log_mine = log_ref[0, head : head + 1, here]
                inner_mine = inner_row[:, here]
                summed = jnp.zeros((HD, count), F32)
                for start, keys, masked in spans:
                    there = slice(start, start + keys)
                    raw = outer_cols(qkv_ref[there, LANES : 2 * LANES], mine)
                    chance = jnp.exp(raw - log_mine)
                    if masked:
                        chance = jnp.where(
                            visible(raw.shape, start, first, limit), chance, 0.0
                        )
                    grad_chance = outer_cols(qkv_ref[there, 2 * LANES :], grad_mine)
                    grad_score = (chance * (grad_chance - inner_mine)).astype(BF16)
                    grad_key[there, :] += matmul(grad_score, mine)
                    grad_value[there, :] += matmul(chance.astype(BF16), grad_mine)
                    summed = summed + matmul(keys_across[band, there], grad_score)
                turned[band, here] = summed

        @pl.when(2 * pair + head >= heads)
        def _():
            turned[band, :] = jnp.zeros((HD, LEN), F32)

    cosine, sine = cos_ref[...], sin_ref[...]
    grad_query = turned[...].T * HD**-0.5
    back_ref[:, :LANES] = (grad_query * cosine - swap_halves(grad_query) * sine).astype(BF16)
    back = grad_key[...]
    back_ref[:, LANES : 2 * LANES] = (back * cosine - swap_halves(back) * sine).astype(BF16)
    back_ref[:, 2 * LANES :] = grad_value[...].astype(BF16)


def attend_back(qkv, attended, arrived, log_total, tables, prefix, heads, waits=()):
    pairs = qkv.shape[1] // (3 * LANES)
    count, rows = len(arrived), arrived[0].shape[0]
    return pl.pallas_call(
        functools.partial(attend_back_kernel, heads, count),
        out_shape=jax.ShapeDtypeStruct(qkv.shape, BF16),
        grid_spec=pltpu.PrefetchScalarGridSpec(
            num_scalar_prefetch=1,
            grid=(pairs,),
            in_specs=[
                pl.BlockSpec((LEN, 3 * LANES), lambda i, s: (0, i)),
                pl.BlockSpec((LEN, LANES), lambda i, s: (0, i)),
            ]
            + [pl.BlockSpec((rows, LANES), lambda i, s: (0, i))] * count
            + [
                pl.BlockSpec((1, 2, LEN), lambda i, s: (i, 0, 0)),
                pl.BlockSpec((LEN, LANES), lambda i, s: (0, 0)),
                pl.BlockSpec((LEN, LANES), lambda i, s: (0, 0)),
            ]
            + after_all(waits),
            out_specs=pl.BlockSpec((LEN, 3 * LANES), lambda i, s: (0, i)),
            scratch_shapes=[
                pltpu.VMEM((LANES, LEN), F32),
                pltpu.VMEM((LEN, LANES), F32),
                pltpu.VMEM((LEN, LANES), F32),
                pltpu.VMEM((LEN, LANES), BF16),
            ],
        ),
        compiler_params=params(),
        cost_estimate=cost(28),
        name="attend_back",
    )(prefix, qkv, attended, *arrived, log_total, *tables, *waits)


def middle_kernel(count, place_ref, *refs):
    pieces = refs[:count]
    w_ref, x_ref, gain_ref, normed_ref, split_ref, own_ref = refs[count:]
    depth = pieces[0].shape[1]
    total = None
    for k in range(count):
        term = outer_cols(pieces[k][...], w_ref[:, k * depth : (k + 1) * depth])
        total = term if total is None else total + term
    middle = x_ref[...].astype(F32) + BRANCH * total
    factor = lax.rsqrt(jnp.mean(middle * middle, axis=-1, keepdims=True) + EPSILON)
    normed = (middle * factor * gain_ref[...]).astype(BF16)
    normed_ref[...] = normed
    put_split(split_ref, normed, place_ref[1], AROUND)
    rows, own = x_ref.shape[0], own_ref.shape[0]
    for part in range(rows // own):

        @pl.when(pl.program_id(0) * (rows // own) + part == place_ref[0])
        def _():
            own_ref[...] = middle[part * own : (part + 1) * own]


def finish_middle(place, pieces, weights, tokens, gain, own):
    width = tokens.shape[1]
    depth = pieces[0].shape[1]
    count = len(pieces)
    rows = 2 * own
    return pl.pallas_call(
        functools.partial(middle_kernel, count),
        out_shape=(
            jax.ShapeDtypeStruct((LEN, width), BF16),
            jax.ShapeDtypeStruct(split_shape(LEN, width), BF16),
            jax.ShapeDtypeStruct((own, width), F32),
        ),
        grid_spec=pltpu.PrefetchScalarGridSpec(
            num_scalar_prefetch=1,
            grid=(LEN // rows,),
            in_specs=[pl.BlockSpec((rows, depth), lambda i, s: (i, 0))] * count
            + [
                pl.BlockSpec((width, count * depth), lambda i, s: (0, 0)),
                pl.BlockSpec((rows, width), lambda i, s: (i, 0)),
                pl.BlockSpec((1, width), lambda i, s: (0, 0)),
            ],
            out_specs=(
                pl.BlockSpec((rows, width), lambda i, s: (i, 0)),
                pl.BlockSpec(split_shape(rows, width), lambda i, s: (0, i, 0)),
                pl.BlockSpec((own, width), lambda i, s: (0, 0)),
            ),
        ),
        compiler_params=params(),
        cost_estimate=cost(22),
        name="finish_middle",
    )(place, *pieces, weights, tokens, gain)


def gate_kernel(normed_ref, weight_ref, hidden_ref, slope_ref):
    rows = 256
    for start in range(0, LEN, rows):
        here = slice(start, start + rows)
        product = matmul(normed_ref[here], weight_ref[...])
        gate, up = product[:, :FF_BLOCK], product[:, FF_BLOCK:]
        sigmoid = jax.nn.sigmoid(gate)
        silu = gate * sigmoid
        hidden_ref[here, :] = (silu * up).astype(BF16)
        slope_ref[here, :FF_BLOCK] = (up * (sigmoid + silu * (1.0 - sigmoid))).astype(BF16)
        slope_ref[here, FF_BLOCK:] = silu.astype(BF16)


def feed(normed, gate_up):
    width = normed.shape[1]
    hidden = gate_up.shape[1] // 2
    return pl.pallas_call(
        gate_kernel,
        out_shape=(
            jax.ShapeDtypeStruct((LEN, hidden), BF16),
            jax.ShapeDtypeStruct((LEN, 2 * hidden), BF16),
        ),
        grid=(hidden // FF_BLOCK,),
        in_specs=[
            pl.BlockSpec((LEN, width), lambda i: (0, 0)),
            pl.BlockSpec((width, 2 * FF_BLOCK), lambda i: (0, i)),
        ],
        out_specs=(
            pl.BlockSpec((LEN, FF_BLOCK), lambda i: (0, i)),
            pl.BlockSpec((LEN, 2 * FF_BLOCK), lambda i: (0, i)),
        ),
        compiler_params=params(),
        cost_estimate=cost(21),
        name="feed",
    )(normed, gate_up)


def feed_back_kernel(where_ref, grad_ref, slope_ref, down_ref, weight_ref, *refs):
    both_ref, copy_ref, sum_ref, total = refs[-4:]
    step = pl.program_id(0)

    @pl.when(step == 0)
    def _():
        put_split(copy_ref, grad_ref[...], where_ref[1], AROUND)
        total[...] = jnp.zeros_like(total)

    grad = matmul(grad_ref[...], down_ref[...])
    grads = jnp.concatenate([grad, grad], axis=1)
    both = (grads * slope_ref[...].astype(F32)).astype(BF16)
    both_ref[...] = both
    total[...] += outer_cols(both, weight_ref[...])

    @pl.when(step == pl.num_programs(0) - 1)
    def _():
        sum_ref[...] = total[...].astype(sum_ref.dtype)


def feed_back(where, piece, slopes, down, gate_up, held, kind, waits=()):
    rows, width = piece.shape
    hidden = down.shape[1]
    specs = [
        pl.BlockSpec((rows, width), lambda i, w: (0, 0)),
        pl.BlockSpec((rows, 2 * FF_BLOCK), lambda i, w: (w[0], i)),
        pl.BlockSpec((width, FF_BLOCK), lambda i, w: (0, i)),
        pl.BlockSpec((width, 2 * FF_BLOCK), lambda i, w: (0, i)),
    ]
    args = [piece, slopes, down, gate_up]
    aliases = {}
    if held is not None:
        for index, array in enumerate(held):
            aliases[1 + len(args)] = index
            args.append(array)
            specs.append(pl.BlockSpec(memory_space=pl.ANY))
    args += waits
    specs += after_all(waits)
    return pl.pallas_call(
        feed_back_kernel,
        out_shape=(
            jax.ShapeDtypeStruct((LEN, 2 * hidden), BF16),
            jax.ShapeDtypeStruct(split_shape(LEN, width), BF16),
            jax.ShapeDtypeStruct((rows, width), kind),
        ),
        grid_spec=pltpu.PrefetchScalarGridSpec(
            num_scalar_prefetch=1,
            grid=(hidden // FF_BLOCK,),
            in_specs=specs,
            out_specs=(
                pl.BlockSpec((rows, 2 * FF_BLOCK), lambda i, w: (w[0], i)),
                pl.BlockSpec(split_shape(rows, width), lambda i, w: (0, w[0], 0)),
                pl.BlockSpec((rows, width), lambda i, w: (0, 0)),
            ),
            scratch_shapes=[pltpu.VMEM((rows, width), F32)],
        ),
        input_output_aliases=aliases,
        compiler_params=params(),
        cost_estimate=cost(15),
        name="feed_back",
    )(where, *args)


def out_sum_kernel(parts, count, width, *refs):
    terms, outs = grouped(parts, refs)
    outs = outs[-count:]
    half = outs[0].shape[0] // len(parts)
    for index, pair in enumerate(terms):
        value = added(pair)
        here = slice(index * half, (index + 1) * half)
        for k in range(count):
            outs[k][here, :] = value[:, k * width : (k + 1) * width].astype(outs[k].dtype)


def out_sum(parts, count, width, waits=()):
    rows = len(parts) * parts[0][0].shape[0]
    arrays = [a for pair in parts for a in pair if a is not None]
    return pl.pallas_call(
        functools.partial(out_sum_kernel, parts_mask(parts), count, width),
        out_shape=tuple(
            jax.ShapeDtypeStruct((rows, width), BF16 if k else F32) for k in range(count)
        ),
        in_specs=[pl.BlockSpec(memory_space=pltpu.VMEM)] * len(arrays) + after_all(waits),
        compiler_params=params(),
        cost_estimate=cost(3),
        name="out_sum",
    )(*arrays, *waits)


def out_final_kernel(count, *refs):
    total = refs[0][...]
    for ref in refs[1:count]:
        total = total + ref[...].astype(F32)
    refs[-1][...] = total[:, : refs[-1].shape[1]]


def out_final(own, moved, width, waits):
    whole = pl.BlockSpec(memory_space=pltpu.VMEM)
    count = 1 + len(moved)
    return pl.pallas_call(
        functools.partial(out_final_kernel, count),
        out_shape=jax.ShapeDtypeStruct((own.shape[0], width), F32),
        in_specs=[whole] * count + after_all(waits),
        out_specs=whole,
        compiler_params=params(),
        cost_estimate=cost(3),
        name="out_final",
    )(own, *moved, *waits)


def spread_kernel(count, value_ref, weight_ref, *refs):
    product = matmul(value_ref[...], weight_ref[...]).astype(BF16)
    refs[-1][0] = 0
    for k in range(count):

        @pl.when(pl.program_id(0) == k)
        def _():
            refs[k][...] = product


def spread(value, weights, count):
    rows, depth = value.shape
    width = weights.shape[1] // count
    return pl.pallas_call(
        functools.partial(spread_kernel, count),
        out_shape=tuple(jax.ShapeDtypeStruct((rows, width), BF16) for _ in range(count))
        + (jax.ShapeDtypeStruct((1,), jnp.int32),),
        grid=(count,),
        in_specs=[
            pl.BlockSpec((rows, depth), lambda i: (0, 0)),
            pl.BlockSpec((depth, width), lambda i: (0, i)),
        ],
        out_specs=tuple(pl.BlockSpec((rows, width), lambda i: (0, 0)) for _ in range(count))
        + (pl.BlockSpec(memory_space=pltpu.SMEM),),
        compiler_params=params(),
        cost_estimate=cost(8),
        name="spread",
    )(value, weights)


def norm_back(value, gain, incoming):
    factor = lax.rsqrt(jnp.mean(value * value, axis=-1, keepdims=True) + EPSILON)
    normed = value * factor
    scaled_in = incoming * gain
    inner = jnp.mean(scaled_in * normed, axis=-1, keepdims=True)
    return (
        factor * (scaled_in - normed * inner),
        jnp.sum(incoming * normed, axis=0, keepdims=True),
    )


def own_back_kernel(
    core_ref, term_ref, arrived_ref, middle_ref, grad_ref, gain_ref, *refs
):
    sum_ref, send_ref, split_ref, gain_sum_ref, zero_ref = refs[-5:]
    incoming = term_ref[...].astype(F32) + arrived_ref[...].astype(F32)
    back, gain_sum = norm_back(middle_ref[...], gain_ref[...], incoming)
    total = grad_ref[...].astype(F32) + back
    sum_ref[...] = total
    sent = (BRANCH * total).astype(BF16)
    send_ref[...] = sent
    put_split(split_ref, sent, core_ref[0])
    zero_ref[0] = 0

    @pl.when(pl.program_id(0) == 0)
    def _():
        gain_sum_ref[...] = jnp.zeros_like(gain_sum_ref)

    gain_sum_ref[...] += gain_sum


def own_back(core, term, arrived, middle, grad, gain, waits=()):
    rows, width = middle.shape
    step = rows // 2
    block = pl.BlockSpec((step, width), lambda i, s: (i, 0))
    line = pl.BlockSpec((1, width), lambda i, s: (0, 0))
    return pl.pallas_call(
        own_back_kernel,
        out_shape=(
            jax.ShapeDtypeStruct((rows, width), F32),
            jax.ShapeDtypeStruct((rows, width), BF16),
            jax.ShapeDtypeStruct(split_shape(rows, width), BF16),
            jax.ShapeDtypeStruct((1, width), F32),
            jax.ShapeDtypeStruct((1,), jnp.int32),
        ),
        grid_spec=pltpu.PrefetchScalarGridSpec(
            num_scalar_prefetch=1,
            grid=(2,),
            in_specs=[block, block, block, block, line] + after_all(waits),
            out_specs=(
                block,
                block,
                pl.BlockSpec(split_shape(step, width), lambda i, s: (0, i, 0)),
                line,
                pl.BlockSpec(memory_space=pltpu.SMEM),
            ),
        ),
        compiler_params=params(),
        cost_estimate=cost(5),
        name="own_back",
    )(core, term, arrived, middle, grad, gain, *waits)


def finish_input_kernel(term_ref, arrived_ref, x_ref, sum_ref, gain_ref, *refs):
    out_ref, gain_sum_ref, zero_ref = refs[-3:]
    incoming = term_ref[...] + arrived_ref[...].astype(F32)
    back, gain_sum = norm_back(x_ref[...].astype(F32), gain_ref[...], incoming)
    out_ref[...] = (sum_ref[...] + back).astype(BF16)
    zero_ref[0] = 0

    @pl.when(pl.program_id(0) == 0)
    def _():
        gain_sum_ref[...] = jnp.zeros_like(gain_sum_ref)

    gain_sum_ref[...] += gain_sum


def finish_input(term, arrived, x, total, gain, waits=()):
    rows, width = x.shape
    block = pl.BlockSpec((rows // 2, width), lambda i: (i, 0))
    line = pl.BlockSpec((1, width), lambda i: (0, 0))
    return pl.pallas_call(
        finish_input_kernel,
        out_shape=(
            jax.ShapeDtypeStruct((rows, width), BF16),
            jax.ShapeDtypeStruct((1, width), F32),
            jax.ShapeDtypeStruct((1,), jnp.int32),
        ),
        grid=(2,),
        in_specs=[block, block, block, block, line] + after_all(waits),
        out_specs=(block, line, pl.BlockSpec(memory_space=pltpu.SMEM)),
        compiler_params=params(),
        cost_estimate=cost(5),
        name="finish_input",
    )(term, arrived, x, total, gain, *waits)


def finish_block_kernel(middle_ref, term_ref, arrived_ref, *refs):
    total = term_ref[...] + arrived_ref[...].astype(F32)
    refs[-1][...] = (middle_ref[...] + BRANCH * total).astype(BF16)


def finish_block(middle, term, arrived, waits=()):
    rows, width = middle.shape
    block = pl.BlockSpec((rows // 2, width), lambda i: (i, 0))
    return pl.pallas_call(
        finish_block_kernel,
        out_shape=jax.ShapeDtypeStruct((rows, width), BF16),
        grid=(2,),
        in_specs=[block, block, block] + after_all(waits),
        out_specs=block,
        compiler_params=params(),
        cost_estimate=cost(3),
        name="finish_block",
    )(middle, term, arrived, *waits)


def mix(out_ref, refs, block):
    width = refs[0].shape[1]
    count = len(refs)
    for first in range(0, width, block):
        size = min(block, width - first)
        base = first * count
        for index, ref in enumerate(refs):
            spot = base + index * block
            out_ref[:, spot : spot + size] = ref[:, first : first + size]
            if size < block:
                out_ref[:, spot + size : spot + block] = jnp.zeros(
                    (ref.shape[0], block - size), out_ref.dtype
                )


def pack_kernel(count, block, *refs):
    mix(refs[-1], refs[:count], block)


def pack(values, block, width, *waits):
    count = len(values)
    rows = values[0].shape[0]
    whole = pl.BlockSpec(memory_space=pltpu.VMEM)
    return pl.pallas_call(
        functools.partial(pack_kernel, count, block),
        out_shape=jax.ShapeDtypeStruct((rows, count * width), BF16),
        in_specs=[whole] * count + after_all(waits),
        out_specs=whole,
        compiler_params=params(),
        cost_estimate=cost(3),
        name="pack",
    )(*values, *waits)


def chain_kernel(count, *refs):
    out_ref = refs[-1]
    width = refs[0].shape[1]
    for k in range(count):
        out_ref[:, k * width : (k + 1) * width] = refs[k][...]


def chain(values, *waits):
    rows, width = values[0].shape
    whole = pl.BlockSpec(memory_space=pltpu.VMEM)
    return pl.pallas_call(
        functools.partial(chain_kernel, len(values)),
        out_shape=jax.ShapeDtypeStruct((rows, len(values) * width), values[0].dtype),
        in_specs=[whole] * len(values) + after_all(waits),
        out_specs=whole,
        compiler_params=params(),
        cost_estimate=cost(2),
        name="chain",
    )(*values, *waits)


def own_rows_kernel(count, place_ref, *refs):
    width = refs[0].shape[1]
    for k in range(count):
        refs[-1][:, k * width : (k + 1) * width] = refs[k][...]


def own_rows(place, pieces, rows):
    width = pieces[0].shape[1]
    count = len(pieces)
    return pl.pallas_call(
        functools.partial(own_rows_kernel, count),
        out_shape=jax.ShapeDtypeStruct((rows, count * width), pieces[0].dtype),
        grid_spec=pltpu.PrefetchScalarGridSpec(
            num_scalar_prefetch=1,
            grid=(1,),
            in_specs=[pl.BlockSpec((rows, width), lambda i, s: (s[0], 0))] * count,
            out_specs=pl.BlockSpec((rows, count * width), lambda i, s: (0, 0)),
        ),
        compiler_params=params(),
        cost_estimate=cost(2),
        name="own_rows",
    )(place, *pieces)


def scale_kernel(value_ref, *refs):
    refs[-1][...] = (BRANCH * value_ref[...].astype(F32)).astype(BF16)


def scaled(value, *waits):
    whole = pl.BlockSpec(memory_space=pltpu.VMEM)
    return pl.pallas_call(
        scale_kernel,
        out_shape=jax.ShapeDtypeStruct(value.shape, BF16),
        in_specs=[whole] + [pl.BlockSpec(memory_space=pl.ANY)] * len(waits),
        out_specs=whole,
        compiler_params=params(),
        cost_estimate=cost(3),
        name="scaled",
    )(value, *waits)


def added(terms):
    one, two = terms
    value = one[...].astype(F32)
    return value if two is None else value + two[...].astype(F32)


def grouped(parts, refs):
    refs = list(refs)
    out = [tuple(None if a is None else refs.pop(0) for a in pair) for pair in parts]
    return out, refs


def unmix_kernel(parts, block, count, *refs):
    terms, outs = grouped(parts, refs)
    outs = outs[-count:]
    width = outs[0].shape[1]
    half = outs[0].shape[0] // len(parts)
    for index, pair in enumerate(terms):
        value = added(pair)
        for first in range(0, width, block):
            size = min(block, width - first)
            for turn, out_ref in enumerate(outs):
                spot = first * len(outs) + turn * block
                out_ref[index * half : (index + 1) * half, first : first + size] = value[
                    :, spot : spot + size
                ]


def unmix(parts, count, block, width, waits=()):
    rows = len(parts) * parts[0][0].shape[0]
    arrays = [a for pair in parts for a in pair if a is not None]
    return pl.pallas_call(
        functools.partial(unmix_kernel, parts_mask(parts), block, count),
        out_shape=tuple(jax.ShapeDtypeStruct((rows, width), F32) for _ in range(count)),
        in_specs=[pl.BlockSpec(memory_space=pltpu.VMEM)] * len(arrays) + after_all(waits),
        compiler_params=params(),
        cost_estimate=cost(3),
        name="unmix",
    )(*arrays, *waits)


def parts_mask(parts):
    return [tuple(None if a is None else True for a in pair) for pair in parts]


def body(
    tokens,
    attn_gain,
    mlp_gain,
    w_query,
    w_key,
    w_value,
    w_out,
    w_gate,
    w_up,
    w_down,
    prefix,
    out_grad,
):
    mp = lax.axis_size("mp")
    place = lax.axis_index("mp")
    rows = tokens.shape[0]
    width_heads = w_query.shape[1]
    heads = width_heads // HD
    padded_heads = round_up(width_heads, LANES)
    width_ff = w_gate.shape[1]
    padded_ff = round_up(width_ff, FF_BLOCK)
    own = place * rows

    def row_block(value, index):
        return lax.dynamic_slice_in_dim(value, index * rows, rows, 0)

    tables = angle_tables()
    core = lax.axis_index("dp") % 2
    at = [jnp.stack([(place + mp - k) % mp, core]) for k in range(mp)]

    attn_pack = pack([w_query, w_key, w_value], LANES, padded_heads)
    attn_weights = dp_gather(attn_pack)
    ff_pack = pack([w_gate, w_up], FF_BLOCK, padded_ff, attn_pack)
    gate_up = dp_gather(ff_pack)
    token_pieces = ring_gather(tokens)
    qkv = None
    for k in range(mp - 1):
        qkv, mark = project(
            at[k], token_pieces[k], attn_gain[None], attn_weights, tables, qkv
        )
    out_own = gate(
        pack([w_out.T], LANES, padded_heads, ff_pack), token_pieces[-1], mark
    )
    out_pieces = [out_own] + [shift_back(out_own, mp - j) for j in range(1, mp)]
    qkv, _ = project(
        at[mp - 1], token_pieces[-1], attn_gain[None], attn_weights, tables, qkv
    )
    attended, attended_send, log_total = attend(qkv, prefix, heads)
    out_pack = chain(out_pieces, attended)
    attended_pieces = [attended, ring_up(gate(attended_send, out_pack))]
    out_weights = dp_gather(gate(out_pack, attended_pieces[1], gate_up))
    normed_one, whole_tokens = lay_tokens(
        at[0], token_pieces, attn_gain[None], (attended_pieces[1],)
    )
    down_pack = pack([w_down.T], LANES, padded_ff, whole_tokens)
    down = dp_gather(down_pack)
    while len(attended_pieces) < mp:
        attended_pieces.append(ring_up(attended_pieces[-1]))

    grad_pieces = [scaled(out_grad, attended_pieces[-1], down_pack, out_weights)]
    grad_pieces.append(ring_up(grad_pieces[0]))
    normed_two, split_two, middle = finish_middle(
        at[0], attended_pieces, out_weights, whole_tokens, mlp_gain[None], rows
    )
    grad_pieces.append(ring_up(gate(grad_pieces[1], normed_two)))
    hidden, slopes = feed(normed_two, gate_up)
    while len(grad_pieces) < mp:
        grad_pieces.append(ring_up(grad_pieces[-1]))
    by_chip = paired()

    def back_of(k, held, kind=BF16, waits=()):
        *held, term = feed_back(
            at[k % mp], grad_pieces[k % mp], slopes, down, gate_up, held, kind, waits
        )
        return held, term

    width = normed_two.shape[1]
    grad_pieces.append(ring_up(grad_pieces[-1]))
    held, total = back_of(1, None, waits=(grad_pieces[2],))
    arrived = ring_up(total)
    held, term = back_of(2, held, waits=(grad_pieces[3],))
    held, term_three = back_of(3, held)
    total = join(term, arrived, (term_three,))
    arrived = ring_up(total)
    attended_own = own_rows(at[0], attended_pieces, rows)
    (grad_both, grad_mlp), term_own = back_of(mp, held, F32, (total, attended_own))
    if by_chip:
        down_other = scatter_other(grad_mlp, hidden, 768, 6)
        total = join(term_three, arrived, (down_other,))
        arrived = ring_up(total)
        ff_other = scatter_other(split_two, grad_both, 1024, 11, (total,))
        down_chip = scatter_mine(
            grad_mlp, hidden, 768, 6, swap(gate(down_other, total), 1), (ff_other,)
        )
        waits = (down_chip, ff_other)
    else:
        total = join(term_three, arrived)
        arrived = ring_up(total)
        waits = ()
    grad_middle, grad_attn, split_attn, gain_two, zero = own_back(
        core[None], term_own, arrived, middle, out_grad, mlp_gain[None], waits
    )
    *mine, zero = spread(grad_attn, out_weights, mp)
    def mlp_chunk(k, zero):
        return lax.optimization_barrier(
            outer_cols(row_block(hidden, at[k % mp][0] + zero[0]), down)
        )

    arrived = [mine[0]] + [shift_back(mine[k], k) for k in range(1, mp)]
    chunk_one = mlp_chunk(1, zero).astype(BF16)
    if by_chip:
        ff_chip = scatter_mine(
            split_two, grad_both, 1024, 11, swap(gate(ff_other, split_attn), 1), (chunk_one,)
        )
        ff_share = scatter_around(ff_chip)
        down_share = scatter_around(gate(down_chip, zero))
        waits = (ff_chip,)
    else:
        ff_share = scatter_plain(split_two, grad_both)
        down_share = scatter_plain(grad_mlp, hidden)
        waits = ()
    out_other = scatter_other(split_attn, attended_own, 1280, 5, (chunk_one,))
    mlp_arrived = ring_up(gate(chunk_one, *arrived[1:]))
    out_arrived = swap(out_other, 1) if by_chip else None
    spots = jnp.stack([prefix[0], place])
    back = attend_back(
        qkv, attended, arrived, log_total, tables, spots, heads,
        (*waits, out_other) if by_chip else (),
    )

    def grad_one_term(k, zero=0):
        return lax.optimization_barrier(
            outer_cols(row_block(back, at[k % mp][0] + zero), attn_weights)
        )

    total = grad_one_term(1).astype(BF16)
    arrived = ring_up(total)
    index = lax.axis_index("dp")
    chip = jnp.stack([index // 2 % 2, index // 4])
    if by_chip:
        attn_other = scatter_other(normed_one, back, 640, 8, (total, mlp_arrived))
        attn_arrived = swap(attn_other, 1)
        out_parts, zero = scatter_chip(
            chip, split_attn, attended_own, 1280, 8, out_arrived, (total, attn_other)
        )
        out_moved = scatter_first(out_parts)
        chunk = mlp_chunk(2, zero)
        total, zero = join_marked(
            grad_one_term(2, zero[0]), arrived,
            (attn_other, out_parts[1], out_parts[3], chunk),
        )
        arrived = ring_up(total)
        mlp_total = join(chunk, mlp_arrived, (total,))
        mlp_arrived = ring_up(mlp_total)
        attn_parts, zero = scatter_chip(
            chip, normed_one, back, 640, 10, attn_arrived, (total, mlp_total)
        )
        attn_moved = scatter_first(attn_parts)
        term = grad_one_term(3, zero[0])
        chunk = mlp_chunk(3, zero)
        total, zero = join_marked(term, arrived, (attn_parts[1], attn_parts[3], chunk))
        arrived = ring_up(total)
        term = grad_one_term(4, zero[0])
        out_half = scatter_halves(chip, out_parts, out_moved, (total,))
        out_share = scatter_second(out_half)
        mlp_total = join(chunk, mlp_arrived, (total, out_half[0][1], out_half[1][1]))
        mlp_arrived = ring_up(mlp_total)
        attn_half = scatter_halves(chip, attn_parts, attn_moved, (mlp_total,))
        attn_share = scatter_second(attn_half)
        waits = (attn_half[0][1], attn_half[1][1])
    else:
        out_share = scatter_plain(split_attn, attended_own)
        attn_share = scatter_plain(normed_one, back)
        total = join(grad_one_term(2), arrived)
        arrived = ring_up(total)
        mlp_arrived = ring_up(join(mlp_chunk(2, zero), mlp_arrived))
        total = join(grad_one_term(3), arrived)
        arrived = ring_up(total)
        mlp_arrived = ring_up(join(mlp_chunk(3, zero), mlp_arrived))
        term = grad_one_term(4)
        waits = ()
    out_total, *out_mine = out_sum(out_share, mp, padded_heads)
    input_grad, gain_one, zero = finish_input(
        term, arrived, tokens, grad_middle, attn_gain[None],
        (*waits, mlp_arrived, *out_mine),
    )
    out_moved = [shift_back(out_mine[k - 1], k) for k in range(1, mp)]
    gains = sum_over(jnp.concatenate([gain_one, gain_two]), "dp")
    chunk = mlp_chunk(4, zero)
    grad_w_query, grad_w_key, grad_w_value = unmix(attn_share, 3, LANES, width_heads)
    grad_w_gate, grad_w_up = unmix(ff_share, 2, FF_BLOCK, width_ff)
    (grad_w_down,) = unmix(down_share, 1, LANES, width_ff)
    block_out = finish_block(middle, chunk, mlp_arrived)
    gains = sum_over(
        gate(gains, *out_moved, grad_w_query, grad_w_gate, grad_w_down, block_out), "mp"
    )
    grad_w_out = out_final(out_total, out_moved, width_heads, (block_out,))
    return (
        block_out,
        input_grad,
        grad_w_query,
        grad_w_key,
        grad_w_value,
        grad_w_out.T,
        grad_w_gate,
        grad_w_up,
        grad_w_down.T,
        gains[0],
        gains[1],
    )


def solution(mesh):
    return jax.shard_map(
        body,
        mesh=mesh,
        in_specs=(
            P(("dp", "mp"), None),
            P(),
            P(),
            P("dp", "mp"),
            P("dp", "mp"),
            P("dp", "mp"),
            P("mp", "dp"),
            P("dp", "mp"),
            P("dp", "mp"),
            P("mp", "dp"),
            P("dp"),
            P(("dp", "mp"), None),
        ),
        out_specs=(
            P(("dp", "mp"), None),
            P(("dp", "mp"), None),
            P("dp", "mp"),
            P("dp", "mp"),
            P("dp", "mp"),
            P("mp", "dp"),
            P("dp", "mp"),
            P("dp", "mp"),
            P("mp", "dp"),
            P(),
            P(),
        ),
        check_vma=False,
    )
```

```python
import functools

import jax
import jax.numpy as jnp
import numpy as np
from jax import lax
from jax.experimental import pallas as pl
from jax.experimental.pallas import tpu as pltpu
from jax.sharding import PartitionSpec as P

HD = 64
LEN = 1024
LANES = 128
EPSILON = 1e-05
BRANCH = 1.4 / 40**0.5
MASKED = -1e30
FF_BLOCK = 512
VMEM_LIMIT = 56 * 1024 * 1024

F32 = jnp.float32
BF16 = jnp.bfloat16


def round_up(value, unit):
    return -(-value // unit) * unit


def matmul(left, right):
    return jnp.dot(left, right, preferred_element_type=F32)


def inner_rows(left, right):
    return lax.dot_general(
        left, right, (((0,), (0,)), ((), ())), preferred_element_type=F32
    )


def outer_cols(left, right):
    return lax.dot_general(
        left, right, (((1,), (1,)), ((), ())), preferred_element_type=F32
    )


def cost(micros):
    return pl.CostEstimate(
        flops=int(micros * 3.0e9), bytes_accessed=0, transcendentals=0
    )


def params(limit=VMEM_LIMIT):
    return pltpu.CompilerParams(vmem_limit_bytes=limit)


def ring_up(value):
    n = lax.axis_size("mp")
    return lax.ppermute(value, "mp", [(i, (i + 1) % n) for i in range(n)])


def ring_gather(value):
    pieces = [value]
    for _ in range(lax.axis_size("mp") - 1):
        pieces.append(ring_up(pieces[-1]))
    return pieces


def ring_scatter(part):
    n = lax.axis_size("mp")
    place = lax.axis_index("mp")
    total = part((place + n - 1) % n)
    for step in range(1, n):
        sent = total.astype(BF16)
        arrived = ring_up(sent)
        term = lax.optimization_barrier(part((place + 2 * n - 1 - step) % n))
        total = term + arrived.astype(F32)
    return total


def shift_back(value, count):
    n = lax.axis_size("mp")
    return lax.ppermute(value, "mp", [(i, (i - count) % n) for i in range(n)])


def sum_over(value, axis):
    n = lax.axis_size(axis)
    bit = 1
    while bit < n:
        value = value + lax.ppermute(value, axis, [(i, i ^ bit) for i in range(n)])
        bit *= 2
    return value


def swap(value, bit):
    n = lax.axis_size("dp")
    return lax.ppermute(value, "dp", [(i, i ^ bit) for i in range(n)])


def dp_gather(value):
    return lax.all_gather(value, "dp", axis=0, tiled=True)


def paired():
    return lax.axis_size("dp") == 8


def split_columns(value):
    if not paired():
        return value[None]
    core = lax.axis_index("dp") % 2
    rows, width = value.shape
    shaped = value.reshape(rows, 4, 2, width // 8)

    def pick(which):
        return lax.dynamic_index_in_dim(shaped, which, 2, False).reshape(rows, width // 2)

    return jnp.stack([pick(core), pick(1 - core)])


def after_all(waits):
    return [pl.BlockSpec(memory_space=pl.ANY)] * len(waits)


def weight_kernel(joined, left_ref, right_ref, *refs):
    value = inner_rows(left_ref[...], right_ref[...])
    if joined:
        value = value + refs[0][...].astype(F32)
    refs[-1][...] = value.astype(BF16)


def weight_grad(left, right, side, height, width, micros, arrived=None, waits=()):
    depth, columns = left.shape[-2:]
    others = right.shape[1]
    specs = [
        pl.BlockSpec((None, depth, height), lambda i, j: (side, 0, i))
        if left.ndim == 3
        else pl.BlockSpec((depth, height), lambda i, j: (0, i)),
        pl.BlockSpec((depth, width), lambda i, j: (0, j)),
    ]
    args = [left, right]
    if arrived is not None:
        specs.append(pl.BlockSpec((height, width), lambda i, j: (i, j)))
        args.append(arrived)
    return pl.pallas_call(
        functools.partial(weight_kernel, arrived is not None),
        out_shape=jax.ShapeDtypeStruct((columns, others), BF16),
        grid=(columns // height, others // width),
        in_specs=specs + after_all(waits),
        out_specs=pl.BlockSpec((height, width), lambda i, j: (i, j)),
        compiler_params=params(),
        cost_estimate=cost(micros),
        name="weight_grad",
    )(*args, *waits)


def scatter_other(left, right, width, micros, waits=()):
    if not paired():
        return None
    return weight_grad(left, right, 1, left.shape[2], width, micros, waits=waits)


def chip_kernel(where_ref, left_ref, right_ref, arrived_ref, *refs):
    one_kept, one_sent, two_kept, two_sent, zero_ref, total = refs[-6:]
    zero_ref[0] = 0
    value = inner_rows(left_ref[...], right_ref[...]) + arrived_ref[...].astype(F32)
    total[...] = value.astype(BF16)
    x, y = where_ref[0], where_ref[1]
    rows = total.shape[0] // 4
    half = rows // 2
    for k in (0, 1):
        for one_ref, two_ref, near_x, near_y in (
            (one_kept, two_kept, x, y),
            (one_sent, two_sent, 1 - x, 1 - y),
        ):
            start = pl.multiple_of((2 * near_y + k) * rows, 16)
            one_ref[k] = total[pl.ds(start, half), :]
            start = pl.multiple_of((2 * k + near_x) * rows + half, 16)
            two_ref[k] = total[pl.ds(start, half), :]


def scatter_chip(where, left, right, width, micros, arrived, waits=()):
    depth, columns = left.shape[1:]
    others = right.shape[1]
    half = columns // 8
    out = jax.ShapeDtypeStruct((2, half, others), BF16)
    block = pl.BlockSpec((2, half, width), lambda j, w: (0, 0, j))
    *parts, zero = pl.pallas_call(
        chip_kernel,
        out_shape=(out, out, out, out, jax.ShapeDtypeStruct((1,), jnp.int32)),
        grid_spec=pltpu.PrefetchScalarGridSpec(
            num_scalar_prefetch=1,
            grid=(others // width,),
            in_specs=[
                pl.BlockSpec((None, depth, columns), lambda j, w: (0, 0, 0)),
                pl.BlockSpec((depth, width), lambda j, w: (0, j)),
                pl.BlockSpec((columns, width), lambda j, w: (0, j)),
            ]
            + after_all(waits),
            out_specs=(block, block, block, block, pl.BlockSpec(memory_space=pltpu.SMEM)),
            scratch_shapes=[pltpu.VMEM((columns, width), BF16)],
        ),
        compiler_params=params(),
        cost_estimate=cost(micros),
        name="scatter_chip",
    )(where, left, right, arrived, *waits)
    return parts, zero


def scatter_first(parts):
    return swap(parts[1], 4), swap(parts[3], 2)


def halves_kernel(where_ref, kept_ref, moved_ref, *refs):
    keep_ref, send_ref, total = refs[-3:]
    total[...] = (kept_ref[...].astype(F32) + moved_ref[...].astype(F32)).astype(BF16)
    keep_ref[...] = total[where_ref[0]]
    send_ref[...] = total[1 - where_ref[0]]


def halves(where, kept, moved, waits):
    whole = pl.BlockSpec(memory_space=pltpu.VMEM)
    out = jax.ShapeDtypeStruct(kept.shape[1:], BF16)
    return pl.pallas_call(
        halves_kernel,
        out_shape=(out, out),
        in_specs=[pl.BlockSpec(memory_space=pltpu.SMEM), whole, whole] + after_all(waits),
        out_specs=(whole, whole),
        scratch_shapes=[pltpu.VMEM(kept.shape, BF16)],
        compiler_params=params(),
        cost_estimate=cost(3),
        name="halves",
    )(where, kept, moved, *waits)


def scatter_halves(where, parts, moved, waits=()):
    return (
        halves(where[0:1], parts[0], moved[0], waits),
        halves(where[1:2], parts[2], moved[1], waits),
    )


def scatter_second(both):
    (one, one_sent), (two, two_sent) = both
    return [(one, swap(one_sent, 2)), (two, swap(two_sent, 4))]


def scatter_plain(left, right):
    return scatter_whole(inner_rows(left[0], right).astype(BF16))


def pass_kernel(*refs):
    pass


def gate(value, *waits):
    return pl.pallas_call(
        pass_kernel,
        out_shape=jax.ShapeDtypeStruct(value.shape, value.dtype),
        in_specs=after_all((value, *waits)),
        out_specs=pl.BlockSpec(memory_space=pl.ANY),
        input_output_aliases={0: 0},
        cost_estimate=cost(1),
        name="gate",
    )(value, *waits)


def join_kernel(one_ref, two_ref, *refs):
    out_ref, zero_ref = refs[-2:]
    out_ref[...] = (one_ref[...].astype(F32) + two_ref[...].astype(F32)).astype(BF16)
    zero_ref[0] = 0


def join_marked(one, two, waits=()):
    whole = pl.BlockSpec(memory_space=pltpu.VMEM)
    return pl.pallas_call(
        join_kernel,
        out_shape=(
            jax.ShapeDtypeStruct(one.shape, BF16),
            jax.ShapeDtypeStruct((1,), jnp.int32),
        ),
        in_specs=[whole, whole] + after_all(waits),
        out_specs=(whole, pl.BlockSpec(memory_space=pltpu.SMEM)),
        compiler_params=params(),
        cost_estimate=cost(3),
        name="join",
    )(one, two, *waits)


def join(one, two, waits=()):
    return join_marked(one, two, waits)[0]


def scatter_mine(left, right, width, micros, arrived, waits=()):
    return weight_grad(left, right, 0, left.shape[2], width, micros, arrived, waits)


def scatter_around(chip):
    share = lax.psum_scatter(
        chip,
        "dp",
        scatter_dimension=0,
        tiled=True,
        axis_index_groups=[[2 * k + core for k in AROUND] for core in (0, 1)],
    )
    return [(share, None)]


def scatter_whole(partial):
    share = lax.psum_scatter(partial, "dp", scatter_dimension=0, tiled=True)
    return [(share, None)]


def angle_tables():
    half = HD // 2
    rates = 10000.0 ** (-np.arange(half) * 2.0 / HD)
    angles = np.arange(LEN)[:, None] * rates[None, :]
    cosine, sine = np.cos(angles), np.sin(angles)
    return (
        jnp.asarray(np.concatenate([cosine] * 4, axis=-1), F32),
        jnp.asarray(np.concatenate([-sine, sine] * 2, axis=-1), F32),
    )


def swap_halves(value):
    lane = lax.broadcasted_iota(jnp.int32, value.shape, 1)
    low = (lane % HD) < HD // 2
    return jnp.where(
        low, pltpu.roll(value, LANES - HD // 2, 1), pltpu.roll(value, HD // 2, 1)
    )


AROUND = (0, 1, 3, 2)


def put_split(ref, value, core, chips=(0, 1, 2, 3), rows=slice(None)):
    if ref.shape[0] == 1:
        ref[0, rows, :] = value
        return
    block = value.shape[1] // 8
    for which in (0, 1):

        @pl.when(core == which)
        def _():
            for side in (0, 1):
                for spot, chip in enumerate(chips):
                    start = (2 * chip + (which ^ side)) * block
                    ref[side, rows, spot * block : (spot + 1) * block] = value[
                        :, start : start + block
                    ]


def split_shape(rows, width):
    return (2, rows, width // 2) if paired() else (1, rows, width)


def normed_of(value, gain):
    value = value.astype(F32)
    factor = lax.rsqrt(jnp.mean(value * value, axis=-1, keepdims=True) + EPSILON)
    return (value * factor * gain).astype(BF16)


def project_kernel(where_ref, x_ref, gain_ref, w_ref, cos_ref, sin_ref, *refs):
    qkv_ref, mark_ref, held = refs[-3:]

    @pl.when(pl.program_id(0) == 0)
    def _():
        mark_ref[...] = jnp.zeros_like(mark_ref)
        held[...] = normed_of(x_ref[...], gain_ref[...])

    product = matmul(held[...], w_ref[...])
    cosine, sine = cos_ref[...], sin_ref[...]
    query = product[:, :LANES]
    key = product[:, LANES : 2 * LANES]
    query = (query * cosine + swap_halves(query) * sine).astype(BF16)
    qkv_ref[:, :LANES] = query * HD**-0.5
    qkv_ref[:, LANES : 2 * LANES] = (key * cosine + swap_halves(key) * sine).astype(BF16)
    qkv_ref[:, 2 * LANES :] = product[:, 2 * LANES :].astype(BF16)


def project(where, piece, gain, weights, tables, held):
    rows, width = piece.shape
    columns = weights.shape[1]
    block = 3 * LANES
    specs = [
        pl.BlockSpec((rows, width), lambda i, w: (0, 0)),
        pl.BlockSpec((1, width), lambda i, w: (0, 0)),
        pl.BlockSpec((width, block), lambda i, w: (0, i)),
        pl.BlockSpec((rows, LANES), lambda i, w: (w[0], 0)),
        pl.BlockSpec((rows, LANES), lambda i, w: (w[0], 0)),
    ]
    args = [piece, gain, weights, *tables]
    aliases = {}
    if held is not None:
        aliases[1 + len(args)] = 0
        args.append(held)
        specs.append(pl.BlockSpec(memory_space=pl.ANY))
    return pl.pallas_call(
        project_kernel,
        out_shape=(
            jax.ShapeDtypeStruct((LEN, columns), BF16),
            jax.ShapeDtypeStruct((8, LANES), F32),
        ),
        grid_spec=pltpu.PrefetchScalarGridSpec(
            num_scalar_prefetch=1,
            grid=(columns // block,),
            in_specs=specs,
            out_specs=(
                pl.BlockSpec((rows, block), lambda i, w: (w[0], i)),
                pl.BlockSpec((8, LANES), lambda i, w: (0, 0)),
            ),
            scratch_shapes=[pltpu.VMEM((rows, width), BF16)],
        ),
        input_output_aliases=aliases,
        compiler_params=params(),
        cost_estimate=cost(9),
        name="project",
    )(where, *args)


def lay_tokens_kernel(count, place_ref, gain_ref, *refs):
    norm_ref, copy_ref = refs[-2:]
    rows = refs[0].shape[0]
    for k in range(count):
        start = pl.multiple_of(lax.rem(place_ref[0] + count - k, count) * rows, rows)
        here = pl.ds(start, rows)
        copy_ref[here, :] = refs[k][...]
        put_split(norm_ref, normed_of(refs[k][...], gain_ref[...]), place_ref[1], rows=here)


def lay_tokens(place, pieces, gain, waits):
    rows, width = pieces[0].shape
    count = len(pieces)
    whole = pl.BlockSpec(memory_space=pltpu.VMEM)
    return pl.pallas_call(
        functools.partial(lay_tokens_kernel, count),
        out_shape=(
            jax.ShapeDtypeStruct(split_shape(count * rows, width), BF16),
            jax.ShapeDtypeStruct((count * rows, width), BF16),
        ),
        in_specs=[pl.BlockSpec(memory_space=pltpu.SMEM)] + [whole] * (1 + count)
        + after_all(waits),
        out_specs=(whole, whole),
        compiler_params=params(),
        cost_estimate=cost(10),
        name="lay_tokens",
    )(place, gain, *pieces, *waits)


PARTS = (
    (0, 512, ((0, 512, True),)),
    (512, 256, ((0, 512, False), (512, 256, True))),
    (768, 256, ((0, 768, False), (768, 256, True))),
)


def visible(shape, first_key, first_query, limit):
    key = first_key + lax.broadcasted_iota(jnp.int32, shape, 0)
    query = first_query + lax.broadcasted_iota(jnp.int32, shape, 1)
    return (key < limit) | (key <= query)


def head_only(value, head):
    lane = lax.broadcasted_iota(jnp.int32, value.shape, 1)
    return jnp.where((lane >= HD) == (head == 1), value, jnp.zeros_like(value))


def attend_kernel(heads, prefix_ref, qkv_ref, out_ref, send_ref, log_ref, turned):
    limit = prefix_ref[0]
    pair = pl.program_id(0)
    values_across = qkv_ref[:, 2 * LANES :].T
    for head in (0, 1):

        @pl.when(2 * pair + head < heads)
        def _():
            queries = head_only(qkv_ref[:, :LANES], head)
            for first, count, spans in PARTS:
                mine = queries[first : first + count]
                scores = []
                for start, keys, masked in spans:
                    raw = outer_cols(qkv_ref[start : start + keys, LANES : 2 * LANES], mine)
                    if masked:
                        raw = jnp.where(visible(raw.shape, start, first, limit), raw, MASKED)
                    scores.append(raw)
                top = functools.reduce(
                    jnp.maximum, [jnp.max(s, axis=0, keepdims=True) for s in scores]
                )
                total = jnp.zeros_like(top)
                summed = jnp.zeros((HD, count), F32)
                for (start, keys, _), raw in zip(spans, scores):
                    weight = jnp.exp(raw - top)
                    total = total + jnp.sum(weight, axis=0, keepdims=True)
                    summed = summed + matmul(
                        values_across[head * HD : (head + 1) * HD, start : start + keys],
                        weight.astype(BF16),
                    )
                turned[head * HD : (head + 1) * HD, first : first + count] = summed / total
                log_ref[0, head : head + 1, first : first + count] = top + jnp.log(total)

        @pl.when(2 * pair + head >= heads)
        def _():
            turned[head * HD : (head + 1) * HD, :] = jnp.zeros((HD, LEN), F32)
            log_ref[0, head : head + 1, :] = jnp.zeros((1, LEN), F32)

    value = turned[...].T.astype(BF16)
    out_ref[...] = value
    send_ref[...] = value


def attend(qkv, prefix, heads):
    pairs = qkv.shape[1] // (3 * LANES)
    return pl.pallas_call(
        functools.partial(attend_kernel, heads),
        out_shape=(
            jax.ShapeDtypeStruct((LEN, pairs * LANES), BF16),
            jax.ShapeDtypeStruct((LEN, pairs * LANES), BF16),
            jax.ShapeDtypeStruct((pairs, 2, LEN), F32),
        ),
        grid_spec=pltpu.PrefetchScalarGridSpec(
            num_scalar_prefetch=1,
            grid=(pairs,),
            in_specs=[pl.BlockSpec((LEN, 3 * LANES), lambda i, s: (0, i))],
            out_specs=(
                pl.BlockSpec((LEN, LANES), lambda i, s: (0, i)),
                pl.BlockSpec((LEN, LANES), lambda i, s: (0, i)),
                pl.BlockSpec((1, 2, LEN), lambda i, s: (i, 0, 0)),
            ),
            scratch_shapes=[pltpu.VMEM((LANES, LEN), F32)],
        ),
        compiler_params=params(),
        cost_estimate=cost(18),
        name="attend",
    )(prefix, qkv)


def attend_back_kernel(
    heads, count, prefix_ref, qkv_ref, out_ref, *refs
):
    arrived = refs[:count]
    log_ref, cos_ref, sin_ref = refs[count : count + 3]
    back_ref, turned, grad_key, grad_value, grad_ref = refs[-5:]
    limit = prefix_ref[0]
    rows = arrived[0].shape[0]
    for k in range(count):
        start = pl.multiple_of(lax.rem(prefix_ref[1] + k, count) * rows, rows)
        grad_ref[pl.ds(start, rows), :] = arrived[k][...]
    pair = pl.program_id(0)
    keys_across = qkv_ref[:, LANES : 2 * LANES].T
    inner = (out_ref[...].astype(F32) * grad_ref[...].astype(F32)).T
    grad_key[...] = jnp.zeros_like(grad_key)
    grad_value[...] = jnp.zeros_like(grad_value)
    for head in (0, 1):
        band = slice(head * HD, (head + 1) * HD)

        @pl.when(2 * pair + head < heads)
        def _():
            queries = head_only(qkv_ref[:, :LANES], head)
            grads = head_only(grad_ref[...], head)
            inner_row = jnp.sum(inner[band], axis=0, keepdims=True)
            for first, count, spans in PARTS:
                here = slice(first, first + count)
                mine, grad_mine = queries[here], grads[here]
                log_mine = log_ref[0, head : head + 1, here]
                inner_mine = inner_row[:, here]
                summed = jnp.zeros((HD, count), F32)
                for start, keys, masked in spans:
                    there = slice(start, start + keys)
                    raw = outer_cols(qkv_ref[there, LANES : 2 * LANES], mine)
                    chance = jnp.exp(raw - log_mine)
                    if masked:
                        chance = jnp.where(
                            visible(raw.shape, start, first, limit), chance, 0.0
                        )
                    grad_chance = outer_cols(qkv_ref[there, 2 * LANES :], grad_mine)
                    grad_score = (chance * (grad_chance - inner_mine)).astype(BF16)
                    grad_key[there, :] += matmul(grad_score, mine)
                    grad_value[there, :] += matmul(chance.astype(BF16), grad_mine)
                    summed = summed + matmul(keys_across[band, there], grad_score)
                turned[band, here] = summed

        @pl.when(2 * pair + head >= heads)
        def _():
            turned[band, :] = jnp.zeros((HD, LEN), F32)

    cosine, sine = cos_ref[...], sin_ref[...]
    grad_query = turned[...].T * HD**-0.5
    back_ref[:, :LANES] = (grad_query * cosine - swap_halves(grad_query) * sine).astype(BF16)
    back = grad_key[...]
    back_ref[:, LANES : 2 * LANES] = (back * cosine - swap_halves(back) * sine).astype(BF16)
    back_ref[:, 2 * LANES :] = grad_value[...].astype(BF16)


def attend_back(qkv, attended, arrived, log_total, tables, prefix, heads, waits=()):
    pairs = qkv.shape[1] // (3 * LANES)
    count, rows = len(arrived), arrived[0].shape[0]
    return pl.pallas_call(
        functools.partial(attend_back_kernel, heads, count),
        out_shape=jax.ShapeDtypeStruct(qkv.shape, BF16),
        grid_spec=pltpu.PrefetchScalarGridSpec(
            num_scalar_prefetch=1,
            grid=(pairs,),
            in_specs=[
                pl.BlockSpec((LEN, 3 * LANES), lambda i, s: (0, i)),
                pl.BlockSpec((LEN, LANES), lambda i, s: (0, i)),
            ]
            + [pl.BlockSpec((rows, LANES), lambda i, s: (0, i))] * count
            + [
                pl.BlockSpec((1, 2, LEN), lambda i, s: (i, 0, 0)),
                pl.BlockSpec((LEN, LANES), lambda i, s: (0, 0)),
                pl.BlockSpec((LEN, LANES), lambda i, s: (0, 0)),
            ]
            + after_all(waits),
            out_specs=pl.BlockSpec((LEN, 3 * LANES), lambda i, s: (0, i)),
            scratch_shapes=[
                pltpu.VMEM((LANES, LEN), F32),
                pltpu.VMEM((LEN, LANES), F32),
                pltpu.VMEM((LEN, LANES), F32),
                pltpu.VMEM((LEN, LANES), BF16),
            ],
        ),
        compiler_params=params(),
        cost_estimate=cost(28),
        name="attend_back",
    )(prefix, qkv, attended, *arrived, log_total, *tables, *waits)


def middle_kernel(count, place_ref, *refs):
    pieces = refs[:count]
    w_ref, x_ref, gain_ref, normed_ref, split_ref, own_ref = refs[count:]
    depth = pieces[0].shape[1]
    total = None
    for k in range(count):
        term = outer_cols(pieces[k][...], w_ref[:, k * depth : (k + 1) * depth])
        total = term if total is None else total + term
    middle = x_ref[...].astype(F32) + BRANCH * total
    factor = lax.rsqrt(jnp.mean(middle * middle, axis=-1, keepdims=True) + EPSILON)
    normed = (middle * factor * gain_ref[...]).astype(BF16)
    normed_ref[...] = normed
    put_split(split_ref, normed, place_ref[1], AROUND)
    rows, own = x_ref.shape[0], own_ref.shape[0]
    for part in range(rows // own):

        @pl.when(pl.program_id(0) * (rows // own) + part == place_ref[0])
        def _():
            own_ref[...] = middle[part * own : (part + 1) * own]


def finish_middle(place, pieces, weights, tokens, gain, own):
    width = tokens.shape[1]
    depth = pieces[0].shape[1]
    count = len(pieces)
    rows = 2 * own
    return pl.pallas_call(
        functools.partial(middle_kernel, count),
        out_shape=(
            jax.ShapeDtypeStruct((LEN, width), BF16),
            jax.ShapeDtypeStruct(split_shape(LEN, width), BF16),
            jax.ShapeDtypeStruct((own, width), F32),
        ),
        grid_spec=pltpu.PrefetchScalarGridSpec(
            num_scalar_prefetch=1,
            grid=(LEN // rows,),
            in_specs=[pl.BlockSpec((rows, depth), lambda i, s: (i, 0))] * count
            + [
                pl.BlockSpec((width, count * depth), lambda i, s: (0, 0)),
                pl.BlockSpec((rows, width), lambda i, s: (i, 0)),
                pl.BlockSpec((1, width), lambda i, s: (0, 0)),
            ],
            out_specs=(
                pl.BlockSpec((rows, width), lambda i, s: (i, 0)),
                pl.BlockSpec(split_shape(rows, width), lambda i, s: (0, i, 0)),
                pl.BlockSpec((own, width), lambda i, s: (0, 0)),
            ),
        ),
        compiler_params=params(),
        cost_estimate=cost(22),
        name="finish_middle",
    )(place, *pieces, weights, tokens, gain)


def gate_kernel(normed_ref, weight_ref, hidden_ref, slope_ref):
    rows = 256
    for start in range(0, LEN, rows):
        here = slice(start, start + rows)
        product = matmul(normed_ref[here], weight_ref[...])
        gate, up = product[:, :FF_BLOCK], product[:, FF_BLOCK:]
        sigmoid = jax.nn.sigmoid(gate)
        silu = gate * sigmoid
        hidden_ref[here, :] = (silu * up).astype(BF16)
        slope_ref[here, :FF_BLOCK] = (up * (sigmoid + silu * (1.0 - sigmoid))).astype(BF16)
        slope_ref[here, FF_BLOCK:] = silu.astype(BF16)


def feed(normed, gate_up):
    width = normed.shape[1]
    hidden = gate_up.shape[1] // 2
    return pl.pallas_call(
        gate_kernel,
        out_shape=(
            jax.ShapeDtypeStruct((LEN, hidden), BF16),
            jax.ShapeDtypeStruct((LEN, 2 * hidden), BF16),
        ),
        grid=(hidden // FF_BLOCK,),
        in_specs=[
            pl.BlockSpec((LEN, width), lambda i: (0, 0)),
            pl.BlockSpec((width, 2 * FF_BLOCK), lambda i: (0, i)),
        ],
        out_specs=(
            pl.BlockSpec((LEN, FF_BLOCK), lambda i: (0, i)),
            pl.BlockSpec((LEN, 2 * FF_BLOCK), lambda i: (0, i)),
        ),
        compiler_params=params(),
        cost_estimate=cost(21),
        name="feed",
    )(normed, gate_up)


def feed_back_kernel(where_ref, grad_ref, slope_ref, down_ref, weight_ref, *refs):
    both_ref, copy_ref, sum_ref, total = refs[-4:]
    step = pl.program_id(0)

    @pl.when(step == 0)
    def _():
        put_split(copy_ref, grad_ref[...], where_ref[1], AROUND)
        total[...] = jnp.zeros_like(total)

    grad = matmul(grad_ref[...], down_ref[...])
    grads = jnp.concatenate([grad, grad], axis=1)
    both = (grads * slope_ref[...].astype(F32)).astype(BF16)
    both_ref[...] = both
    total[...] += outer_cols(both, weight_ref[...])

    @pl.when(step == pl.num_programs(0) - 1)
    def _():
        sum_ref[...] = total[...].astype(sum_ref.dtype)


def feed_back(where, piece, slopes, down, gate_up, held, kind, waits=()):
    rows, width = piece.shape
    hidden = down.shape[1]
    specs = [
        pl.BlockSpec((rows, width), lambda i, w: (0, 0)),
        pl.BlockSpec((rows, 2 * FF_BLOCK), lambda i, w: (w[0], i)),
        pl.BlockSpec((width, FF_BLOCK), lambda i, w: (0, i)),
        pl.BlockSpec((width, 2 * FF_BLOCK), lambda i, w: (0, i)),
    ]
    args = [piece, slopes, down, gate_up]
    aliases = {}
    if held is not None:
        for index, array in enumerate(held):
            aliases[1 + len(args)] = index
            args.append(array)
            specs.append(pl.BlockSpec(memory_space=pl.ANY))
    args += waits
    specs += after_all(waits)
    return pl.pallas_call(
        feed_back_kernel,
        out_shape=(
            jax.ShapeDtypeStruct((LEN, 2 * hidden), BF16),
            jax.ShapeDtypeStruct(split_shape(LEN, width), BF16),
            jax.ShapeDtypeStruct((rows, width), kind),
        ),
        grid_spec=pltpu.PrefetchScalarGridSpec(
            num_scalar_prefetch=1,
            grid=(hidden // FF_BLOCK,),
            in_specs=specs,
            out_specs=(
                pl.BlockSpec((rows, 2 * FF_BLOCK), lambda i, w: (w[0], i)),
                pl.BlockSpec(split_shape(rows, width), lambda i, w: (0, w[0], 0)),
                pl.BlockSpec((rows, width), lambda i, w: (0, 0)),
            ),
            scratch_shapes=[pltpu.VMEM((rows, width), F32)],
        ),
        input_output_aliases=aliases,
        compiler_params=params(),
        cost_estimate=cost(15),
        name="feed_back",
    )(where, *args)


def out_sum_kernel(parts, count, width, *refs):
    terms, outs = grouped(parts, refs)
    outs = outs[-count:]
    half = outs[0].shape[0] // len(parts)
    for index, pair in enumerate(terms):
        value = added(pair)
        here = slice(index * half, (index + 1) * half)
        for k in range(count):
            outs[k][here, :] = value[:, k * width : (k + 1) * width].astype(outs[k].dtype)


def out_sum(parts, count, width, waits=()):
    rows = len(parts) * parts[0][0].shape[0]
    arrays = [a for pair in parts for a in pair if a is not None]
    return pl.pallas_call(
        functools.partial(out_sum_kernel, parts_mask(parts), count, width),
        out_shape=tuple(
            jax.ShapeDtypeStruct((rows, width), BF16 if k else F32) for k in range(count)
        ),
        in_specs=[pl.BlockSpec(memory_space=pltpu.VMEM)] * len(arrays) + after_all(waits),
        compiler_params=params(),
        cost_estimate=cost(3),
        name="out_sum",
    )(*arrays, *waits)


def out_final_kernel(count, *refs):
    total = refs[0][...]
    for ref in refs[1:count]:
        total = total + ref[...].astype(F32)
    refs[-1][...] = total[:, : refs[-1].shape[1]]


def out_final(own, moved, width, waits):
    whole = pl.BlockSpec(memory_space=pltpu.VMEM)
    count = 1 + len(moved)
    return pl.pallas_call(
        functools.partial(out_final_kernel, count),
        out_shape=jax.ShapeDtypeStruct((own.shape[0], width), F32),
        in_specs=[whole] * count + after_all(waits),
        out_specs=whole,
        compiler_params=params(),
        cost_estimate=cost(3),
        name="out_final",
    )(own, *moved, *waits)


def spread_kernel(count, value_ref, weight_ref, *refs):
    product = matmul(value_ref[...], weight_ref[...]).astype(BF16)
    refs[-1][0] = 0
    for k in range(count):

        @pl.when(pl.program_id(0) == k)
        def _():
            refs[k][...] = product


def spread(value, weights, count):
    rows, depth = value.shape
    width = weights.shape[1] // count
    return pl.pallas_call(
        functools.partial(spread_kernel, count),
        out_shape=tuple(jax.ShapeDtypeStruct((rows, width), BF16) for _ in range(count))
        + (jax.ShapeDtypeStruct((1,), jnp.int32),),
        grid=(count,),
        in_specs=[
            pl.BlockSpec((rows, depth), lambda i: (0, 0)),
            pl.BlockSpec((depth, width), lambda i: (0, i)),
        ],
        out_specs=tuple(pl.BlockSpec((rows, width), lambda i: (0, 0)) for _ in range(count))
        + (pl.BlockSpec(memory_space=pltpu.SMEM),),
        compiler_params=params(),
        cost_estimate=cost(8),
        name="spread",
    )(value, weights)


def norm_back(value, gain, incoming):
    factor = lax.rsqrt(jnp.mean(value * value, axis=-1, keepdims=True) + EPSILON)
    normed = value * factor
    scaled_in = incoming * gain
    inner = jnp.mean(scaled_in * normed, axis=-1, keepdims=True)
    return (
        factor * (scaled_in - normed * inner),
        jnp.sum(incoming * normed, axis=0, keepdims=True),
    )


def own_back_kernel(
    core_ref, term_ref, arrived_ref, middle_ref, grad_ref, gain_ref, *refs
):
    sum_ref, send_ref, split_ref, gain_sum_ref, zero_ref = refs[-5:]
    incoming = term_ref[...].astype(F32) + arrived_ref[...].astype(F32)
    back, gain_sum = norm_back(middle_ref[...], gain_ref[...], incoming)
    total = grad_ref[...].astype(F32) + back
    sum_ref[...] = total
    sent = (BRANCH * total).astype(BF16)
    send_ref[...] = sent
    put_split(split_ref, sent, core_ref[0])
    zero_ref[0] = 0

    @pl.when(pl.program_id(0) == 0)
    def _():
        gain_sum_ref[...] = jnp.zeros_like(gain_sum_ref)

    gain_sum_ref[...] += gain_sum


def own_back(core, term, arrived, middle, grad, gain, waits=()):
    rows, width = middle.shape
    step = rows // 2
    block = pl.BlockSpec((step, width), lambda i, s: (i, 0))
    line = pl.BlockSpec((1, width), lambda i, s: (0, 0))
    return pl.pallas_call(
        own_back_kernel,
        out_shape=(
            jax.ShapeDtypeStruct((rows, width), F32),
            jax.ShapeDtypeStruct((rows, width), BF16),
            jax.ShapeDtypeStruct(split_shape(rows, width), BF16),
            jax.ShapeDtypeStruct((1, width), F32),
            jax.ShapeDtypeStruct((1,), jnp.int32),
        ),
        grid_spec=pltpu.PrefetchScalarGridSpec(
            num_scalar_prefetch=1,
            grid=(2,),
            in_specs=[block, block, block, block, line] + after_all(waits),
            out_specs=(
                block,
                block,
                pl.BlockSpec(split_shape(step, width), lambda i, s: (0, i, 0)),
                line,
                pl.BlockSpec(memory_space=pltpu.SMEM),
            ),
        ),
        compiler_params=params(),
        cost_estimate=cost(5),
        name="own_back",
    )(core, term, arrived, middle, grad, gain, *waits)


def finish_input_kernel(term_ref, arrived_ref, x_ref, sum_ref, gain_ref, *refs):
    out_ref, gain_sum_ref, zero_ref = refs[-3:]
    incoming = term_ref[...] + arrived_ref[...].astype(F32)
    back, gain_sum = norm_back(x_ref[...].astype(F32), gain_ref[...], incoming)
    out_ref[...] = (sum_ref[...] + back).astype(BF16)
    zero_ref[0] = 0

    @pl.when(pl.program_id(0) == 0)
    def _():
        gain_sum_ref[...] = jnp.zeros_like(gain_sum_ref)

    gain_sum_ref[...] += gain_sum


def finish_input(term, arrived, x, total, gain, waits=()):
    rows, width = x.shape
    block = pl.BlockSpec((rows // 2, width), lambda i: (i, 0))
    line = pl.BlockSpec((1, width), lambda i: (0, 0))
    return pl.pallas_call(
        finish_input_kernel,
        out_shape=(
            jax.ShapeDtypeStruct((rows, width), BF16),
            jax.ShapeDtypeStruct((1, width), F32),
            jax.ShapeDtypeStruct((1,), jnp.int32),
        ),
        grid=(2,),
        in_specs=[block, block, block, block, line] + after_all(waits),
        out_specs=(block, line, pl.BlockSpec(memory_space=pltpu.SMEM)),
        compiler_params=params(),
        cost_estimate=cost(5),
        name="finish_input",
    )(term, arrived, x, total, gain, *waits)


def finish_block_kernel(middle_ref, term_ref, arrived_ref, *refs):
    total = term_ref[...] + arrived_ref[...].astype(F32)
    refs[-1][...] = (middle_ref[...] + BRANCH * total).astype(BF16)


def finish_block(middle, term, arrived, waits=()):
    rows, width = middle.shape
    block = pl.BlockSpec((rows // 2, width), lambda i: (i, 0))
    return pl.pallas_call(
        finish_block_kernel,
        out_shape=jax.ShapeDtypeStruct((rows, width), BF16),
        grid=(2,),
        in_specs=[block, block, block] + after_all(waits),
        out_specs=block,
        compiler_params=params(),
        cost_estimate=cost(3),
        name="finish_block",
    )(middle, term, arrived, *waits)


def mix(out_ref, refs, block):
    width = refs[0].shape[1]
    count = len(refs)
    for first in range(0, width, block):
        size = min(block, width - first)
        base = first * count
        for index, ref in enumerate(refs):
            spot = base + index * block
            out_ref[:, spot : spot + size] = ref[:, first : first + size]
            if size < block:
                out_ref[:, spot + size : spot + block] = jnp.zeros(
                    (ref.shape[0], block - size), out_ref.dtype
                )


def pack_kernel(count, block, *refs):
    mix(refs[-1], refs[:count], block)


def pack(values, block, width, *waits):
    count = len(values)
    rows = values[0].shape[0]
    whole = pl.BlockSpec(memory_space=pltpu.VMEM)
    return pl.pallas_call(
        functools.partial(pack_kernel, count, block),
        out_shape=jax.ShapeDtypeStruct((rows, count * width), BF16),
        in_specs=[whole] * count + after_all(waits),
        out_specs=whole,
        compiler_params=params(),
        cost_estimate=cost(3),
        name="pack",
    )(*values, *waits)


def chain_kernel(count, *refs):
    out_ref = refs[-1]
    width = refs[0].shape[1]
    for k in range(count):
        out_ref[:, k * width : (k + 1) * width] = refs[k][...]


def chain(values, *waits):
    rows, width = values[0].shape
    whole = pl.BlockSpec(memory_space=pltpu.VMEM)
    return pl.pallas_call(
        functools.partial(chain_kernel, len(values)),
        out_shape=jax.ShapeDtypeStruct((rows, len(values) * width), values[0].dtype),
        in_specs=[whole] * len(values) + after_all(waits),
        out_specs=whole,
        compiler_params=params(),
        cost_estimate=cost(2),
        name="chain",
    )(*values, *waits)


def own_rows_kernel(count, place_ref, *refs):
    width = refs[0].shape[1]
    for k in range(count):
        refs[-1][:, k * width : (k + 1) * width] = refs[k][...]


def own_rows(place, pieces, rows):
    width = pieces[0].shape[1]
    count = len(pieces)
    return pl.pallas_call(
        functools.partial(own_rows_kernel, count),
        out_shape=jax.ShapeDtypeStruct((rows, count * width), pieces[0].dtype),
        grid_spec=pltpu.PrefetchScalarGridSpec(
            num_scalar_prefetch=1,
            grid=(1,),
            in_specs=[pl.BlockSpec((rows, width), lambda i, s: (s[0], 0))] * count,
            out_specs=pl.BlockSpec((rows, count * width), lambda i, s: (0, 0)),
        ),
        compiler_params=params(),
        cost_estimate=cost(2),
        name="own_rows",
    )(place, *pieces)


def scale_kernel(value_ref, *refs):
    refs[-1][...] = (BRANCH * value_ref[...].astype(F32)).astype(BF16)


def scaled(value, *waits):
    whole = pl.BlockSpec(memory_space=pltpu.VMEM)
    return pl.pallas_call(
        scale_kernel,
        out_shape=jax.ShapeDtypeStruct(value.shape, BF16),
        in_specs=[whole] + [pl.BlockSpec(memory_space=pl.ANY)] * len(waits),
        out_specs=whole,
        compiler_params=params(),
        cost_estimate=cost(3),
        name="scaled",
    )(value, *waits)


def added(terms):
    one, two = terms
    value = one[...].astype(F32)
    return value if two is None else value + two[...].astype(F32)


def grouped(parts, refs):
    refs = list(refs)
    out = [tuple(None if a is None else refs.pop(0) for a in pair) for pair in parts]
    return out, refs


def unmix_kernel(parts, block, count, *refs):
    terms, outs = grouped(parts, refs)
    outs = outs[-count:]
    width = outs[0].shape[1]
    half = outs[0].shape[0] // len(parts)
    for index, pair in enumerate(terms):
        value = added(pair)
        for first in range(0, width, block):
            size = min(block, width - first)
            for turn, out_ref in enumerate(outs):
                spot = first * len(outs) + turn * block
                out_ref[index * half : (index + 1) * half, first : first + size] = value[
                    :, spot : spot + size
                ]


def unmix(parts, count, block, width, waits=()):
    rows = len(parts) * parts[0][0].shape[0]
    arrays = [a for pair in parts for a in pair if a is not None]
    return pl.pallas_call(
        functools.partial(unmix_kernel, parts_mask(parts), block, count),
        out_shape=tuple(jax.ShapeDtypeStruct((rows, width), F32) for _ in range(count)),
        in_specs=[pl.BlockSpec(memory_space=pltpu.VMEM)] * len(arrays) + after_all(waits),
        compiler_params=params(),
        cost_estimate=cost(3),
        name="unmix",
    )(*arrays, *waits)


def parts_mask(parts):
    return [tuple(None if a is None else True for a in pair) for pair in parts]


def body(
    tokens,
    attn_gain,
    mlp_gain,
    w_query,
    w_key,
    w_value,
    w_out,
    w_gate,
    w_up,
    w_down,
    prefix,
    out_grad,
):
    mp = lax.axis_size("mp")
    place = lax.axis_index("mp")
    rows = tokens.shape[0]
    width_heads = w_query.shape[1]
    heads = width_heads // HD
    padded_heads = round_up(width_heads, LANES)
    width_ff = w_gate.shape[1]
    padded_ff = round_up(width_ff, FF_BLOCK)
    own = place * rows

    def row_block(value, index):
        return lax.dynamic_slice_in_dim(value, index * rows, rows, 0)

    tables = angle_tables()
    core = lax.axis_index("dp") % 2
    at = [jnp.stack([(place + mp - k) % mp, core]) for k in range(mp)]

    attn_pack = pack([w_query, w_key, w_value], LANES, padded_heads)
    attn_weights = dp_gather(attn_pack)
    ff_pack = pack([w_gate, w_up], FF_BLOCK, padded_ff, attn_pack)
    gate_up = dp_gather(ff_pack)
    token_pieces = ring_gather(tokens)
    qkv = None
    for k in range(mp - 1):
        qkv, mark = project(
            at[k], token_pieces[k], attn_gain[None], attn_weights, tables, qkv
        )
    out_own = gate(
        pack([w_out.T], LANES, padded_heads, ff_pack), token_pieces[-1], mark
    )
    out_pieces = [out_own] + [shift_back(out_own, mp - j) for j in range(1, mp)]
    qkv, _ = project(
        at[mp - 1], token_pieces[-1], attn_gain[None], attn_weights, tables, qkv
    )
    attended, attended_send, log_total = attend(qkv, prefix, heads)
    out_pack = chain(out_pieces, attended)
    attended_pieces = [attended, ring_up(gate(attended_send, out_pack))]
    out_weights = dp_gather(gate(out_pack, attended_pieces[1], gate_up))
    normed_one, whole_tokens = lay_tokens(
        at[0], token_pieces, attn_gain[None], (attended_pieces[1],)
    )
    down_pack = pack([w_down.T], LANES, padded_ff, whole_tokens)
    down = dp_gather(down_pack)
    while len(attended_pieces) < mp:
        attended_pieces.append(ring_up(attended_pieces[-1]))

    grad_pieces = [scaled(out_grad, attended_pieces[-1], down_pack, out_weights)]
    grad_pieces.append(ring_up(grad_pieces[0]))
    normed_two, split_two, middle = finish_middle(
        at[0], attended_pieces, out_weights, whole_tokens, mlp_gain[None], rows
    )
    grad_pieces.append(ring_up(gate(grad_pieces[1], normed_two)))
    hidden, slopes = feed(normed_two, gate_up)
    while len(grad_pieces) < mp:
        grad_pieces.append(ring_up(grad_pieces[-1]))
    by_chip = paired()

    def back_of(k, held, kind=BF16, waits=()):
        *held, term = feed_back(
            at[k % mp], grad_pieces[k % mp], slopes, down, gate_up, held, kind, waits
        )
        return held, term

    width = normed_two.shape[1]
    grad_pieces.append(ring_up(grad_pieces[-1]))
    held, total = back_of(1, None, waits=(grad_pieces[2],))
    arrived = ring_up(total)
    held, term = back_of(2, held, waits=(grad_pieces[3],))
    held, term_three = back_of(3, held)
    total = join(term, arrived, (term_three,))
    arrived = ring_up(total)
    attended_own = own_rows(at[0], attended_pieces, rows)
    (grad_both, grad_mlp), term_own = back_of(mp, held, F32, (total, attended_own))
    if by_chip:
        down_other = scatter_other(grad_mlp, hidden, 768, 6)
        total = join(term_three, arrived, (down_other,))
        arrived = ring_up(total)
        ff_other = scatter_other(split_two, grad_both, 1024, 11, (total,))
        down_chip = scatter_mine(
            grad_mlp, hidden, 768, 6, swap(gate(down_other, total), 1), (ff_other,)
        )
        waits = (down_chip, ff_other)
    else:
        total = join(term_three, arrived)
        arrived = ring_up(total)
        waits = ()
    grad_middle, grad_attn, split_attn, gain_two, zero = own_back(
        core[None], term_own, arrived, middle, out_grad, mlp_gain[None], waits
    )
    *mine, zero = spread(grad_attn, out_weights, mp)
    def mlp_chunk(k, zero):
        return lax.optimization_barrier(
            outer_cols(row_block(hidden, at[k % mp][0] + zero[0]), down)
        )

    arrived = [mine[0]] + [shift_back(mine[k], k) for k in range(1, mp)]
    chunk_one = mlp_chunk(1, zero).astype(BF16)
    if by_chip:
        ff_chip = scatter_mine(
            split_two, grad_both, 1024, 11, swap(gate(ff_other, split_attn), 1), (chunk_one,)
        )
        ff_share = scatter_around(ff_chip)
        down_share = scatter_around(gate(down_chip, zero))
        waits = (ff_chip,)
    else:
        ff_share = scatter_plain(split_two, grad_both)
        down_share = scatter_plain(grad_mlp, hidden)
        waits = ()
    out_other = scatter_other(split_attn, attended_own, 1280, 5, (chunk_one,))
    mlp_arrived = ring_up(gate(chunk_one, *arrived[1:]))
    out_arrived = swap(out_other, 1) if by_chip else None
    spots = jnp.stack([prefix[0], place])
    back = attend_back(
        qkv, attended, arrived, log_total, tables, spots, heads,
        (*waits, out_other) if by_chip else (),
    )

    def grad_one_term(k, zero=0):
        return lax.optimization_barrier(
            outer_cols(row_block(back, at[k % mp][0] + zero), attn_weights)
        )

    total = grad_one_term(1).astype(BF16)
    arrived = ring_up(total)
    index = lax.axis_index("dp")
    chip = jnp.stack([index // 2 % 2, index // 4])
    if by_chip:
        attn_other = scatter_other(normed_one, back, 640, 8, (total, mlp_arrived))
        attn_arrived = swap(attn_other, 1)
        out_parts, zero = scatter_chip(
            chip, split_attn, attended_own, 1280, 8, out_arrived, (total, attn_other)
        )
        out_moved = scatter_first(out_parts)
        total, zero = join_marked(
            grad_one_term(2, zero[0]), arrived, (attn_other, out_parts[1], out_parts[3])
        )
        arrived = ring_up(total)
        mlp_total = join(mlp_chunk(2, zero), mlp_arrived, (total,))
        mlp_arrived = ring_up(mlp_total)
        attn_parts, zero = scatter_chip(
            chip, normed_one, back, 640, 10, attn_arrived, (total, mlp_total)
        )
        attn_moved = scatter_first(attn_parts)
        total, zero = join_marked(
            grad_one_term(3, zero[0]), arrived, (attn_parts[1], attn_parts[3])
        )
        arrived = ring_up(total)
        term = grad_one_term(4, zero[0])
        out_half = scatter_halves(chip, out_parts, out_moved, (total,))
        out_share = scatter_second(out_half)
        mlp_total = join(
            mlp_chunk(3, zero), mlp_arrived, (total, out_half[0][1], out_half[1][1], term)
        )
        mlp_arrived = ring_up(mlp_total)
        attn_half = scatter_halves(chip, attn_parts, attn_moved, (mlp_total,))
        attn_share = scatter_second(attn_half)
        waits = (attn_half[0][1], attn_half[1][1])
    else:
        out_share = scatter_plain(split_attn, attended_own)
        attn_share = scatter_plain(normed_one, back)
        total = join(grad_one_term(2), arrived)
        arrived = ring_up(total)
        mlp_arrived = ring_up(join(mlp_chunk(2, zero), mlp_arrived))
        total = join(grad_one_term(3), arrived)
        arrived = ring_up(total)
        mlp_arrived = ring_up(join(mlp_chunk(3, zero), mlp_arrived))
        term = grad_one_term(4)
        waits = ()
    out_total, *out_mine = out_sum(out_share, mp, padded_heads)
    input_grad, gain_one, zero = finish_input(
        term, arrived, tokens, grad_middle, attn_gain[None],
        (*waits, mlp_arrived, *out_mine),
    )
    out_moved = [shift_back(out_mine[k - 1], k) for k in range(1, mp)]
    gains = sum_over(jnp.concatenate([gain_one, gain_two]), "dp")
    chunk = mlp_chunk(4, zero)
    grad_w_query, grad_w_key, grad_w_value = unmix(attn_share, 3, LANES, width_heads)
    grad_w_gate, grad_w_up = unmix(ff_share, 2, FF_BLOCK, width_ff)
    (grad_w_down,) = unmix(down_share, 1, LANES, width_ff)
    block_out = finish_block(middle, chunk, mlp_arrived)
    gains = sum_over(
        gate(gains, *out_moved, grad_w_query, grad_w_gate, grad_w_down, block_out), "mp"
    )
    grad_w_out = out_final(out_total, out_moved, width_heads, (block_out,))
    return (
        block_out,
        input_grad,
        grad_w_query,
        grad_w_key,
        grad_w_value,
        grad_w_out.T,
        grad_w_gate,
        grad_w_up,
        grad_w_down.T,
        gains[0],
        gains[1],
    )


def solution(mesh):
    return jax.shard_map(
        body,
        mesh=mesh,
        in_specs=(
            P(("dp", "mp"), None),
            P(),
            P(),
            P("dp", "mp"),
            P("dp", "mp"),
            P("dp", "mp"),
            P("mp", "dp"),
            P("dp", "mp"),
            P("dp", "mp"),
            P("mp", "dp"),
            P("dp"),
            P(("dp", "mp"), None),
        ),
        out_specs=(
            P(("dp", "mp"), None),
            P(("dp", "mp"), None),
            P("dp", "mp"),
            P("dp", "mp"),
            P("dp", "mp"),
            P("mp", "dp"),
            P("dp", "mp"),
            P("dp", "mp"),
            P("mp", "dp"),
            P(),
            P(),
        ),
        check_vma=False,
    )
```

```python
import functools

import jax
import jax.numpy as jnp
import numpy as np
from jax import lax
from jax.experimental import pallas as pl
from jax.experimental.pallas import tpu as pltpu
from jax.sharding import PartitionSpec as P

HD = 64
LEN = 1024
LANES = 128
EPSILON = 1e-05
BRANCH = 1.4 / 40**0.5
MASKED = -1e30
FF_BLOCK = 512
VMEM_LIMIT = 56 * 1024 * 1024

F32 = jnp.float32
BF16 = jnp.bfloat16


def round_up(value, unit):
    return -(-value // unit) * unit


def matmul(left, right):
    return jnp.dot(left, right, preferred_element_type=F32)


def inner_rows(left, right):
    return lax.dot_general(
        left, right, (((0,), (0,)), ((), ())), preferred_element_type=F32
    )


def outer_cols(left, right):
    return lax.dot_general(
        left, right, (((1,), (1,)), ((), ())), preferred_element_type=F32
    )


def cost(micros):
    return pl.CostEstimate(
        flops=int(micros * 3.0e9), bytes_accessed=0, transcendentals=0
    )


def params(limit=VMEM_LIMIT):
    return pltpu.CompilerParams(vmem_limit_bytes=limit)


def ring_up(value):
    n = lax.axis_size("mp")
    return lax.ppermute(value, "mp", [(i, (i + 1) % n) for i in range(n)])


def ring_gather(value):
    pieces = [value]
    for _ in range(lax.axis_size("mp") - 1):
        pieces.append(ring_up(pieces[-1]))
    return pieces


def ring_scatter(part):
    n = lax.axis_size("mp")
    place = lax.axis_index("mp")
    total = part((place + n - 1) % n)
    for step in range(1, n):
        sent = total.astype(BF16)
        arrived = ring_up(sent)
        term = lax.optimization_barrier(part((place + 2 * n - 1 - step) % n))
        total = term + arrived.astype(F32)
    return total


def shift_back(value, count):
    n = lax.axis_size("mp")
    return lax.ppermute(value, "mp", [(i, (i - count) % n) for i in range(n)])


def sum_over(value, axis):
    n = lax.axis_size(axis)
    bit = 1
    while bit < n:
        value = value + lax.ppermute(value, axis, [(i, i ^ bit) for i in range(n)])
        bit *= 2
    return value


def swap(value, bit):
    n = lax.axis_size("dp")
    return lax.ppermute(value, "dp", [(i, i ^ bit) for i in range(n)])


def dp_gather(value):
    return lax.all_gather(value, "dp", axis=0, tiled=True)


def paired():
    return lax.axis_size("dp") == 8


def split_columns(value):
    if not paired():
        return value[None]
    core = lax.axis_index("dp") % 2
    rows, width = value.shape
    shaped = value.reshape(rows, 4, 2, width // 8)

    def pick(which):
        return lax.dynamic_index_in_dim(shaped, which, 2, False).reshape(rows, width // 2)

    return jnp.stack([pick(core), pick(1 - core)])


def after_all(waits):
    return [pl.BlockSpec(memory_space=pl.ANY)] * len(waits)


def weight_kernel(joined, left_ref, right_ref, *refs):
    value = inner_rows(left_ref[...], right_ref[...])
    if joined:
        value = value + refs[0][...].astype(F32)
    refs[-1][...] = value.astype(BF16)


def weight_grad(left, right, side, height, width, micros, arrived=None, waits=()):
    depth, columns = left.shape[-2:]
    others = right.shape[1]
    specs = [
        pl.BlockSpec((None, depth, height), lambda i, j: (side, 0, i))
        if left.ndim == 3
        else pl.BlockSpec((depth, height), lambda i, j: (0, i)),
        pl.BlockSpec((depth, width), lambda i, j: (0, j)),
    ]
    args = [left, right]
    if arrived is not None:
        specs.append(pl.BlockSpec((height, width), lambda i, j: (i, j)))
        args.append(arrived)
    return pl.pallas_call(
        functools.partial(weight_kernel, arrived is not None),
        out_shape=jax.ShapeDtypeStruct((columns, others), BF16),
        grid=(columns // height, others // width),
        in_specs=specs + after_all(waits),
        out_specs=pl.BlockSpec((height, width), lambda i, j: (i, j)),
        compiler_params=params(),
        cost_estimate=cost(micros),
        name="weight_grad",
    )(*args, *waits)


def scatter_other(left, right, width, micros, waits=()):
    if not paired():
        return None
    return weight_grad(left, right, 1, left.shape[2], width, micros, waits=waits)


def chip_kernel(where_ref, left_ref, right_ref, arrived_ref, *refs):
    one_kept, one_sent, two_kept, two_sent, zero_ref, total = refs[-6:]
    zero_ref[0] = 0
    value = inner_rows(left_ref[...], right_ref[...]) + arrived_ref[...].astype(F32)
    total[...] = value.astype(BF16)
    x, y = where_ref[0], where_ref[1]
    rows = total.shape[0] // 4
    half = rows // 2
    for k in (0, 1):
        for one_ref, two_ref, near_x, near_y in (
            (one_kept, two_kept, x, y),
            (one_sent, two_sent, 1 - x, 1 - y),
        ):
            start = pl.multiple_of((2 * near_y + k) * rows, 16)
            one_ref[k] = total[pl.ds(start, half), :]
            start = pl.multiple_of((2 * k + near_x) * rows + half, 16)
            two_ref[k] = total[pl.ds(start, half), :]


def scatter_chip(where, left, right, width, micros, arrived, waits=()):
    depth, columns = left.shape[1:]
    others = right.shape[1]
    half = columns // 8
    out = jax.ShapeDtypeStruct((2, half, others), BF16)
    block = pl.BlockSpec((2, half, width), lambda j, w: (0, 0, j))
    *parts, zero = pl.pallas_call(
        chip_kernel,
        out_shape=(out, out, out, out, jax.ShapeDtypeStruct((1,), jnp.int32)),
        grid_spec=pltpu.PrefetchScalarGridSpec(
            num_scalar_prefetch=1,
            grid=(others // width,),
            in_specs=[
                pl.BlockSpec((None, depth, columns), lambda j, w: (0, 0, 0)),
                pl.BlockSpec((depth, width), lambda j, w: (0, j)),
                pl.BlockSpec((columns, width), lambda j, w: (0, j)),
            ]
            + after_all(waits),
            out_specs=(block, block, block, block, pl.BlockSpec(memory_space=pltpu.SMEM)),
            scratch_shapes=[pltpu.VMEM((columns, width), BF16)],
        ),
        compiler_params=params(),
        cost_estimate=cost(micros),
        name="scatter_chip",
    )(where, left, right, arrived, *waits)
    return parts, zero


def scatter_first(parts):
    return swap(parts[1], 4), swap(parts[3], 2)


def halves_kernel(where_ref, kept_ref, moved_ref, *refs):
    keep_ref, send_ref, total = refs[-3:]
    total[...] = (kept_ref[...].astype(F32) + moved_ref[...].astype(F32)).astype(BF16)
    keep_ref[...] = total[where_ref[0]]
    send_ref[...] = total[1 - where_ref[0]]


def halves(where, kept, moved, waits):
    whole = pl.BlockSpec(memory_space=pltpu.VMEM)
    out = jax.ShapeDtypeStruct(kept.shape[1:], BF16)
    return pl.pallas_call(
        halves_kernel,
        out_shape=(out, out),
        in_specs=[pl.BlockSpec(memory_space=pltpu.SMEM), whole, whole] + after_all(waits),
        out_specs=(whole, whole),
        scratch_shapes=[pltpu.VMEM(kept.shape, BF16)],
        compiler_params=params(),
        cost_estimate=cost(3),
        name="halves",
    )(where, kept, moved, *waits)


def scatter_halves(where, parts, moved, waits=()):
    return (
        halves(where[0:1], parts[0], moved[0], waits),
        halves(where[1:2], parts[2], moved[1], waits),
    )


def scatter_second(both):
    (one, one_sent), (two, two_sent) = both
    return [(one, swap(one_sent, 2)), (two, swap(two_sent, 4))]


def scatter_plain(left, right):
    return scatter_whole(inner_rows(left[0], right).astype(BF16))


def pass_kernel(*refs):
    pass


def gate(value, *waits):
    return pl.pallas_call(
        pass_kernel,
        out_shape=jax.ShapeDtypeStruct(value.shape, value.dtype),
        in_specs=after_all((value, *waits)),
        out_specs=pl.BlockSpec(memory_space=pl.ANY),
        input_output_aliases={0: 0},
        cost_estimate=cost(1),
        name="gate",
    )(value, *waits)


def join_kernel(one_ref, two_ref, *refs):
    out_ref, zero_ref = refs[-2:]
    out_ref[...] = (one_ref[...].astype(F32) + two_ref[...].astype(F32)).astype(BF16)
    zero_ref[0] = 0


def join_marked(one, two, waits=()):
    rows, width = one.shape
    block = pl.BlockSpec((rows // 2, width), lambda i: (i, 0))
    return pl.pallas_call(
        join_kernel,
        out_shape=(
            jax.ShapeDtypeStruct(one.shape, BF16),
            jax.ShapeDtypeStruct((1,), jnp.int32),
        ),
        grid=(2,),
        in_specs=[block, block] + after_all(waits),
        out_specs=(block, pl.BlockSpec(memory_space=pltpu.SMEM)),
        compiler_params=params(),
        cost_estimate=cost(3),
        name="join",
    )(one, two, *waits)


def join(one, two, waits=()):
    return join_marked(one, two, waits)[0]


def scatter_mine(left, right, width, micros, arrived, waits=()):
    return weight_grad(left, right, 0, left.shape[2], width, micros, arrived, waits)


def scatter_around(chip):
    share = lax.psum_scatter(
        chip,
        "dp",
        scatter_dimension=0,
        tiled=True,
        axis_index_groups=[[2 * k + core for k in AROUND] for core in (0, 1)],
    )
    return [(share, None)]


def scatter_whole(partial):
    share = lax.psum_scatter(partial, "dp", scatter_dimension=0, tiled=True)
    return [(share, None)]


def angle_tables():
    half = HD // 2
    rates = 10000.0 ** (-np.arange(half) * 2.0 / HD)
    angles = np.arange(LEN)[:, None] * rates[None, :]
    cosine, sine = np.cos(angles), np.sin(angles)
    return (
        jnp.asarray(np.concatenate([cosine] * 4, axis=-1), F32),
        jnp.asarray(np.concatenate([-sine, sine] * 2, axis=-1), F32),
    )


def swap_halves(value):
    lane = lax.broadcasted_iota(jnp.int32, value.shape, 1)
    low = (lane % HD) < HD // 2
    return jnp.where(
        low, pltpu.roll(value, LANES - HD // 2, 1), pltpu.roll(value, HD // 2, 1)
    )


AROUND = (0, 1, 3, 2)


def put_split(ref, value, core, chips=(0, 1, 2, 3), rows=slice(None)):
    if ref.shape[0] == 1:
        ref[0, rows, :] = value
        return
    block = value.shape[1] // 8
    for which in (0, 1):

        @pl.when(core == which)
        def _():
            for side in (0, 1):
                for spot, chip in enumerate(chips):
                    start = (2 * chip + (which ^ side)) * block
                    ref[side, rows, spot * block : (spot + 1) * block] = value[
                        :, start : start + block
                    ]


def split_shape(rows, width):
    return (2, rows, width // 2) if paired() else (1, rows, width)


def normed_of(value, gain):
    value = value.astype(F32)
    factor = lax.rsqrt(jnp.mean(value * value, axis=-1, keepdims=True) + EPSILON)
    return (value * factor * gain).astype(BF16)


def project_kernel(where_ref, x_ref, gain_ref, w_ref, cos_ref, sin_ref, *refs):
    qkv_ref, mark_ref, held = refs[-3:]

    @pl.when(pl.program_id(0) == 0)
    def _():
        mark_ref[...] = jnp.zeros_like(mark_ref)
        held[...] = normed_of(x_ref[...], gain_ref[...])

    product = matmul(held[...], w_ref[...])
    cosine, sine = cos_ref[...], sin_ref[...]
    query = product[:, :LANES]
    key = product[:, LANES : 2 * LANES]
    query = (query * cosine + swap_halves(query) * sine).astype(BF16)
    qkv_ref[:, :LANES] = query * HD**-0.5
    qkv_ref[:, LANES : 2 * LANES] = (key * cosine + swap_halves(key) * sine).astype(BF16)
    qkv_ref[:, 2 * LANES :] = product[:, 2 * LANES :].astype(BF16)


def project(where, piece, gain, weights, tables, held):
    rows, width = piece.shape
    columns = weights.shape[1]
    block = 3 * LANES
    specs = [
        pl.BlockSpec((rows, width), lambda i, w: (0, 0)),
        pl.BlockSpec((1, width), lambda i, w: (0, 0)),
        pl.BlockSpec((width, block), lambda i, w: (0, i)),
        pl.BlockSpec((rows, LANES), lambda i, w: (w[0], 0)),
        pl.BlockSpec((rows, LANES), lambda i, w: (w[0], 0)),
    ]
    args = [piece, gain, weights, *tables]
    aliases = {}
    if held is not None:
        aliases[1 + len(args)] = 0
        args.append(held)
        specs.append(pl.BlockSpec(memory_space=pl.ANY))
    return pl.pallas_call(
        project_kernel,
        out_shape=(
            jax.ShapeDtypeStruct((LEN, columns), BF16),
            jax.ShapeDtypeStruct((8, LANES), F32),
        ),
        grid_spec=pltpu.PrefetchScalarGridSpec(
            num_scalar_prefetch=1,
            grid=(columns // block,),
            in_specs=specs,
            out_specs=(
                pl.BlockSpec((rows, block), lambda i, w: (w[0], i)),
                pl.BlockSpec((8, LANES), lambda i, w: (0, 0)),
            ),
            scratch_shapes=[pltpu.VMEM((rows, width), BF16)],
        ),
        input_output_aliases=aliases,
        compiler_params=params(),
        cost_estimate=cost(9),
        name="project",
    )(where, *args)


def lay_tokens_kernel(count, place_ref, gain_ref, *refs):
    norm_ref, copy_ref = refs[-2:]
    rows = refs[0].shape[0]
    for k in range(count):
        start = pl.multiple_of(lax.rem(place_ref[0] + count - k, count) * rows, rows)
        here = pl.ds(start, rows)
        copy_ref[here, :] = refs[k][...]
        put_split(norm_ref, normed_of(refs[k][...], gain_ref[...]), place_ref[1], rows=here)


def lay_tokens(place, pieces, gain, waits):
    rows, width = pieces[0].shape
    count = len(pieces)
    whole = pl.BlockSpec(memory_space=pltpu.VMEM)
    return pl.pallas_call(
        functools.partial(lay_tokens_kernel, count),
        out_shape=(
            jax.ShapeDtypeStruct(split_shape(count * rows, width), BF16),
            jax.ShapeDtypeStruct((count * rows, width), BF16),
        ),
        in_specs=[pl.BlockSpec(memory_space=pltpu.SMEM)] + [whole] * (1 + count)
        + after_all(waits),
        out_specs=(whole, whole),
        compiler_params=params(),
        cost_estimate=cost(10),
        name="lay_tokens",
    )(place, gain, *pieces, *waits)


PARTS = (
    (0, 512, ((0, 512, True),)),
    (512, 256, ((0, 512, False), (512, 256, True))),
    (768, 256, ((0, 768, False), (768, 256, True))),
)


def visible(shape, first_key, first_query, limit):
    key = first_key + lax.broadcasted_iota(jnp.int32, shape, 0)
    query = first_query + lax.broadcasted_iota(jnp.int32, shape, 1)
    return (key < limit) | (key <= query)


def head_only(value, head):
    lane = lax.broadcasted_iota(jnp.int32, value.shape, 1)
    return jnp.where((lane >= HD) == (head == 1), value, jnp.zeros_like(value))


def attend_kernel(heads, prefix_ref, qkv_ref, out_ref, send_ref, log_ref, turned):
    limit = prefix_ref[0]
    pair = pl.program_id(0)
    values_across = qkv_ref[:, 2 * LANES :].T
    for head in (0, 1):

        @pl.when(2 * pair + head < heads)
        def _():
            queries = head_only(qkv_ref[:, :LANES], head)
            for first, count, spans in PARTS:
                mine = queries[first : first + count]
                scores = []
                for start, keys, masked in spans:
                    raw = outer_cols(qkv_ref[start : start + keys, LANES : 2 * LANES], mine)
                    if masked:
                        raw = jnp.where(visible(raw.shape, start, first, limit), raw, MASKED)
                    scores.append(raw)
                top = functools.reduce(
                    jnp.maximum, [jnp.max(s, axis=0, keepdims=True) for s in scores]
                )
                total = jnp.zeros_like(top)
                summed = jnp.zeros((HD, count), F32)
                for (start, keys, _), raw in zip(spans, scores):
                    weight = jnp.exp(raw - top)
                    total = total + jnp.sum(weight, axis=0, keepdims=True)
                    summed = summed + matmul(
                        values_across[head * HD : (head + 1) * HD, start : start + keys],
                        weight.astype(BF16),
                    )
                turned[head * HD : (head + 1) * HD, first : first + count] = summed / total
                log_ref[0, head : head + 1, first : first + count] = top + jnp.log(total)

        @pl.when(2 * pair + head >= heads)
        def _():
            turned[head * HD : (head + 1) * HD, :] = jnp.zeros((HD, LEN), F32)
            log_ref[0, head : head + 1, :] = jnp.zeros((1, LEN), F32)

    value = turned[...].T.astype(BF16)
    out_ref[...] = value
    send_ref[...] = value


def attend(qkv, prefix, heads):
    pairs = qkv.shape[1] // (3 * LANES)
    return pl.pallas_call(
        functools.partial(attend_kernel, heads),
        out_shape=(
            jax.ShapeDtypeStruct((LEN, pairs * LANES), BF16),
            jax.ShapeDtypeStruct((LEN, pairs * LANES), BF16),
            jax.ShapeDtypeStruct((pairs, 2, LEN), F32),
        ),
        grid_spec=pltpu.PrefetchScalarGridSpec(
            num_scalar_prefetch=1,
            grid=(pairs,),
            in_specs=[pl.BlockSpec((LEN, 3 * LANES), lambda i, s: (0, i))],
            out_specs=(
                pl.BlockSpec((LEN, LANES), lambda i, s: (0, i)),
                pl.BlockSpec((LEN, LANES), lambda i, s: (0, i)),
                pl.BlockSpec((1, 2, LEN), lambda i, s: (i, 0, 0)),
            ),
            scratch_shapes=[pltpu.VMEM((LANES, LEN), F32)],
        ),
        compiler_params=params(),
        cost_estimate=cost(18),
        name="attend",
    )(prefix, qkv)


def attend_back_kernel(
    heads, count, prefix_ref, qkv_ref, out_ref, *refs
):
    arrived = refs[:count]
    log_ref, cos_ref, sin_ref = refs[count : count + 3]
    back_ref, turned, grad_key, grad_value, grad_ref = refs[-5:]
    limit = prefix_ref[0]
    rows = arrived[0].shape[0]
    for k in range(count):
        start = pl.multiple_of(lax.rem(prefix_ref[1] + k, count) * rows, rows)
        grad_ref[pl.ds(start, rows), :] = arrived[k][...]
    pair = pl.program_id(0)
    keys_across = qkv_ref[:, LANES : 2 * LANES].T
    inner = (out_ref[...].astype(F32) * grad_ref[...].astype(F32)).T
    grad_key[...] = jnp.zeros_like(grad_key)
    grad_value[...] = jnp.zeros_like(grad_value)
    for head in (0, 1):
        band = slice(head * HD, (head + 1) * HD)

        @pl.when(2 * pair + head < heads)
        def _():
            queries = head_only(qkv_ref[:, :LANES], head)
            grads = head_only(grad_ref[...], head)
            inner_row = jnp.sum(inner[band], axis=0, keepdims=True)
            for first, count, spans in PARTS:
                here = slice(first, first + count)
                mine, grad_mine = queries[here], grads[here]
                log_mine = log_ref[0, head : head + 1, here]
                inner_mine = inner_row[:, here]
                summed = jnp.zeros((HD, count), F32)
                for start, keys, masked in spans:
                    there = slice(start, start + keys)
                    raw = outer_cols(qkv_ref[there, LANES : 2 * LANES], mine)
                    chance = jnp.exp(raw - log_mine)
                    if masked:
                        chance = jnp.where(
                            visible(raw.shape, start, first, limit), chance, 0.0
                        )
                    grad_chance = outer_cols(qkv_ref[there, 2 * LANES :], grad_mine)
                    grad_score = (chance * (grad_chance - inner_mine)).astype(BF16)
                    grad_key[there, :] += matmul(grad_score, mine)
                    grad_value[there, :] += matmul(chance.astype(BF16), grad_mine)
                    summed = summed + matmul(keys_across[band, there], grad_score)
                turned[band, here] = summed

        @pl.when(2 * pair + head >= heads)
        def _():
            turned[band, :] = jnp.zeros((HD, LEN), F32)

    cosine, sine = cos_ref[...], sin_ref[...]
    grad_query = turned[...].T * HD**-0.5
    back_ref[:, :LANES] = (grad_query * cosine - swap_halves(grad_query) * sine).astype(BF16)
    back = grad_key[...]
    back_ref[:, LANES : 2 * LANES] = (back * cosine - swap_halves(back) * sine).astype(BF16)
    back_ref[:, 2 * LANES :] = grad_value[...].astype(BF16)


def attend_back(qkv, attended, arrived, log_total, tables, prefix, heads, waits=()):
    pairs = qkv.shape[1] // (3 * LANES)
    count, rows = len(arrived), arrived[0].shape[0]
    return pl.pallas_call(
        functools.partial(attend_back_kernel, heads, count),
        out_shape=jax.ShapeDtypeStruct(qkv.shape, BF16),
        grid_spec=pltpu.PrefetchScalarGridSpec(
            num_scalar_prefetch=1,
            grid=(pairs,),
            in_specs=[
                pl.BlockSpec((LEN, 3 * LANES), lambda i, s: (0, i)),
                pl.BlockSpec((LEN, LANES), lambda i, s: (0, i)),
            ]
            + [pl.BlockSpec((rows, LANES), lambda i, s: (0, i))] * count
            + [
                pl.BlockSpec((1, 2, LEN), lambda i, s: (i, 0, 0)),
                pl.BlockSpec((LEN, LANES), lambda i, s: (0, 0)),
                pl.BlockSpec((LEN, LANES), lambda i, s: (0, 0)),
            ]
            + after_all(waits),
            out_specs=pl.BlockSpec((LEN, 3 * LANES), lambda i, s: (0, i)),
            scratch_shapes=[
                pltpu.VMEM((LANES, LEN), F32),
                pltpu.VMEM((LEN, LANES), F32),
                pltpu.VMEM((LEN, LANES), F32),
                pltpu.VMEM((LEN, LANES), BF16),
            ],
        ),
        compiler_params=params(),
        cost_estimate=cost(28),
        name="attend_back",
    )(prefix, qkv, attended, *arrived, log_total, *tables, *waits)


def middle_kernel(count, place_ref, *refs):
    pieces = refs[:count]
    w_ref, x_ref, gain_ref, normed_ref, split_ref, own_ref = refs[count:]
    depth = pieces[0].shape[1]
    total = None
    for k in range(count):
        term = outer_cols(pieces[k][...], w_ref[:, k * depth : (k + 1) * depth])
        total = term if total is None else total + term
    middle = x_ref[...].astype(F32) + BRANCH * total
    factor = lax.rsqrt(jnp.mean(middle * middle, axis=-1, keepdims=True) + EPSILON)
    normed = (middle * factor * gain_ref[...]).astype(BF16)
    normed_ref[...] = normed
    put_split(split_ref, normed, place_ref[1], AROUND)
    rows, own = x_ref.shape[0], own_ref.shape[0]
    for part in range(rows // own):

        @pl.when(pl.program_id(0) * (rows // own) + part == place_ref[0])
        def _():
            own_ref[...] = middle[part * own : (part + 1) * own]


def finish_middle(place, pieces, weights, tokens, gain, own):
    width = tokens.shape[1]
    depth = pieces[0].shape[1]
    count = len(pieces)
    rows = 2 * own
    return pl.pallas_call(
        functools.partial(middle_kernel, count),
        out_shape=(
            jax.ShapeDtypeStruct((LEN, width), BF16),
            jax.ShapeDtypeStruct(split_shape(LEN, width), BF16),
            jax.ShapeDtypeStruct((own, width), F32),
        ),
        grid_spec=pltpu.PrefetchScalarGridSpec(
            num_scalar_prefetch=1,
            grid=(LEN // rows,),
            in_specs=[pl.BlockSpec((rows, depth), lambda i, s: (i, 0))] * count
            + [
                pl.BlockSpec((width, count * depth), lambda i, s: (0, 0)),
                pl.BlockSpec((rows, width), lambda i, s: (i, 0)),
                pl.BlockSpec((1, width), lambda i, s: (0, 0)),
            ],
            out_specs=(
                pl.BlockSpec((rows, width), lambda i, s: (i, 0)),
                pl.BlockSpec(split_shape(rows, width), lambda i, s: (0, i, 0)),
                pl.BlockSpec((own, width), lambda i, s: (0, 0)),
            ),
        ),
        compiler_params=params(),
        cost_estimate=cost(22),
        name="finish_middle",
    )(place, *pieces, weights, tokens, gain)


def gate_kernel(normed_ref, weight_ref, hidden_ref, slope_ref):
    rows = 256
    for start in range(0, LEN, rows):
        here = slice(start, start + rows)
        product = matmul(normed_ref[here], weight_ref[...])
        gate, up = product[:, :FF_BLOCK], product[:, FF_BLOCK:]
        sigmoid = jax.nn.sigmoid(gate)
        silu = gate * sigmoid
        hidden_ref[here, :] = (silu * up).astype(BF16)
        slope_ref[here, :FF_BLOCK] = (up * (sigmoid + silu * (1.0 - sigmoid))).astype(BF16)
        slope_ref[here, FF_BLOCK:] = silu.astype(BF16)


def feed(normed, gate_up):
    width = normed.shape[1]
    hidden = gate_up.shape[1] // 2
    return pl.pallas_call(
        gate_kernel,
        out_shape=(
            jax.ShapeDtypeStruct((LEN, hidden), BF16),
            jax.ShapeDtypeStruct((LEN, 2 * hidden), BF16),
        ),
        grid=(hidden // FF_BLOCK,),
        in_specs=[
            pl.BlockSpec((LEN, width), lambda i: (0, 0)),
            pl.BlockSpec((width, 2 * FF_BLOCK), lambda i: (0, i)),
        ],
        out_specs=(
            pl.BlockSpec((LEN, FF_BLOCK), lambda i: (0, i)),
            pl.BlockSpec((LEN, 2 * FF_BLOCK), lambda i: (0, i)),
        ),
        compiler_params=params(),
        cost_estimate=cost(21),
        name="feed",
    )(normed, gate_up)


def feed_back_kernel(where_ref, grad_ref, slope_ref, down_ref, weight_ref, *refs):
    both_ref, copy_ref, sum_ref, total = refs[-4:]
    step = pl.program_id(0)

    @pl.when(step == 0)
    def _():
        put_split(copy_ref, grad_ref[...], where_ref[1], AROUND)
        total[...] = jnp.zeros_like(total)

    grad = matmul(grad_ref[...], down_ref[...])
    grads = jnp.concatenate([grad, grad], axis=1)
    both = (grads * slope_ref[...].astype(F32)).astype(BF16)
    both_ref[...] = both
    total[...] += outer_cols(both, weight_ref[...])

    @pl.when(step == pl.num_programs(0) - 1)
    def _():
        sum_ref[...] = total[...].astype(sum_ref.dtype)


def feed_back(where, piece, slopes, down, gate_up, held, kind, waits=()):
    rows, width = piece.shape
    hidden = down.shape[1]
    specs = [
        pl.BlockSpec((rows, width), lambda i, w: (0, 0)),
        pl.BlockSpec((rows, 2 * FF_BLOCK), lambda i, w: (w[0], i)),
        pl.BlockSpec((width, FF_BLOCK), lambda i, w: (0, i)),
        pl.BlockSpec((width, 2 * FF_BLOCK), lambda i, w: (0, i)),
    ]
    args = [piece, slopes, down, gate_up]
    aliases = {}
    if held is not None:
        for index, array in enumerate(held):
            aliases[1 + len(args)] = index
            args.append(array)
            specs.append(pl.BlockSpec(memory_space=pl.ANY))
    args += waits
    specs += after_all(waits)
    return pl.pallas_call(
        feed_back_kernel,
        out_shape=(
            jax.ShapeDtypeStruct((LEN, 2 * hidden), BF16),
            jax.ShapeDtypeStruct(split_shape(LEN, width), BF16),
            jax.ShapeDtypeStruct((rows, width), kind),
        ),
        grid_spec=pltpu.PrefetchScalarGridSpec(
            num_scalar_prefetch=1,
            grid=(hidden // FF_BLOCK,),
            in_specs=specs,
            out_specs=(
                pl.BlockSpec((rows, 2 * FF_BLOCK), lambda i, w: (w[0], i)),
                pl.BlockSpec(split_shape(rows, width), lambda i, w: (0, w[0], 0)),
                pl.BlockSpec((rows, width), lambda i, w: (0, 0)),
            ),
            scratch_shapes=[pltpu.VMEM((rows, width), F32)],
        ),
        input_output_aliases=aliases,
        compiler_params=params(),
        cost_estimate=cost(15),
        name="feed_back",
    )(where, *args)


def out_sum_kernel(parts, count, width, *refs):
    terms, outs = grouped(parts, refs)
    outs = outs[-count:]
    half = outs[0].shape[0] // len(parts)
    for index, pair in enumerate(terms):
        value = added(pair)
        here = slice(index * half, (index + 1) * half)
        for k in range(count):
            outs[k][here, :] = value[:, k * width : (k + 1) * width].astype(outs[k].dtype)


def out_sum(parts, count, width, waits=()):
    rows = len(parts) * parts[0][0].shape[0]
    arrays = [a for pair in parts for a in pair if a is not None]
    return pl.pallas_call(
        functools.partial(out_sum_kernel, parts_mask(parts), count, width),
        out_shape=tuple(
            jax.ShapeDtypeStruct((rows, width), BF16 if k else F32) for k in range(count)
        ),
        in_specs=[pl.BlockSpec(memory_space=pltpu.VMEM)] * len(arrays) + after_all(waits),
        compiler_params=params(),
        cost_estimate=cost(3),
        name="out_sum",
    )(*arrays, *waits)


def out_final_kernel(count, *refs):
    total = refs[0][...]
    for ref in refs[1:count]:
        total = total + ref[...].astype(F32)
    refs[-1][...] = total[:, : refs[-1].shape[1]]


def out_final(own, moved, width, waits):
    whole = pl.BlockSpec(memory_space=pltpu.VMEM)
    count = 1 + len(moved)
    return pl.pallas_call(
        functools.partial(out_final_kernel, count),
        out_shape=jax.ShapeDtypeStruct((own.shape[0], width), F32),
        in_specs=[whole] * count + after_all(waits),
        out_specs=whole,
        compiler_params=params(),
        cost_estimate=cost(3),
        name="out_final",
    )(own, *moved, *waits)


def spread_kernel(count, value_ref, weight_ref, *refs):
    product = matmul(value_ref[...], weight_ref[...]).astype(BF16)
    refs[-1][0] = 0
    for k in range(count):

        @pl.when(pl.program_id(0) == k)
        def _():
            refs[k][...] = product


def spread(value, weights, count):
    rows, depth = value.shape
    width = weights.shape[1] // count
    return pl.pallas_call(
        functools.partial(spread_kernel, count),
        out_shape=tuple(jax.ShapeDtypeStruct((rows, width), BF16) for _ in range(count))
        + (jax.ShapeDtypeStruct((1,), jnp.int32),),
        grid=(count,),
        in_specs=[
            pl.BlockSpec((rows, depth), lambda i: (0, 0)),
            pl.BlockSpec((depth, width), lambda i: (0, i)),
        ],
        out_specs=tuple(pl.BlockSpec((rows, width), lambda i: (0, 0)) for _ in range(count))
        + (pl.BlockSpec(memory_space=pltpu.SMEM),),
        compiler_params=params(),
        cost_estimate=cost(8),
        name="spread",
    )(value, weights)


def norm_back(value, gain, incoming):
    factor = lax.rsqrt(jnp.mean(value * value, axis=-1, keepdims=True) + EPSILON)
    normed = value * factor
    scaled_in = incoming * gain
    inner = jnp.mean(scaled_in * normed, axis=-1, keepdims=True)
    return (
        factor * (scaled_in - normed * inner),
        jnp.sum(incoming * normed, axis=0, keepdims=True),
    )


def own_back_kernel(
    core_ref, term_ref, arrived_ref, middle_ref, grad_ref, gain_ref, *refs
):
    sum_ref, send_ref, split_ref, gain_sum_ref, zero_ref = refs[-5:]
    incoming = term_ref[...].astype(F32) + arrived_ref[...].astype(F32)
    back, gain_sum = norm_back(middle_ref[...], gain_ref[...], incoming)
    total = grad_ref[...].astype(F32) + back
    sum_ref[...] = total
    sent = (BRANCH * total).astype(BF16)
    send_ref[...] = sent
    put_split(split_ref, sent, core_ref[0])
    zero_ref[0] = 0

    @pl.when(pl.program_id(0) == 0)
    def _():
        gain_sum_ref[...] = jnp.zeros_like(gain_sum_ref)

    gain_sum_ref[...] += gain_sum


def own_back(core, term, arrived, middle, grad, gain, waits=()):
    rows, width = middle.shape
    step = rows // 2
    block = pl.BlockSpec((step, width), lambda i, s: (i, 0))
    line = pl.BlockSpec((1, width), lambda i, s: (0, 0))
    return pl.pallas_call(
        own_back_kernel,
        out_shape=(
            jax.ShapeDtypeStruct((rows, width), F32),
            jax.ShapeDtypeStruct((rows, width), BF16),
            jax.ShapeDtypeStruct(split_shape(rows, width), BF16),
            jax.ShapeDtypeStruct((1, width), F32),
            jax.ShapeDtypeStruct((1,), jnp.int32),
        ),
        grid_spec=pltpu.PrefetchScalarGridSpec(
            num_scalar_prefetch=1,
            grid=(2,),
            in_specs=[block, block, block, block, line] + after_all(waits),
            out_specs=(
                block,
                block,
                pl.BlockSpec(split_shape(step, width), lambda i, s: (0, i, 0)),
                line,
                pl.BlockSpec(memory_space=pltpu.SMEM),
            ),
        ),
        compiler_params=params(),
        cost_estimate=cost(5),
        name="own_back",
    )(core, term, arrived, middle, grad, gain, *waits)


def finish_input_kernel(term_ref, arrived_ref, x_ref, sum_ref, gain_ref, *refs):
    out_ref, gain_sum_ref, zero_ref = refs[-3:]
    incoming = term_ref[...] + arrived_ref[...].astype(F32)
    back, gain_sum = norm_back(x_ref[...].astype(F32), gain_ref[...], incoming)
    out_ref[...] = (sum_ref[...] + back).astype(BF16)
    zero_ref[0] = 0

    @pl.when(pl.program_id(0) == 0)
    def _():
        gain_sum_ref[...] = jnp.zeros_like(gain_sum_ref)

    gain_sum_ref[...] += gain_sum


def finish_input(term, arrived, x, total, gain, waits=()):
    rows, width = x.shape
    block = pl.BlockSpec((rows // 2, width), lambda i: (i, 0))
    line = pl.BlockSpec((1, width), lambda i: (0, 0))
    return pl.pallas_call(
        finish_input_kernel,
        out_shape=(
            jax.ShapeDtypeStruct((rows, width), BF16),
            jax.ShapeDtypeStruct((1, width), F32),
            jax.ShapeDtypeStruct((1,), jnp.int32),
        ),
        grid=(2,),
        in_specs=[block, block, block, block, line] + after_all(waits),
        out_specs=(block, line, pl.BlockSpec(memory_space=pltpu.SMEM)),
        compiler_params=params(),
        cost_estimate=cost(5),
        name="finish_input",
    )(term, arrived, x, total, gain, *waits)


def finish_block_kernel(middle_ref, term_ref, arrived_ref, *refs):
    total = term_ref[...] + arrived_ref[...].astype(F32)
    refs[-1][...] = (middle_ref[...] + BRANCH * total).astype(BF16)


def finish_block(middle, term, arrived, waits=()):
    rows, width = middle.shape
    block = pl.BlockSpec((rows // 2, width), lambda i: (i, 0))
    return pl.pallas_call(
        finish_block_kernel,
        out_shape=jax.ShapeDtypeStruct((rows, width), BF16),
        grid=(2,),
        in_specs=[block, block, block] + after_all(waits),
        out_specs=block,
        compiler_params=params(),
        cost_estimate=cost(3),
        name="finish_block",
    )(middle, term, arrived, *waits)


def mix(out_ref, refs, block):
    width = refs[0].shape[1]
    count = len(refs)
    for first in range(0, width, block):
        size = min(block, width - first)
        base = first * count
        for index, ref in enumerate(refs):
            spot = base + index * block
            out_ref[:, spot : spot + size] = ref[:, first : first + size]
            if size < block:
                out_ref[:, spot + size : spot + block] = jnp.zeros(
                    (ref.shape[0], block - size), out_ref.dtype
                )


def pack_kernel(count, block, *refs):
    mix(refs[-1], refs[:count], block)


def pack(values, block, width, *waits):
    count = len(values)
    rows = values[0].shape[0]
    whole = pl.BlockSpec(memory_space=pltpu.VMEM)
    return pl.pallas_call(
        functools.partial(pack_kernel, count, block),
        out_shape=jax.ShapeDtypeStruct((rows, count * width), BF16),
        in_specs=[whole] * count + after_all(waits),
        out_specs=whole,
        compiler_params=params(),
        cost_estimate=cost(3),
        name="pack",
    )(*values, *waits)


def chain_kernel(count, *refs):
    out_ref = refs[-1]
    width = refs[0].shape[1]
    for k in range(count):
        out_ref[:, k * width : (k + 1) * width] = refs[k][...]


def chain(values, *waits):
    rows, width = values[0].shape
    whole = pl.BlockSpec(memory_space=pltpu.VMEM)
    return pl.pallas_call(
        functools.partial(chain_kernel, len(values)),
        out_shape=jax.ShapeDtypeStruct((rows, len(values) * width), values[0].dtype),
        in_specs=[whole] * len(values) + after_all(waits),
        out_specs=whole,
        compiler_params=params(),
        cost_estimate=cost(2),
        name="chain",
    )(*values, *waits)


def own_rows_kernel(count, place_ref, *refs):
    width = refs[0].shape[1]
    for k in range(count):
        refs[-1][:, k * width : (k + 1) * width] = refs[k][...]


def own_rows(place, pieces, rows):
    width = pieces[0].shape[1]
    count = len(pieces)
    return pl.pallas_call(
        functools.partial(own_rows_kernel, count),
        out_shape=jax.ShapeDtypeStruct((rows, count * width), pieces[0].dtype),
        grid_spec=pltpu.PrefetchScalarGridSpec(
            num_scalar_prefetch=1,
            grid=(1,),
            in_specs=[pl.BlockSpec((rows, width), lambda i, s: (s[0], 0))] * count,
            out_specs=pl.BlockSpec((rows, count * width), lambda i, s: (0, 0)),
        ),
        compiler_params=params(),
        cost_estimate=cost(2),
        name="own_rows",
    )(place, *pieces)


def scale_kernel(value_ref, *refs):
    refs[-1][...] = (BRANCH * value_ref[...].astype(F32)).astype(BF16)


def scaled(value, *waits):
    whole = pl.BlockSpec(memory_space=pltpu.VMEM)
    return pl.pallas_call(
        scale_kernel,
        out_shape=jax.ShapeDtypeStruct(value.shape, BF16),
        in_specs=[whole] + [pl.BlockSpec(memory_space=pl.ANY)] * len(waits),
        out_specs=whole,
        compiler_params=params(),
        cost_estimate=cost(3),
        name="scaled",
    )(value, *waits)


def added(terms):
    one, two = terms
    value = one[...].astype(F32)
    return value if two is None else value + two[...].astype(F32)


def grouped(parts, refs):
    refs = list(refs)
    out = [tuple(None if a is None else refs.pop(0) for a in pair) for pair in parts]
    return out, refs


def unmix_kernel(parts, block, count, *refs):
    terms, outs = grouped(parts, refs)
    outs = outs[-count:]
    width = outs[0].shape[1]
    half = outs[0].shape[0] // len(parts)
    for index, pair in enumerate(terms):
        value = added(pair)
        for first in range(0, width, block):
            size = min(block, width - first)
            for turn, out_ref in enumerate(outs):
                spot = first * len(outs) + turn * block
                out_ref[index * half : (index + 1) * half, first : first + size] = value[
                    :, spot : spot + size
                ]


def unmix(parts, count, block, width, waits=()):
    rows = len(parts) * parts[0][0].shape[0]
    arrays = [a for pair in parts for a in pair if a is not None]
    return pl.pallas_call(
        functools.partial(unmix_kernel, parts_mask(parts), block, count),
        out_shape=tuple(jax.ShapeDtypeStruct((rows, width), F32) for _ in range(count)),
        in_specs=[pl.BlockSpec(memory_space=pltpu.VMEM)] * len(arrays) + after_all(waits),
        compiler_params=params(),
        cost_estimate=cost(3),
        name="unmix",
    )(*arrays, *waits)


def parts_mask(parts):
    return [tuple(None if a is None else True for a in pair) for pair in parts]


def body(
    tokens,
    attn_gain,
    mlp_gain,
    w_query,
    w_key,
    w_value,
    w_out,
    w_gate,
    w_up,
    w_down,
    prefix,
    out_grad,
):
    mp = lax.axis_size("mp")
    place = lax.axis_index("mp")
    rows = tokens.shape[0]
    width_heads = w_query.shape[1]
    heads = width_heads // HD
    padded_heads = round_up(width_heads, LANES)
    width_ff = w_gate.shape[1]
    padded_ff = round_up(width_ff, FF_BLOCK)
    own = place * rows

    def row_block(value, index):
        return lax.dynamic_slice_in_dim(value, index * rows, rows, 0)

    tables = angle_tables()
    core = lax.axis_index("dp") % 2
    at = [jnp.stack([(place + mp - k) % mp, core]) for k in range(mp)]

    attn_pack = pack([w_query, w_key, w_value], LANES, padded_heads)
    attn_weights = dp_gather(attn_pack)
    ff_pack = pack([w_gate, w_up], FF_BLOCK, padded_ff, attn_pack)
    gate_up = dp_gather(ff_pack)
    token_pieces = ring_gather(tokens)
    qkv = None
    for k in range(mp - 1):
        qkv, mark = project(
            at[k], token_pieces[k], attn_gain[None], attn_weights, tables, qkv
        )
    out_own = gate(
        pack([w_out.T], LANES, padded_heads, ff_pack), token_pieces[-1], mark
    )
    out_pieces = [out_own] + [shift_back(out_own, mp - j) for j in range(1, mp)]
    qkv, _ = project(
        at[mp - 1], token_pieces[-1], attn_gain[None], attn_weights, tables, qkv
    )
    attended, attended_send, log_total = attend(qkv, prefix, heads)
    out_pack = chain(out_pieces, attended)
    attended_pieces = [attended, ring_up(gate(attended_send, out_pack))]
    out_weights = dp_gather(gate(out_pack, attended_pieces[1], gate_up))
    normed_one, whole_tokens = lay_tokens(
        at[0], token_pieces, attn_gain[None], (attended_pieces[1],)
    )
    down_pack = pack([w_down.T], LANES, padded_ff, whole_tokens)
    down = dp_gather(down_pack)
    while len(attended_pieces) < mp:
        attended_pieces.append(ring_up(attended_pieces[-1]))

    grad_pieces = [scaled(out_grad, attended_pieces[-1], down_pack, out_weights)]
    grad_pieces.append(ring_up(grad_pieces[0]))
    normed_two, split_two, middle = finish_middle(
        at[0], attended_pieces, out_weights, whole_tokens, mlp_gain[None], rows
    )
    grad_pieces.append(ring_up(gate(grad_pieces[1], normed_two)))
    hidden, slopes = feed(normed_two, gate_up)
    while len(grad_pieces) < mp:
        grad_pieces.append(ring_up(grad_pieces[-1]))
    by_chip = paired()

    def back_of(k, held, kind=BF16, waits=()):
        *held, term = feed_back(
            at[k % mp], grad_pieces[k % mp], slopes, down, gate_up, held, kind, waits
        )
        return held, term

    width = normed_two.shape[1]
    grad_pieces.append(ring_up(grad_pieces[-1]))
    held, total = back_of(1, None, waits=(grad_pieces[2],))
    arrived = ring_up(total)
    held, term = back_of(2, held, waits=(grad_pieces[3],))
    held, term_three = back_of(3, held)
    total = join(term, arrived, (term_three,))
    arrived = ring_up(total)
    attended_own = own_rows(at[0], attended_pieces, rows)
    (grad_both, grad_mlp), term_own = back_of(mp, held, F32, (total, attended_own))
    if by_chip:
        down_other = scatter_other(grad_mlp, hidden, 768, 6)
        total = join(term_three, arrived, (down_other,))
        arrived = ring_up(total)
        ff_other = scatter_other(split_two, grad_both, 1024, 11, (total,))
        down_chip = scatter_mine(
            grad_mlp, hidden, 768, 6, swap(gate(down_other, total), 1), (ff_other,)
        )
        waits = (down_chip, ff_other)
    else:
        total = join(term_three, arrived)
        arrived = ring_up(total)
        waits = ()
    grad_middle, grad_attn, split_attn, gain_two, zero = own_back(
        core[None], term_own, arrived, middle, out_grad, mlp_gain[None], waits
    )
    *mine, zero = spread(grad_attn, out_weights, mp)
    def mlp_chunk(k, zero):
        return lax.optimization_barrier(
            outer_cols(row_block(hidden, at[k % mp][0] + zero[0]), down)
        )

    arrived = [mine[0]] + [shift_back(mine[k], k) for k in range(1, mp)]
    chunk_one = mlp_chunk(1, zero).astype(BF16)
    if by_chip:
        ff_chip = scatter_mine(
            split_two, grad_both, 1024, 11, swap(gate(ff_other, split_attn), 1), (chunk_one,)
        )
        ff_share = scatter_around(ff_chip)
        down_share = scatter_around(gate(down_chip, zero))
        waits = (ff_chip,)
    else:
        ff_share = scatter_plain(split_two, grad_both)
        down_share = scatter_plain(grad_mlp, hidden)
        waits = ()
    out_other = scatter_other(split_attn, attended_own, 1280, 5, (chunk_one,))
    mlp_arrived = ring_up(gate(chunk_one, *arrived[1:]))
    out_arrived = swap(out_other, 1) if by_chip else None
    spots = jnp.stack([prefix[0], place])
    back = attend_back(
        qkv, attended, arrived, log_total, tables, spots, heads,
        (*waits, out_other) if by_chip else (),
    )

    def grad_one_term(k, zero=0):
        return lax.optimization_barrier(
            outer_cols(row_block(back, at[k % mp][0] + zero), attn_weights)
        )

    total = grad_one_term(1).astype(BF16)
    arrived = ring_up(total)
    index = lax.axis_index("dp")
    chip = jnp.stack([index // 2 % 2, index // 4])
    if by_chip:
        attn_other = scatter_other(normed_one, back, 640, 8, (total, mlp_arrived))
        attn_arrived = swap(attn_other, 1)
        out_parts, zero = scatter_chip(
            chip, split_attn, attended_own, 1280, 8, out_arrived, (total, attn_other)
        )
        out_moved = scatter_first(out_parts)
        total, zero = join_marked(
            grad_one_term(2, zero[0]), arrived, (attn_other, out_parts[1], out_parts[3])
        )
        arrived = ring_up(total)
        mlp_total = join(mlp_chunk(2, zero), mlp_arrived, (total,))
        mlp_arrived = ring_up(mlp_total)
        attn_parts, zero = scatter_chip(
            chip, normed_one, back, 640, 10, attn_arrived, (total, mlp_total)
        )
        attn_moved = scatter_first(attn_parts)
        total, zero = join_marked(
            grad_one_term(3, zero[0]), arrived, (attn_parts[1], attn_parts[3])
        )
        arrived = ring_up(total)
        term = grad_one_term(4, zero[0])
        out_half = scatter_halves(chip, out_parts, out_moved, (total,))
        out_share = scatter_second(out_half)
        mlp_total = join(
            mlp_chunk(3, zero), mlp_arrived, (total, out_half[0][1], out_half[1][1], term)
        )
        mlp_arrived = ring_up(mlp_total)
        attn_half = scatter_halves(chip, attn_parts, attn_moved, (mlp_total,))
        attn_share = scatter_second(attn_half)
        waits = (attn_half[0][1], attn_half[1][1])
    else:
        out_share = scatter_plain(split_attn, attended_own)
        attn_share = scatter_plain(normed_one, back)
        total = join(grad_one_term(2), arrived)
        arrived = ring_up(total)
        mlp_arrived = ring_up(join(mlp_chunk(2, zero), mlp_arrived))
        total = join(grad_one_term(3), arrived)
        arrived = ring_up(total)
        mlp_arrived = ring_up(join(mlp_chunk(3, zero), mlp_arrived))
        term = grad_one_term(4)
        waits = ()
    out_total, *out_mine = out_sum(out_share, mp, padded_heads)
    input_grad, gain_one, zero = finish_input(
        term, arrived, tokens, grad_middle, attn_gain[None],
        (*waits, mlp_arrived, *out_mine),
    )
    out_moved = [shift_back(out_mine[k - 1], k) for k in range(1, mp)]
    gains = sum_over(jnp.concatenate([gain_one, gain_two]), "dp")
    chunk = mlp_chunk(4, zero)
    grad_w_query, grad_w_key, grad_w_value = unmix(attn_share, 3, LANES, width_heads)
    grad_w_gate, grad_w_up = unmix(ff_share, 2, FF_BLOCK, width_ff)
    (grad_w_down,) = unmix(down_share, 1, LANES, width_ff)
    block_out = finish_block(middle, chunk, mlp_arrived)
    gains = sum_over(
        gate(gains, *out_moved, grad_w_query, grad_w_gate, grad_w_down, block_out), "mp"
    )
    grad_w_out = out_final(out_total, out_moved, width_heads, (block_out,))
    return (
        block_out,
        input_grad,
        grad_w_query,
        grad_w_key,
        grad_w_value,
        grad_w_out.T,
        grad_w_gate,
        grad_w_up,
        grad_w_down.T,
        gains[0],
        gains[1],
    )


def solution(mesh):
    return jax.shard_map(
        body,
        mesh=mesh,
        in_specs=(
            P(("dp", "mp"), None),
            P(),
            P(),
            P("dp", "mp"),
            P("dp", "mp"),
            P("dp", "mp"),
            P("mp", "dp"),
            P("dp", "mp"),
            P("dp", "mp"),
            P("mp", "dp"),
            P("dp"),
            P(("dp", "mp"), None),
        ),
        out_specs=(
            P(("dp", "mp"), None),
            P(("dp", "mp"), None),
            P("dp", "mp"),
            P("dp", "mp"),
            P("dp", "mp"),
            P("mp", "dp"),
            P("dp", "mp"),
            P("dp", "mp"),
            P("mp", "dp"),
            P(),
            P(),
        ),
        check_vma=False,
    )
```
